32 devices in a mesh: ctx: 8 (over z, x), tp: 4 (over y, core).
Axes of the slice: x: 2, y: 2, z: 4, core: 2. Of those that a mesh axis runs over, the one named last changes fastest.
Arguments:
- prompt_embeds: bfloat16 [2048, 2048], P('ctx', 'tp'), may hold values from -6 to 6
- decode_ids: int32 [128, 4], P('ctx'), may hold values from 0 to 32767, as said below
- embed_table: bfloat16 [32768, 2048], P('ctx', 'tp'), may hold values from -6 to 6
- norm_gain: float32 [2048], replicated, may hold values from 0.5 to 1.5
- x_weight: bfloat16 [2048, 4096], P(None, 'tp'), may hold values from -0.125 to 0.125
- bc_weight: bfloat16 [2048, 4, 2, 64], P(None, 'tp'), may hold values from -0.125 to 0.125
- dt_weight: bfloat16 [2048, 64], P(None, 'tp'), may hold values from -0.125 to 0.125
- dt_bias: float32 [64], P('tp'), may hold values from -4.91 to -1.75
- decay_log: float32 [64], P('tp'), may hold values from -8 to -0.68
- conv_x: float32 [4, 4096], P(None, 'tp'), may hold values from -3 to 3
- conv_bc: float32 [4, 4, 2, 64], P(None, 'tp'), may hold values from -3 to 3
- skip_gain: float32 [64], P('tp'), may hold values from 0.5 to 2
- out_gain: float32 [4096], P('tp'), may hold values from 0.5 to 1.5
- out_weight: bfloat16 [4096, 2048], P('tp'), may hold values from -0.09375 to 0.09375
Outputs:
- prompt_out: bfloat16 [2048, 2048], P('ctx', 'tp')
- decode_out: bfloat16 [128, 4, 2048], P('ctx', None, 'tp')
The draws below stay inside these ranges and needn't reach their ends.
Inputs may be any that keep to these rules, and one draw needn't show every extreme that they name: `decode_ids`: in every draw, all 64 ids of some sampler group lie in one of the 8 equal parts of the vocabulary.
All inputs are finite; a program needn't handle non-finite values.
Results may differ from the reference program's by a relative error of at most 0.0075.
Values may be sent and summed in bfloat16 or wider, within the bound.
No kernel may reach another device: no remote copies, remote signals or barrier semaphores. Data moves between devices by JAX's collectives and lax.ppermute only.
A program may use at most 128 MiB of HBM per device.

```python
import jax
import jax.numpy as jnp
from jax import lax

D = 2048
HEADS = 64
HEAD_DIM = 64
STATE = 64
GROUPS = 4
VOCAB = 32768
CONV = 4
SPAN = 256
STEPS = 4
ROWS = 16
TOKENS = 2048
GROUP_ROWS = 128


def head_kinds(key, share):
    return jax.random.uniform(key, (HEADS,)) < share


def draw_dt_bias(key, part):
    slower = head_kinds(key, 0.5)
    key = jax.random.fold_in(key, 7)
    spread = jax.random.uniform(key, (HEADS,), jnp.float32, -0.5, 0.5)
    return jnp.where(slower, -4.4 + spread, -2.25 + spread).astype(jnp.float32)


def draw_decay_log(key, part):
    slower = head_kinds(key, 0.5)
    key = jax.random.fold_in(key, 9)
    slow_key, fast_key = jax.random.split(key)
    slow_spread = jax.random.uniform(slow_key, (HEADS,), jnp.float32, -0.7, 0.7)
    fast_spread = jax.random.uniform(fast_key, (HEADS,), jnp.float32, -1.5, 1.5)
    slow_center = jnp.minimum(jnp.log(100.0 / TOKENS), -3.0)
    return jnp.where(slower, slow_center + slow_spread, -2.2 + fast_spread).astype(jnp.float32)


def draw_decode_ids(key, part):
    key = jax.random.fold_in(key, 11)
    group_count = GROUP_ROWS // ROWS
    part_words = VOCAB // group_count
    key_home, key_kind, key_forced, key_inner, key_any, key_coin = jax.random.split(key, 6)
    home_part = jax.random.randint(key_home, (group_count,), 0, group_count)
    group_kind = jax.random.randint(key_kind, (group_count,), 0, 3)
    forced_group = jax.random.randint(key_forced, (), 0, group_count)
    group_kind = jnp.where(jnp.arange(group_count) == forced_group, 0, group_kind)
    inner_ids = jax.random.randint(key_inner, (group_count, ROWS, STEPS), 0, part_words)
    anywhere = jax.random.randint(key_any, (group_count, ROWS, STEPS), 0, VOCAB)
    coin_flip = jax.random.randint(key_coin, (group_count, ROWS, STEPS), 0, 2)
    local_ids = home_part[:, None, None] * part_words + inner_ids
    kind_wide = group_kind[:, None, None]
    from_home = jnp.logical_or(kind_wide == 0, jnp.logical_and(kind_wide == 1, coin_flip == 0))
    chosen = jnp.where(from_home, local_ids, anywhere)
    return chosen.reshape(GROUP_ROWS, STEPS).astype(jnp.int32)


def block_scale(rng, dims, shards, low, largest):
    loudness = 1.0
    for axis_at, blocks in shards:
        heights = jax.random.uniform(jax.random.fold_in(jax.random.fold_in(rng, 6), axis_at), (blocks,), jnp.float32, low / len(shards), largest / len(shards))
        loudness = loudness * jnp.repeat(jnp.exp(heights), dims[axis_at] // blocks).reshape((-1,) + (1,) * (len(dims) - 1 - axis_at))
    return loudness


def bell_draw(key, extent, scale, most, shards=(), kind=jnp.bfloat16):
    result = jax.random.normal(key, extent, jnp.float32) * scale
    if len(shards) > 0:
        result = block_scale(key, extent, shards, -0.22, 0.18) * result
    return jnp.clip(result, min=-most, max=most).astype(kind)


def setup_inputs(seed: int = 0) -> dict:
    keys = jax.random.split(jax.random.key(seed), 15)
    return {
        "prompt_embeds": bell_draw(keys[0], (TOKENS, D), 1.0, 6.0, ((0, 8), (1, 4))),
        "decode_ids": draw_decode_ids(jax.random.fold_in(keys[14], 71), 0),
        "embed_table": bell_draw(keys[2], (VOCAB, D), 1.0, 6.0, ((0, 8), (1, 4))),
        "norm_gain": jnp.clip(1.0 + 0.1 * jax.random.normal(keys[3], (D,), jnp.float32), 0.5, 1.5),
        "x_weight": bell_draw(keys[4], (D, HEADS * HEAD_DIM), D ** -0.5, 0.125, ((1, 4),)),
        "bc_weight": bell_draw(keys[5], (D, GROUPS, 2, STATE), D ** -0.5, 0.125, ((1, 4),)),
        "dt_weight": bell_draw(keys[6], (D, HEADS), D ** -0.5, 0.125, ((1, 4),)),
        "dt_bias": draw_dt_bias(jax.random.fold_in(keys[14], 71), 0),
        "decay_log": draw_decay_log(jax.random.fold_in(keys[14], 71), 0),
        "conv_x": bell_draw(keys[9], (CONV, HEADS * HEAD_DIM), CONV ** -0.5, 3.0, ((1, 4),), jnp.float32),
        "conv_bc": bell_draw(keys[10], (CONV, GROUPS, 2, STATE), 1.0, 3.0, ((1, 4),), jnp.float32),
        "skip_gain": jnp.clip(0.5 + 1.5 * jax.random.uniform(keys[11], (HEADS,), jnp.float32) ** block_scale(keys[11], (HEADS,), ((0, 4),), -0.2, 0.2), 0.5, 2.0),
        "out_gain": jnp.clip(1.0 + 0.1 * jax.random.normal(keys[12], (HEADS * HEAD_DIM,), jnp.float32), 0.5, 1.5),
        "out_weight": bell_draw(keys[13], (HEADS * HEAD_DIM, D), (HEADS * HEAD_DIM) ** -0.5, 0.09375, ((0, 4),)),
    }


EPS = 1e-05

def rms_rows(values, gain_row):
    widened = values.astype(jnp.float32)
    factor = lax.rsqrt(lax.optimization_barrier(jnp.mean(widened * widened, axis=-1, keepdims=True)) + EPS)
    return (widened * factor * gain_row).astype(jnp.bfloat16)

def project(normed, x_weight, bc_weight, dt_weight, dt_bias):
    flat_weight = bc_weight.reshape(bc_weight.shape[0], -1)
    x_raw = jnp.dot(normed, x_weight, preferred_element_type=jnp.float32).astype(jnp.bfloat16)
    bc_raw = jnp.dot(normed, flat_weight, preferred_element_type=jnp.float32).astype(jnp.bfloat16)
    step_size = jax.nn.softplus(jnp.dot(normed, dt_weight, preferred_element_type=jnp.float32) + dt_bias)
    return (x_raw, bc_raw, step_size)

def causal_conv(stream, kernel_rows, rim_rows):
    rim_rows = jnp.broadcast_to(rim_rows, stream.shape[:-2] + rim_rows.shape[-2:])
    joined = jnp.concatenate([rim_rows, stream], axis=-2).astype(jnp.float32)
    length = stream.shape[-2]
    summed = jnp.zeros(stream.shape, jnp.float32)
    for offset in range(kernel_rows.shape[0]):
        summed = summed + kernel_rows[offset] * lax.slice_in_dim(joined, offset, offset + length, axis=joined.ndim - 2)
    return jax.nn.silu(summed).astype(jnp.bfloat16)

def intra_block(x_conv, b_rows, c_rows, step_size, decay_rate):
    length, head_count, head_width = x_conv.shape
    groups = b_rows.shape[1]
    per_group = head_count // groups
    cum_log = jnp.cumsum(step_size * decay_rate, axis=0)
    scores = jnp.einsum('tgn,sgn->gts', c_rows.astype(jnp.float32), b_rows.astype(jnp.float32))
    scores = jnp.repeat(scores, per_group, axis=0)
    log_gaps = cum_log.T[:, :, None] - cum_log.T[:, None, :]
    causal = jnp.arange(length)[:, None] >= jnp.arange(length)[None, :]
    decays = jnp.where(causal, jnp.exp(jnp.where(causal, log_gaps, 0.0)), 0.0)
    mixing = (scores * decays * step_size.T[:, None, :]).astype(jnp.bfloat16)
    within = jnp.einsum('hts,shp->thp', mixing.astype(jnp.float32), x_conv.astype(jnp.float32))
    to_end = jnp.exp(cum_log[-1] - cum_log) * step_size
    weighted = (x_conv.astype(jnp.float32) * to_end[:, :, None]).astype(jnp.bfloat16)
    fresh_state = jnp.einsum('sgkp,sgn->gkpn', weighted.reshape(length, groups, per_group, head_width).astype(jnp.float32), b_rows.astype(jnp.float32))
    return (within, fresh_state.reshape(head_count, head_width, -1), cum_log)

def carried(c_rows, cum_log, state_in):
    length, groups, _ = c_rows.shape
    head_count, head_width, _ = state_in.shape
    grouped = state_in.reshape(groups, head_count // groups, head_width, -1)
    reaches = jnp.einsum('tgn,gkpn->tgkp', c_rows.astype(jnp.float32), grouped, precision=lax.Precision.HIGHEST)
    return reaches.reshape(length, head_count, head_width) * jnp.exp(cum_log)[:, :, None]

def finish(y_sum, x_conv, skip_gain, out_gain, groups):
    length, head_count, head_width = y_sum.shape
    full = y_sum + skip_gain[:, None] * x_conv.astype(jnp.float32)
    grouped = full.reshape(length, groups, -1)
    factor = lax.rsqrt(lax.optimization_barrier(jnp.mean(grouped * grouped, axis=-1, keepdims=True)) + EPS)
    return ((grouped * factor).reshape(length, -1) * out_gain).astype(jnp.bfloat16)

def decode_rows(x_conv, b_rows, c_rows, step_size, decay_rate, state_in):

    def one_row(x_row, b_row, c_row, step_row):
        within, fresh_state, cum_log = intra_block(x_row, b_row, c_row, step_row, decay_rate)
        return within + carried(c_row, cum_log, state_in)
    return jax.vmap(one_row)(x_conv, b_rows, c_rows, step_size)

def reference(prompt_embeds, decode_ids, embed_table, norm_gain, x_weight, bc_weight, dt_weight, dt_bias, decay_log, conv_x, conv_bc, skip_gain, out_gain, out_weight):
    decay_rate = -jnp.exp(decay_log)
    kernel_bc = conv_bc.reshape(CONV, -1)
    margin = CONV - 1
    normed = rms_rows(prompt_embeds, norm_gain)
    x_raw, bc_raw, step_size = project(normed, x_weight, bc_weight, dt_weight, dt_bias)
    x_conv = causal_conv(x_raw, conv_x, jnp.zeros((margin, x_raw.shape[1]), jnp.bfloat16))
    bc_conv = causal_conv(bc_raw, kernel_bc, jnp.zeros((margin, bc_raw.shape[1]), jnp.bfloat16))
    blocks = TOKENS // SPAN
    x_blocks = x_conv.reshape(blocks, SPAN, HEADS, HEAD_DIM)
    bc_blocks = bc_conv.reshape(blocks, SPAN, GROUPS, 2, STATE)
    step_blocks = step_size.reshape(blocks, SPAN, HEADS)

    def block_step(state_in, pieces):
        x_block, b_block, c_block, step_block = pieces
        within, fresh_state, cum_log = intra_block(x_block, b_block, c_block, step_block, decay_rate)
        y_block = within + carried(c_block, cum_log, state_in)
        state_in = jnp.exp(cum_log[-1])[:, None, None] * state_in + fresh_state
        return (state_in, y_block)
    start_state = jnp.zeros((HEADS, HEAD_DIM, STATE), jnp.float32)
    final_state, prompt_y = lax.scan(block_step, start_state, (x_blocks, bc_blocks[:, :, :, 0], bc_blocks[:, :, :, 1], step_blocks))
    prompt_mixed = finish(prompt_y.reshape(TOKENS, HEADS, HEAD_DIM), x_conv.reshape(TOKENS, HEADS, HEAD_DIM), skip_gain, out_gain, GROUPS)
    prompt_out = jnp.dot(prompt_mixed, out_weight, preferred_element_type=jnp.float32).astype(jnp.bfloat16)
    decode_embeds = jnp.take(embed_table, decode_ids, axis=0)
    dec_normed = rms_rows(decode_embeds, norm_gain).reshape(GROUP_ROWS * STEPS, D)
    dx_raw, dbc_raw, dec_step = project(dec_normed, x_weight, bc_weight, dt_weight, dt_bias)
    dec_x_conv = causal_conv(dx_raw.reshape(GROUP_ROWS, STEPS, -1), conv_x, x_raw[-margin:])
    dec_bc = causal_conv(dbc_raw.reshape(GROUP_ROWS, STEPS, -1), kernel_bc, bc_raw[-margin:])
    dec_x_conv = dec_x_conv.reshape(GROUP_ROWS, STEPS, HEADS, HEAD_DIM)
    dec_bc = dec_bc.reshape(GROUP_ROWS, STEPS, GROUPS, 2, STATE)
    dec_y = decode_rows(dec_x_conv, dec_bc[:, :, :, 0], dec_bc[:, :, :, 1], dec_step.reshape(GROUP_ROWS, STEPS, HEADS), decay_rate, final_state)
    dec_mixed = finish(dec_y.reshape(GROUP_ROWS * STEPS, HEADS, HEAD_DIM), dec_x_conv.reshape(GROUP_ROWS * STEPS, HEADS, HEAD_DIM), skip_gain, out_gain, GROUPS)
    decode_out = jnp.dot(dec_mixed, out_weight, preferred_element_type=jnp.float32).astype(jnp.bfloat16)
    return (prompt_out, decode_out.reshape(GROUP_ROWS, STEPS, D))
```

```python
import jax
import jax.numpy as jnp
from jax import lax
from jax.sharding import PartitionSpec as P

EPS = 1e-05
BF16 = jnp.bfloat16
F32 = jnp.float32


def swapped(value, axis, bit):
    count = lax.axis_size(axis)
    return lax.ppermute(value, axis, [(i, i ^ bit) for i in range(count)])


def bits_of(axis):
    count = lax.axis_size(axis)
    assert count & (count - 1) == 0
    return [1 << k for k in range(count.bit_length() - 1)]


def relative(blocks, axis):
    bits = bits_of(axis)
    me = lax.axis_index(axis)
    tail = blocks.shape[1:]
    cube = blocks.reshape((2,) * len(bits) + tail)
    for at, bit in enumerate(reversed(bits)):
        cube = jnp.where((me & bit) != 0, jnp.flip(cube, axis=at), cube)
    order = tuple(reversed(range(len(bits)))) + tuple(range(len(bits), cube.ndim))
    return cube.transpose(order).reshape(blocks.shape)


def rms_rows(values, gain_row):
    widened = values.astype(F32)
    factor = lax.rsqrt(jnp.mean(widened * widened, axis=-1, keepdims=True) + EPS)
    return (widened * factor * gain_row).astype(BF16)


def dot(a, b):
    return jnp.dot(a, b, preferred_element_type=F32)


def expand(per_head, width):
    return jnp.repeat(per_head, width, axis=-1)


def project(normed, x_weight, bc_weight, dt_weight, dt_bias):
    x_raw = dot(normed, x_weight).astype(BF16)
    bc_raw = dot(normed, bc_weight).astype(BF16)
    step_size = jax.nn.softplus(dot(normed, dt_weight) + dt_bias)
    return x_raw, bc_raw, step_size


def conv_rows(joined, kernel_rows, stride, length):
    joined = joined.astype(F32)
    summed = jnp.zeros((length, joined.shape[1]), F32)
    for offset in range(kernel_rows.shape[0]):
        start = offset * stride
        summed = summed + kernel_rows[offset] * joined[start : start + length]
    return jax.nn.silu(summed).astype(BF16)


def local_part(x_conv, bc_conv, step_size, decay_rate, mask, heads):
    length = x_conv.shape[0]
    state_width = bc_conv.shape[1] // 2
    width = x_conv.shape[1] // heads
    b_rows, c_rows = bc_conv[:, :state_width], bc_conv[:, state_width:]
    cum_log = jnp.dot(mask.astype(F32), step_size * decay_rate, precision=lax.Precision.HIGHEST)
    scores = lax.dot_general(c_rows, b_rows, (((1,), (1,)), ((), ())), preferred_element_type=F32)
    gaps = cum_log.T[:, :, None] - cum_log.T[:, None, :]
    decays = jnp.where(mask, jnp.exp(jnp.where(mask, gaps, 0.0)), 0.0)
    mixing = (scores[None] * decays * step_size.T[:, None, :]).astype(BF16)
    x_heads = x_conv.reshape(length, heads, width)
    within = jnp.einsum("hts,shp->thp", mixing, x_heads, preferred_element_type=F32)
    return within.reshape(length, -1), cum_log, b_rows, c_rows


def reach(c_rows, state):
    high = state.astype(BF16)
    low = (state - high.astype(F32)).astype(BF16)
    return dot(jnp.concatenate([c_rows, c_rows], axis=1), jnp.concatenate([high, low], axis=0))


def finish(y_sum, x_conv, skip_row, out_gain):
    full = y_sum + skip_row * x_conv.astype(F32)
    factor = lax.rsqrt(jnp.mean(full * full, axis=-1, keepdims=True) + EPS)
    return (full * factor * out_gain).astype(BF16)


def on_device(
    prompt_embeds,
    decode_ids,
    embed_table,
    norm_gain,
    x_weight,
    bc_weight,
    dt_weight,
    dt_bias,
    decay_log,
    conv_x,
    conv_bc,
    skip_gain,
    out_gain,
    out_weight,
):
    heads = dt_weight.shape[1]
    assert bc_weight.shape[1] == 1 and lax.axis_size("tp") == 4
    width = x_weight.shape[1] // heads
    taps = conv_x.shape[0]
    margin = taps - 1
    decay_rate = -jnp.exp(decay_log)
    kernel_bc = conv_bc.reshape(taps, -1)
    flat_bc = bc_weight.reshape(bc_weight.shape[0], -1)
    state_width = flat_bc.shape[1] // 2
    tokens, part = prompt_embeds.shape
    rows, steps = decode_ids.shape
    asked = rows * steps
    groups = lax.axis_size("ctx")
    me_c = lax.axis_index("ctx")
    me_t = lax.axis_index("tp")
    vocab_here = embed_table.shape[0]

    e2 = swapped(prompt_embeds, "tp", 2)
    e1 = swapped(prompt_embeds, "tp", 1)

    ids = decode_ids.T.reshape(-1)
    digits = jnp.stack([ids & 255, (ids >> 8) & 255, ids >> 16]).astype(BF16).reshape(-1)
    extra = -(-digits.shape[0] // part)
    digits = jnp.pad(digits, (0, extra * part - digits.shape[0])).reshape(extra, part)
    note = jnp.concatenate([prompt_embeds[-margin:], digits], axis=0)
    devices = groups * 4
    notes = lax.all_to_all(
        jnp.broadcast_to(note[None], (devices,) + note.shape), ("ctx", "tp"), 0, 0
    ).reshape(groups, 4, margin + extra, part)
    digits = notes[:, 0, margin:].reshape(groups, -1)[:, : 3 * asked].reshape(groups, 3, asked)
    digits = digits.astype(jnp.int32)
    all_ids = digits[:, 0] + digits[:, 1] * 256 + digits[:, 2] * 65536
    edges = notes[:, :, :margin].transpose(0, 2, 1, 3).reshape(groups, margin, 4 * part)
    before = lax.dynamic_index_in_dim(edges, jnp.maximum(me_c - 1, 0), 0, keepdims=False)
    before = jnp.where(me_c > 0, before, jnp.zeros_like(before))
    tail = edges[-1]

    e3 = swapped(e2, "tp", 1)

    wanted = relative(all_ids, "ctx").reshape(-1) - me_c * vocab_here
    inside = jnp.logical_and(wanted >= 0, wanted < vocab_here)
    picked = jnp.take(embed_table, jnp.clip(wanted, 0, vocab_here - 1), axis=0)
    kept = jnp.where(inside[:, None], picked, jnp.zeros((), BF16))
    for bit in bits_of("ctx"):
        half = kept.shape[0] // 2
        kept = kept[:half] + swapped(kept[half:], "ctx", bit)
    dec2 = jnp.concatenate([kept, swapped(kept, "tp", 2)], axis=0)
    dec4 = jnp.concatenate([dec2, swapped(dec2, "tp", 1)], axis=0).reshape(4, asked, part)

    def in_order(r0, r1, r2, r3):
        cube = jnp.stack([r0, r1, r2, r3])
        cube = jnp.where((me_t & 1) != 0, cube[jnp.array([1, 0, 3, 2])], cube)
        cube = jnp.where((me_t & 2) != 0, cube[jnp.array([2, 3, 0, 1])], cube)
        return jnp.concatenate([cube[0], cube[1], cube[2], cube[3]], axis=1)

    pad = 8 - margin
    features = in_order(prompt_embeds, e1, e2, e3)
    features = jnp.concatenate([jnp.zeros((pad, features.shape[1]), BF16), before, features], axis=0)
    normed = rms_rows(features, norm_gain)
    x_raw, bc_raw, step_size = project(normed, x_weight, flat_bc, dt_weight, dt_bias)
    step_size = step_size[8:]
    x_conv = conv_rows(x_raw[pad:], conv_x, 1, tokens)
    bc_conv = conv_rows(bc_raw[pad:], kernel_bc, 1, tokens)
    mask = jnp.arange(tokens)[:, None] >= jnp.arange(tokens)[None, :]
    y_local, cum_log, b_rows, c_rows = local_part(
        x_conv, bc_conv, step_size, decay_rate, mask, heads
    )
    to_end = jnp.exp(cum_log[-1] - cum_log) * step_size
    weighted = (x_conv.astype(F32) * expand(to_end, width)).astype(BF16)
    state = lax.dot_general(b_rows, weighted, (((0,), (0,)), ((), ())), preferred_element_type=F32)
    decay = expand(jnp.exp(cum_log[-1:]), width)

    came = jnp.zeros_like(state)
    since = jnp.ones_like(decay)
    for bit in bits_of("ctx"):
        high = decay.astype(BF16)
        low = (decay - high.astype(F32)).astype(BF16)
        message = jnp.concatenate([state.astype(BF16), high, low], axis=0)
        message = swapped(message, "ctx", bit).astype(F32)
        other = message[:state_width]
        other_decay = message[state_width : state_width + 1] + message[state_width + 1 :]
        later = (me_c & bit) != 0
        came = jnp.where(later, since * other + came, came)
        since = jnp.where(later, since * other_decay, since)
        state = jnp.where(later, decay * other + state, other_decay * state + other)
        decay = decay * other_decay

    dec_features = in_order(dec4[0], dec4[2], dec4[1], dec4[3])
    dec_features = jnp.concatenate([dec_features, tail], axis=0)
    dec_normed = rms_rows(dec_features, norm_gain)
    dx_raw, dbc_raw, dec_step = project(dec_normed, x_weight, flat_bc, dt_weight, dt_bias)
    dec_step = dec_step[:asked]

    def stepped(raw):
        ahead = jnp.repeat(raw[asked:], rows, axis=0)
        return jnp.concatenate([ahead, raw[:asked]], axis=0)

    dec_x = conv_rows(stepped(dx_raw), conv_x, rows, asked)
    dec_bc = conv_rows(stepped(dbc_raw), kernel_bc, rows, asked)
    at = jnp.arange(asked)
    dec_mask = jnp.logical_and(
        (at % rows)[:, None] == (at % rows)[None, :], at[:, None] >= at[None, :]
    )
    dec_y, dec_cum, _, dec_c = local_part(dec_x, dec_bc, dec_step, decay_rate, dec_mask, heads)

    skip_row = expand(skip_gain, width)
    y = y_local + reach(c_rows, came) * expand(jnp.exp(cum_log), width)
    mixed = finish(y, x_conv, skip_row, out_gain)
    dec_y = dec_y + reach(dec_c, state) * expand(jnp.exp(dec_cum), width)
    dec_mixed = finish(dec_y, dec_x, skip_row, out_gain)
    both = jnp.concatenate([mixed, dec_mixed], axis=0)

    def terms(r):
        columns = lax.dynamic_slice_in_dim(out_weight, (me_t ^ r) * part, part, axis=1)
        return dot(both, columns)

    got3 = swapped(terms(3).astype(BF16), "tp", 1)
    got1 = swapped(terms(1).astype(BF16), "tp", 1)
    far = terms(2) + got3.astype(F32)
    got2 = swapped(far.astype(BF16), "tp", 2)
    total = terms(0) + got1.astype(F32) + got2.astype(F32)
    total = total.astype(BF16)
    decode_out = total[tokens:].reshape(steps, rows, part).transpose(1, 0, 2)
    return (total[:tokens], decode_out)


def solution(mesh):
    return jax.shard_map(
        on_device,
        mesh=mesh,
        in_specs=(
            P("ctx", "tp"),
            P("ctx", None),
            P("ctx", "tp"),
            P(),
            P(None, "tp"),
            P(None, "tp", None, None),
            P(None, "tp"),
            P("tp"),
            P("tp"),
            P(None, "tp"),
            P(None, "tp", None, None),
            P("tp"),
            P("tp"),
            P("tp", None),
        ),
        out_specs=(P("ctx", "tp"), P("ctx", None, "tp")),
        check_vma=False,
    )
```

```python
import functools

import jax
import jax.numpy as jnp
from jax import lax
from jax.experimental import pallas as pl
from jax.experimental.pallas import tpu as pltpu
from jax.sharding import PartitionSpec as P

EPS = 1e-05
BF16 = jnp.bfloat16
F32 = jnp.float32
LANES = 128
PARTS = 4
EDGE = 8
MEBI = 1024 * 1024


def swapped(value, axis, bit):
    count = lax.axis_size(axis)
    return lax.ppermute(value, axis, [(i, i ^ bit) for i in range(count)])


def bits_of(axis):
    count = lax.axis_size(axis)
    assert count & (count - 1) == 0
    return [1 << k for k in range(count.bit_length() - 1)]


def relative(blocks, axis):
    bits = bits_of(axis)
    me = lax.axis_index(axis)
    tail = blocks.shape[1:]
    cube = blocks.reshape((2,) * len(bits) + tail)
    for at, bit in enumerate(reversed(bits)):
        cube = jnp.where((me & bit) != 0, jnp.flip(cube, axis=at), cube)
    order = tuple(reversed(range(len(bits)))) + tuple(range(len(bits), cube.ndim))
    return cube.transpose(order).reshape(blocks.shape)


def dot(a, b):
    return jnp.dot(a, b, preferred_element_type=F32)


def across(a, b, axis):
    return lax.dot_general(a, b, (((axis,), (axis,)), ((), ())), preferred_element_type=F32)


def halves(value):
    high = value.astype(BF16)
    low = (value - high.astype(F32)).astype(BF16)
    return high, low


def iota(shape, axis):
    return lax.broadcasted_iota(jnp.int32, shape, axis)


def spreader(width, channels):
    head = iota((2 * LANES, channels), 0) & (LANES - 1)
    return jnp.where(head == iota((2 * LANES, channels), 1) // width, 1.0, 0.0).astype(BF16)


def widened(per_head, spread):
    high, low = halves(per_head)
    return dot(jnp.concatenate([high, low], axis=1), spread)


def padded(row):
    return jnp.concatenate([row, jnp.zeros((row.shape[0], LANES - row.shape[1]), F32)], axis=1)


def silu(value):
    return value / (1.0 + jnp.exp(-value))


def front_kernel(
    decode,
    rows,
    heads,
    place,
    notes,
    own,
    over1,
    over2,
    over3,
    gain,
    x_weight,
    bc_weight,
    dt_weight,
    dt_bias,
    decay_log,
    conv_x,
    conv_bc,
    skip_gain,
    y_out,
    bc_out,
    reach_out,
    *rest,
):
    if decode:
        normed, x_conv, joined = rest
    else:
        message_out, state_out, decay_out, normed, x_conv, joined = rest
    tokens, part = own.shape
    channels = x_weight.shape[1]
    width = channels // heads
    state_width = bc_weight.shape[1] // 2
    taps = conv_x.shape[0]
    margin = taps - 1
    me, edge_at, edge_on = place[0], place[1], place[2]

    blocks = [ref[...].astype(F32) for ref in (own, over1, over2, over3)]
    square = sum(jnp.sum(b * b, axis=1, keepdims=True) for b in blocks)
    factor = lax.rsqrt(square / (PARTS * part) + EPS)
    for r in range(PARTS):
        normed[me ^ r, :tokens, :] = (blocks[r] * factor * gain[me ^ r]).astype(BF16)
    valid = jnp.logical_and(iota((EDGE, part), 0) >= EDGE - margin, edge_on > 0)
    edges = [jnp.where(valid, notes[edge_at * PARTS + j].astype(F32), 0.0) for j in range(PARTS)]
    square = sum(jnp.sum(e * e, axis=1, keepdims=True) for e in edges)
    factor = lax.rsqrt(square / (PARTS * part) + EPS)
    for j in range(PARTS):
        edge = edges[j] * factor * gain[j]
        normed[j, tokens:, :] = jnp.concatenate([edge, jnp.zeros_like(edge)], axis=0).astype(BF16)

    def projected(weight_of):
        return sum(dot(normed[j], weight_of(j)) for j in range(PARTS))

    def convolved(raw, taps_of):
        raw = raw.astype(BF16).astype(F32)
        lanes = raw.shape[1]
        edge = raw[tokens : tokens + EDGE]
        if decode:
            for m in range(margin):
                one = edge[EDGE - margin + m : EDGE - margin + m + 1]
                joined[m * rows : (m + 1) * rows, :lanes] = jnp.broadcast_to(one, (rows, lanes))
            joined[margin * rows : margin * rows + tokens, :lanes] = raw[:tokens]
            starts = [k * rows for k in range(taps)]
        else:
            joined[:EDGE, :lanes] = edge
            joined[EDGE : EDGE + tokens, :lanes] = raw[:tokens]
            starts = [EDGE - margin + k for k in range(taps)]
        total = sum(taps_of(k) * joined[s : s + tokens, :lanes] for k, s in enumerate(starts))
        return silu(total)

    step_lanes = 2 * LANES
    for lane in range(0, channels, step_lanes):
        raw = projected(lambda j: x_weight[j * part : (j + 1) * part, lane : lane + step_lanes])
        x_conv[:, lane : lane + step_lanes] = convolved(
            raw, lambda k: conv_x[k : k + 1, lane : lane + step_lanes]
        ).astype(BF16)

    def side(j):
        here = slice(j * part, (j + 1) * part)
        fill = jnp.zeros((part, LANES - heads), BF16)
        return jnp.concatenate([bc_weight[here], dt_weight[here], fill], axis=1)

    raw = projected(side)
    bc_conv = convolved(raw[:, : 2 * state_width], lambda k: conv_bc[k : k + 1])
    bc_out[...] = bc_conv.astype(BF16)
    pre = raw[:tokens, 2 * state_width :] + padded(dt_bias[...])
    step_size = jnp.maximum(pre, 0.0) + jnp.log1p(jnp.exp(-jnp.abs(pre)))
    b_rows = bc_conv[:, :state_width].astype(BF16)
    c_rows = bc_conv[:, state_width:].astype(BF16)

    t_at = iota((tokens, tokens), 0)
    s_at = iota((tokens, tokens), 1)
    mask = t_at >= s_at
    if decode:
        mask = jnp.logical_and(mask, t_at % rows == s_at % rows)
    logs = step_size * -jnp.exp(padded(decay_log[...]))
    high, low = halves(logs)
    lowest = (logs - high.astype(F32) - low.astype(F32)).astype(BF16)
    sums = dot(
        jnp.where(mask, 1.0, 0.0).astype(BF16), jnp.concatenate([high, low, lowest], axis=1)
    )
    cum_log = sums[:, :LANES] + sums[:, LANES : 2 * LANES] + sums[:, 2 * LANES :]
    reach_out[...] = jnp.exp(cum_log)
    cum_across = cum_log.T
    step_across = step_size.T
    scores = across(c_rows, b_rows, 1)
    spread = spreader(width, channels)
    skip_row = widened(jnp.broadcast_to(padded(skip_gain[...]), (EDGE, LANES)), spread)[:1]

    per_tile = LANES // width
    lane_head = iota((tokens, LANES), 1) // width
    for tile in range(channels // LANES):
        lanes = slice(tile * LANES, (tile + 1) * LANES)
        x_tile = x_conv[:, lanes].astype(F32)
        left, right = [], []
        for k in range(per_tile):
            h = tile * per_tile + k
            gaps = cum_log[:, h : h + 1] - cum_across[h : h + 1, :]
            decays = jnp.exp(jnp.where(mask, gaps, -1e30))
            left.append((scores * decays * step_across[h : h + 1, :]).astype(BF16))
            right.append(jnp.where(lane_head == k, x_tile, 0.0).astype(BF16))
        within = sum(dot(a, b) for a, b in zip(left, right))
        y_out[:, lanes] = within + skip_row[:, lanes] * x_tile

    if not decode:
        last = cum_log[tokens - 1 : tokens]
        to_end = jnp.exp(last - cum_log) * step_size
        b_turned = bc_conv.T[:state_width].astype(BF16)
        decay = widened(jnp.broadcast_to(jnp.exp(last), (EDGE, LANES)), spread)
        decay_out[...] = decay
        high, low = halves(decay[:1])
        at = iota((2 * EDGE, channels), 0)
        message_out[state_width:, :] = jnp.where(
            at == 0, high.astype(F32), jnp.where(at == 1, low.astype(F32), 0.0)
        ).astype(BF16)
        for lane in range(0, channels, step_lanes):
            lanes = slice(lane, lane + step_lanes)
            scale = widened(to_end, spread[:, lanes])
            weighted = (x_conv[:, lanes].astype(F32) * scale).astype(BF16)
            state = dot(b_turned, weighted)
            state_out[:, lanes] = state
            message_out[:state_width, lanes] = state.astype(BF16)


def unpacked(message, state_width):
    other = message[:state_width, :].astype(F32)
    tail = message[state_width:, :].astype(F32)
    return other, tail[0:1] + tail[1:2]


def step_kernel(first, place, message, state, decay, came, since, message_out, state_out, decay_out, came_out, since_out):
    later = place[0] > 0
    state_width = state.shape[0]
    other, other_decay = unpacked(message, state_width)
    mine, my_decay = state[...], decay[0:1, :]
    before = jnp.zeros_like(mine) if first else came[...]
    passed = jnp.ones_like(my_decay) if first else since[0:1, :]
    came_out[...] = jnp.where(later, passed * other + before, before)
    since_out[...] = jnp.broadcast_to(jnp.where(later, passed * other_decay, passed), since_out.shape)
    total = jnp.where(later, my_decay * other + mine, other_decay * mine + other)
    decayed = my_decay * other_decay
    state_out[...] = total
    decay_out[...] = jnp.broadcast_to(decayed, decay_out.shape)
    message_out[:state_width, :] = total.astype(BF16)
    high, low = halves(decayed)
    at = iota((2 * EDGE, state.shape[1]), 0)
    message_out[state_width:, :] = jnp.where(
        at == 0, high.astype(F32), jnp.where(at == 1, low.astype(F32), 0.0)
    ).astype(BF16)


def back_kernel(decode, heads, place, message, state, decay, came, since, y, bc, reach, gain, weight, sent_out, kept_out, full, mixed):
    me, later = place[0], place[1] > 0
    state_width = state.shape[0]
    tokens, channels = y.shape
    part = weight.shape[1] // PARTS
    other, other_decay = unpacked(message, state_width)
    if decode:
        incoming = jnp.where(later, decay[0:1, :] * other + state[...], other_decay * state[...] + other)
    else:
        incoming = jnp.where(later, since[0:1, :] * other + came[...], came[...])
    high, low = halves(incoming)
    blank = jnp.zeros_like(high)
    table = jnp.concatenate([blank, high, blank, low], axis=0)
    twice = jnp.concatenate([bc[...], bc[...]], axis=1)
    spread = spreader(channels // heads, channels)
    step_lanes = 2 * LANES
    square = jnp.zeros((tokens, 1), F32)
    for lane in range(0, channels, step_lanes):
        lanes = slice(lane, lane + step_lanes)
        total = y[:, lanes] + dot(twice, table[:, lanes]) * widened(reach[...], spread[:, lanes])
        full[:, lanes] = total
        square = square + jnp.sum(total * total, axis=1, keepdims=True)
    factor = lax.rsqrt(square / channels + EPS)
    mixed[...] = (full[...] * factor * gain[...]).astype(BF16)
    for at, r in enumerate((3, 1)):
        columns = pl.ds(pl.multiple_of((me ^ r) * part, part), part)
        sent_out[at] = dot(mixed[...], weight[:, columns]).astype(BF16)
    for at, r in enumerate((2, 0)):
        columns = pl.ds(pl.multiple_of((me ^ r) * part, part), part)
        kept_out[at] = dot(mixed[...], weight[:, columns])


VMEM = pl.BlockSpec(memory_space=pltpu.VMEM)
SMEM = pl.BlockSpec(memory_space=pltpu.SMEM)


def called(kernel, inputs, outs, scratch, flops, limit):
    moved = sum(v.size * v.dtype.itemsize for v in inputs) + sum(
        o.size * o.dtype.itemsize for o in outs
    )
    return pl.pallas_call(
        kernel,
        out_shape=outs,
        in_specs=[SMEM] + [VMEM] * (len(inputs) - 1),
        out_specs=[VMEM] * len(outs),
        scratch_shapes=scratch,
        compiler_params=pltpu.CompilerParams(vmem_limit_bytes=limit * MEBI),
        cost_estimate=pl.CostEstimate(flops=flops, bytes_accessed=moved, transcendentals=0),
    )(*inputs)


def shaped(shape, dtype):
    return jax.ShapeDtypeStruct(shape, dtype)


def on_device(
    prompt_embeds,
    decode_ids,
    embed_table,
    norm_gain,
    x_weight,
    bc_weight,
    dt_weight,
    dt_bias,
    decay_log,
    conv_x,
    conv_bc,
    skip_gain,
    out_gain,
    out_weight,
):
    heads = dt_weight.shape[1]
    assert bc_weight.shape[1] == 1 and lax.axis_size("tp") == PARTS
    channels = x_weight.shape[1]
    taps = conv_x.shape[0]
    margin = taps - 1
    flat_bc = bc_weight.reshape(bc_weight.shape[0], -1)
    state_width = flat_bc.shape[1] // 2
    assert flat_bc.shape[1] == LANES
    tokens, part = prompt_embeds.shape
    rows, steps = decode_ids.shape
    asked = rows * steps
    groups = lax.axis_size("ctx")
    me_c = lax.axis_index("ctx")
    me_t = lax.axis_index("tp")
    vocab_here = embed_table.shape[0]
    bits = bits_of("ctx")
    assert len(bits) >= 2

    e2 = swapped(prompt_embeds, "tp", 2)
    e1 = swapped(prompt_embeds, "tp", 1)

    ids = decode_ids.T.reshape(-1)
    digits = jnp.stack([ids & 255, (ids >> 8) & 255, ids >> 16]).astype(BF16).reshape(-1)
    extra = EDGE - margin
    digits = jnp.pad(digits, (0, extra * part - digits.shape[0])).reshape(extra, part)
    note = jnp.concatenate([digits, prompt_embeds[-margin:]], axis=0)
    devices = groups * PARTS
    notes = lax.all_to_all(
        jnp.broadcast_to(note[None], (devices,) + note.shape), ("ctx", "tp"), 0, 0
    )
    digits = notes.reshape(groups, PARTS, EDGE, part)[:, 0, :extra].reshape(groups, -1)
    digits = digits[:, : 3 * asked].reshape(groups, 3, asked).astype(jnp.int32)
    all_ids = digits[:, 0] + digits[:, 1] * 256 + digits[:, 2] * 65536

    e3 = swapped(e2, "tp", 1)

    wanted = relative(all_ids, "ctx").reshape(-1) - me_c * vocab_here
    inside = jnp.logical_and(wanted >= 0, wanted < vocab_here)
    picked = jnp.take(embed_table, jnp.clip(wanted, 0, vocab_here - 1), axis=0)
    kept = jnp.where(inside[:, None], picked, jnp.zeros((), BF16))
    for bit in bits:
        half = kept.shape[0] // 2
        kept = kept[:half] + swapped(kept[half:], "ctx", bit)
    near = swapped(kept, "tp", 2)
    over = swapped(jnp.concatenate([kept, near], axis=0), "tp", 1)

    weights = [
        norm_gain.reshape(PARTS, 1, part),
        x_weight,
        flat_bc,
        dt_weight,
        dt_bias.reshape(1, -1),
        decay_log.reshape(1, -1),
        conv_x,
        conv_bc.reshape(taps, -1),
        skip_gain.reshape(1, -1),
    ]
    packed = state_width + 2 * EDGE

    def front(decode, place, blocks, count):
        outs = [
            shaped((count, channels), F32),
            shaped((count, LANES), BF16),
            shaped((count, LANES), F32),
        ]
        if not decode:
            outs += [
                shaped((packed, channels), BF16),
                shaped((state_width, channels), F32),
                shaped((EDGE, channels), F32),
            ]
        joined = margin * rows if decode else EDGE
        scratch = [
            pltpu.VMEM((PARTS, count + 2 * EDGE, part), BF16),
            pltpu.VMEM((count, channels), BF16),
            pltpu.VMEM((joined + count, 2 * LANES), F32),
        ]
        return called(
            functools.partial(front_kernel, decode, rows, heads),
            [place, notes] + blocks + weights,
            outs,
            scratch,
            2 * count * PARTS * part * (channels + 2 * LANES),
            24,
        )

    ones = jnp.ones((), jnp.int32)
    place = jnp.stack([me_t, jnp.maximum(me_c - 1, 0), (me_c > 0).astype(jnp.int32)])
    y, bc, reach, message, state, decay = front(
        False, place.astype(jnp.int32), [prompt_embeds, e1, e2, e3], tokens
    )

    came, since = state, decay
    for bit in bits[:-1]:
        got = swapped(message, "ctx", bit)
        later = ((me_c & bit) != 0).astype(jnp.int32).reshape(1)
        message, state, decay, came, since = called(
            functools.partial(step_kernel, bit == bits[0]),
            [later, got, state, decay, came, since],
            [
                shaped((packed, channels), BF16),
                shaped((state_width, channels), F32),
                shaped((EDGE, channels), F32),
                shaped((state_width, channels), F32),
                shaped((EDGE, channels), F32),
            ],
            [],
            8 * state_width * channels,
            8,
        )
    got = swapped(message, "ctx", bits[-1])
    later = ((me_c & bits[-1]) != 0).astype(jnp.int32)
    back_place = jnp.stack([me_t.astype(jnp.int32), later])

    def back(decode, y, bc, reach):
        count = y.shape[0]
        sent, held = called(
            functools.partial(back_kernel, decode, heads),
            [back_place, got, state, decay, came, since, y, bc, reach, out_gain.reshape(1, -1), out_weight],
            [shaped((2, count, part), BF16), shaped((2, count, part), F32)],
            [pltpu.VMEM((count, channels), F32), pltpu.VMEM((count, channels), BF16)],
            2 * count * channels * PARTS * part,
            24,
        )
        got_near = swapped(sent, "tp", 1).astype(F32)
        far = swapped((held[0] + got_near[0]).astype(BF16), "tp", 2)
        return (held[1] + got_near[1] + far.astype(F32)).astype(BF16)

    prompt_out = back(False, y, bc, reach)

    place = jnp.stack([me_t.astype(jnp.int32), ones * (groups - 1), ones])
    blocks = [kept, over[:asked], near, over[asked:]]
    dec_y, dec_bc, dec_reach = front(True, place, blocks, asked)
    decode_out = back(True, dec_y, dec_bc, dec_reach)
    decode_out = decode_out.reshape(steps, rows, part).transpose(1, 0, 2)
    return (prompt_out, decode_out)


def solution(mesh):
    return jax.shard_map(
        on_device,
        mesh=mesh,
        in_specs=(
            P("ctx", "tp"),
            P("ctx", None),
            P("ctx", "tp"),
            P(),
            P(None, "tp"),
            P(None, "tp", None, None),
            P(None, "tp"),
            P("tp"),
            P("tp"),
            P(None, "tp"),
            P(None, "tp", None, None),
            P("tp"),
            P("tp"),
            P("tp", None),
        ),
        out_specs=(P("ctx", "tp"), P("ctx", None, "tp")),
        check_vma=False,
    )
```

```python
import functools

import jax
import jax.numpy as jnp
from jax import lax
from jax.experimental import pallas as pl
from jax.experimental.pallas import tpu as pltpu
from jax.sharding import PartitionSpec as P

EPS = 1e-05
BF16 = jnp.bfloat16
F32 = jnp.float32
LANES = 128
PARTS = 4
EDGE = 8
MEBI = 1024 * 1024


def swapped(value, axis, bit):
    count = lax.axis_size(axis)
    return lax.ppermute(value, axis, [(i, i ^ bit) for i in range(count)])


def bits_of(axis):
    count = lax.axis_size(axis)
    assert count & (count - 1) == 0
    return [1 << k for k in range(count.bit_length() - 1)]


def dot(a, b):
    return jnp.dot(a, b, preferred_element_type=F32)


def across(a, b, axis):
    return lax.dot_general(a, b, (((axis,), (axis,)), ((), ())), preferred_element_type=F32)


def halves(value):
    high = value.astype(BF16)
    low = (value - high.astype(F32)).astype(BF16)
    return high, low


def iota(shape, axis):
    return lax.broadcasted_iota(jnp.int32, shape, axis)


def spreader(width, channels):
    head = iota((2 * LANES, channels), 0) & (LANES - 1)
    return jnp.where(head == iota((2 * LANES, channels), 1) // width, 1.0, 0.0).astype(BF16)


def widened(per_head, spread):
    high, low = halves(per_head)
    return dot(jnp.concatenate([high, low], axis=1), spread)


def padded(row):
    return jnp.concatenate([row, jnp.zeros((row.shape[0], LANES - row.shape[1]), F32)], axis=1)


def silu(value):
    return value / (1.0 + jnp.exp(-value))


def started(pairs, sems, first=0):
    copies = [
        pltpu.make_async_copy(source, target, sems.at[first + at])
        for at, (source, target) in enumerate(pairs)
    ]
    for copy in copies:
        copy.start()
    return copies


def front_kernel(
    decode,
    rows,
    heads,
    place,
    edge0,
    edge1,
    edge2,
    edge3,
    own_in,
    over1,
    over2,
    over3,
    gain_in,
    x_weight_in,
    bc_weight_in,
    dt_weight_in,
    dt_bias_in,
    decay_log_in,
    conv_x_in,
    conv_bc_in,
    skip_gain_in,
    y_out,
    bc_out,
    reach_out,
    *rest,
):
    if not decode:
        message_out, state_out, own = rest[:3]
        rest = rest[3:]
    (
        normed,
        x_conv,
        joined,
        gain,
        x_weight,
        bc_weight,
        dt_weight,
        dt_bias,
        decay_log,
        conv_x,
        conv_bc,
        skip_gain,
        sems,
    ) = rest
    tokens, part = over1.shape
    chunks, _, step_lanes = x_weight.shape
    channels = chunks * step_lanes
    width = channels // heads
    state_width = bc_weight.shape[0] // 2
    taps = conv_x.shape[0]
    margin = taps - 1
    me, edge_on = place[0], place[1]
    if decode:
        own = own_in
        early = []
    else:
        early = started([(own_in, own)], sems)
    early += started([(gain_in, gain)], sems, 1)
    chunk_copies = started(
        [(x_weight_in.at[:, pl.ds(c * step_lanes, step_lanes)], x_weight.at[c]) for c in range(chunks)],
        sems,
        2,
    )
    late = started(
        [
            (conv_x_in, conv_x),
            (bc_weight_in, bc_weight),
            (dt_weight_in, dt_weight),
            (dt_bias_in, dt_bias),
            (decay_log_in, decay_log),
            (conv_bc_in, conv_bc),
            (skip_gain_in, skip_gain),
        ],
        sems,
        2 + chunks,
    )
    for copy in early:
        copy.wait()

    blocks = [ref[...].astype(F32) for ref in (own, over1, over2, over3)]
    square = sum(jnp.sum(b * b, axis=1, keepdims=True) for b in blocks)
    factor = lax.rsqrt(square / (PARTS * part) + EPS)
    for r in range(PARTS):
        normed[me ^ r, :tokens, :] = (blocks[r] * factor * gain[me ^ r]).astype(BF16)
    valid = jnp.logical_and(iota((EDGE, part), 0) >= EDGE - margin, edge_on > 0)
    at = EDGE if decode else 0
    edges = [
        jnp.where(valid, ref[...].astype(F32)[at : at + EDGE], 0.0)
        for ref in (edge0, edge1, edge2, edge3)
    ]
    square = sum(jnp.sum(e * e, axis=1, keepdims=True) for e in edges)
    factor = lax.rsqrt(square / (PARTS * part) + EPS)
    for r in range(PARTS):
        edge = edges[r] * factor * gain[me ^ r]
        normed[me ^ r, tokens:, :] = jnp.concatenate([edge, jnp.zeros_like(edge)], axis=0).astype(BF16)

    def projected(weight_of):
        return sum(dot(normed[j], weight_of(j)) for j in range(PARTS))

    def convolved(raw, taps_of):
        raw = raw.astype(BF16).astype(F32)
        lanes = raw.shape[1]
        edge = raw[tokens : tokens + EDGE]
        if decode:
            for m in range(margin):
                one = edge[EDGE - margin + m : EDGE - margin + m + 1]
                joined[m * rows : (m + 1) * rows, :lanes] = jnp.broadcast_to(one, (rows, lanes))
            joined[margin * rows : margin * rows + tokens, :lanes] = raw[:tokens]
            starts = [k * rows for k in range(taps)]
        else:
            joined[:EDGE, :lanes] = edge
            joined[EDGE : EDGE + tokens, :lanes] = raw[:tokens]
            starts = [EDGE - margin + k for k in range(taps)]
        total = sum(taps_of(k) * joined[s : s + tokens, :lanes] for k, s in enumerate(starts))
        return silu(total)

    late[0].wait()
    for c in range(chunks):
        chunk_copies[c].wait()
        lane = c * step_lanes
        raw = projected(lambda j: x_weight[c, j * part : (j + 1) * part, :])
        x_conv[:, lane : lane + step_lanes] = convolved(
            raw, lambda k: conv_x[k : k + 1, lane : lane + step_lanes]
        ).astype(BF16)

    for copy in late[1:]:
        copy.wait()
    fill = jnp.zeros((LANES - heads, PARTS * part), BF16)
    side = jnp.concatenate([bc_weight[...], dt_weight[...], fill], axis=0)
    raw = sum(across(normed[j], side[:, j * part : (j + 1) * part], 1) for j in range(PARTS))
    bc_taps = jnp.concatenate([conv_bc[:, 0, :], conv_bc[:, 1, :]], axis=1)
    bc_conv = convolved(raw[:, : 2 * state_width], lambda k: bc_taps[k : k + 1])
    bc_out[...] = bc_conv.astype(BF16)
    pre = raw[:tokens, 2 * state_width :] + padded(dt_bias[...])
    step_size = jnp.maximum(pre, 0.0) + jnp.log1p(jnp.exp(-jnp.abs(pre)))
    b_rows = bc_conv[:, :state_width].astype(BF16)
    c_rows = bc_conv[:, state_width:].astype(BF16)

    t_at = iota((tokens, tokens), 0)
    s_at = iota((tokens, tokens), 1)
    mask = t_at >= s_at
    if decode:
        mask = jnp.logical_and(mask, t_at % rows == s_at % rows)
    logs = step_size * -jnp.exp(padded(decay_log[...]))
    high, low = halves(logs)
    lowest = (logs - high.astype(F32) - low.astype(F32)).astype(BF16)
    sums = dot(
        jnp.where(mask, 1.0, 0.0).astype(BF16), jnp.concatenate([high, low, lowest], axis=1)
    )
    cum_log = sums[:, :LANES] + sums[:, LANES : 2 * LANES] + sums[:, 2 * LANES :]
    reach_out[...] = jnp.exp(cum_log)
    cum_across = cum_log.T
    step_across = step_size.T
    scores = across(c_rows, b_rows, 1)
    spread = spreader(width, channels)
    skip_row = widened(jnp.broadcast_to(padded(skip_gain[...]), (EDGE, LANES)), spread)[:1]

    per_tile = LANES // width
    lane_head = iota((tokens, LANES), 1) // width
    for tile in range(channels // LANES):
        lanes = slice(tile * LANES, (tile + 1) * LANES)
        x_tile = x_conv[:, lanes].astype(F32)
        left, right = [], []
        for k in range(per_tile):
            h = tile * per_tile + k
            gaps = cum_log[:, h : h + 1] - cum_across[h : h + 1, :]
            decays = jnp.exp(jnp.where(mask, gaps, -1e30))
            left.append((scores * decays * step_across[h : h + 1, :]).astype(BF16))
            right.append(jnp.where(lane_head == k, x_tile, 0.0).astype(BF16))
        within = sum(dot(a, b) for a, b in zip(left, right))
        y_out[:, lanes] = within + skip_row[:, lanes] * x_tile

    if not decode:
        last = cum_log[tokens - 1 : tokens]
        to_end = jnp.exp(last - cum_log) * step_size
        b_turned = bc_conv.T[:state_width].astype(BF16)
        decay = widened(jnp.broadcast_to(jnp.exp(last), (EDGE, LANES)), spread)
        state_out[state_width:, :] = decay
        high, low = halves(decay[:1])
        at = iota((2 * EDGE, channels), 0)
        message_out[state_width:, :] = jnp.where(
            at == 0, high.astype(F32), jnp.where(at == 1, low.astype(F32), 0.0)
        ).astype(BF16)
        for lane in range(0, channels, step_lanes):
            lanes = slice(lane, lane + step_lanes)
            scale = widened(to_end, spread[:, lanes])
            weighted = (x_conv[:, lanes].astype(F32) * scale).astype(BF16)
            state = dot(b_turned, weighted)
            state_out[:state_width, lanes] = state
            message_out[:state_width, lanes] = state.astype(BF16)


def unpacked(message, state_width):
    other = message[:state_width, :].astype(F32)
    tail = message[state_width:, :].astype(F32)
    return other, tail[0:1] + tail[1:2]


def step_kernel(first, place, message, state, came, message_out, state_out, came_out):
    later = place[0] > 0
    state_width = state.shape[0] - EDGE
    channels = state.shape[1]
    other, other_decay = unpacked(message, state_width)
    mine, my_decay = state[:state_width, :], state[state_width : state_width + 1, :]
    if first:
        before, passed = jnp.zeros_like(mine), jnp.ones_like(my_decay)
    else:
        before, passed = came[:state_width, :], came[state_width : state_width + 1, :]
    came_out[:state_width, :] = jnp.where(later, passed * other + before, before)
    passed = jnp.where(later, passed * other_decay, passed)
    came_out[state_width:, :] = jnp.broadcast_to(passed, (EDGE, channels))
    total = jnp.where(later, my_decay * other + mine, other_decay * mine + other)
    decayed = my_decay * other_decay
    state_out[:state_width, :] = total
    state_out[state_width:, :] = jnp.broadcast_to(decayed, (EDGE, channels))
    message_out[:state_width, :] = total.astype(BF16)
    high, low = halves(decayed)
    at = iota((2 * EDGE, channels), 0)
    message_out[state_width:, :] = jnp.where(
        at == 0, high.astype(F32), jnp.where(at == 1, low.astype(F32), 0.0)
    ).astype(BF16)


def back_kernel(
    decode,
    heads,
    place,
    message,
    held,
    y,
    bc,
    reach,
    gain_in,
    weight_in,
    sent3,
    sent1,
    kept2,
    kept0,
    full,
    mixed,
    gain,
    weight,
    sems,
):
    me, later = place[0], place[1] > 0
    state_width = held.shape[0] - EDGE
    tokens, channels = y.shape
    part = weight.shape[2]
    order = (3, 1, 2, 0)
    copies = started(
        [(gain_in, gain)]
        + [
            (weight_in.at[:, pl.ds(pl.multiple_of((me ^ r) * part, part), part)], weight.at[at])
            for at, r in enumerate(order)
        ],
        sems,
    )
    other, other_decay = unpacked(message, state_width)
    mine, my_decay = held[:state_width, :], held[state_width : state_width + 1, :]
    if decode:
        incoming = jnp.where(later, my_decay * other + mine, other_decay * mine + other)
    else:
        incoming = jnp.where(later, my_decay * other + mine, mine)
    high, low = halves(incoming)
    blank = jnp.zeros_like(high)
    table = jnp.concatenate([blank, high, blank, low], axis=0)
    twice = jnp.concatenate([bc[...], bc[...]], axis=1)
    spread = spreader(channels // heads, channels)
    step_lanes = 2 * LANES
    square = jnp.zeros((tokens, 1), F32)
    for lane in range(0, channels, step_lanes):
        lanes = slice(lane, lane + step_lanes)
        total = y[:, lanes] + dot(twice, table[:, lanes]) * widened(reach[...], spread[:, lanes])
        full[:, lanes] = total
        square = square + jnp.sum(total * total, axis=1, keepdims=True)
    factor = lax.rsqrt(square / channels + EPS)
    copies[0].wait()
    mixed[...] = (full[...] * factor * gain[...]).astype(BF16)
    for at, out in enumerate((sent3, sent1, kept2, kept0)):
        copies[1 + at].wait()
        out[...] = dot(mixed[...], weight[at]).astype(out.dtype)


def far_kernel(place, kept, got, out):
    out[...] = (kept[...] + got[...].astype(F32)).astype(BF16)


def total_kernel(place, kept, got, far, out):
    out[...] = (kept[...] + got[...].astype(F32) + far[...].astype(F32)).astype(BF16)


def note_kernel(margin, place, ids_in, embeds_in, note, ids, embeds, sems):
    steps = ids_in.shape[0]
    for copy in started(
        [(ids_in, ids), (embeds_in.at[pl.ds(embeds_in.shape[0] - 2 * EDGE, 2 * EDGE), :], embeds)], sems
    ):
        copy.wait()
    ids = ids[...]
    part = embeds.shape[1]
    digits = [padded(d.astype(F32)) for d in (ids & 255, (ids >> 8) & 255, ids >> 16)]
    blank = jnp.zeros((steps, part - 3 * LANES), F32)
    top = jnp.concatenate(digits + [blank], axis=1)
    middle = jnp.zeros((EDGE - margin - steps, part), F32)
    last = embeds[...].astype(F32)[2 * EDGE - margin :]
    note[...] = jnp.concatenate([top, middle, last], axis=0).astype(BF16)


def join_kernel(place, mine, got, out):
    out[...] = jnp.concatenate([mine[...].astype(F32), got[...].astype(F32)], axis=0).astype(BF16)


def last_join_kernel(place, mine, got, out, picked, held):
    count = mine.shape[0]
    held[:count, :] = mine[...].astype(F32)
    held[count:, :] = got[...].astype(F32)
    out[...] = held[...].astype(BF16)
    edges = [held[pl.ds(pl.multiple_of(place[k] * EDGE, EDGE), EDGE), :] for k in range(2)]
    picked[...] = jnp.concatenate(edges, axis=0).astype(BF16)


def lookup_kernel(steps, rows, place, notes, table_in, kept_out, sent_out, table, wanted, found, sems):
    chunks, chunk, _ = table.shape
    copies = started(
        [(table_in.at[pl.ds(c * chunk, chunk), :], table.at[c]) for c in range(chunks)], sems
    )
    first = (place[0] * (chunks * chunk)).astype(F32)
    held = notes[...].astype(F32)
    groups = held.shape[0] // EDGE
    digits = held[:, :LANES] + held[:, LANES : 2 * LANES] * 256.0 + held[:, 2 * LANES : 3 * LANES] * 65536.0
    same = iota((rows, LANES), 0) == iota((rows, LANES), 1)
    for q in range(groups):
        for s in range(steps):
            line = jnp.broadcast_to(digits[q * EDGE + s : q * EDGE + s + 1], (rows, LANES))
            column = jnp.sum(jnp.where(same, line, 0.0), axis=1, keepdims=True) - first
            at = (q * steps + s) * rows
            wanted[at : at + rows, :] = jnp.broadcast_to(column, (rows, LANES))
    asked = groups * steps * rows
    block = min(asked, 256)
    lane = iota((block, LANES), 1).astype(F32)
    for c in range(chunks):
        copies[c].wait()
        for at in range(0, asked, block):
            gap = wanted[at : at + block, :] - lane
            hot = [
                jnp.where(gap == float(c * chunk + k), 1.0, 0.0).astype(BF16)
                for k in range(0, chunk, LANES)
            ]
            term = dot(jnp.concatenate(hot, axis=1), table[c])
            if c == 0:
                found[at : at + block, :] = term
            else:
                found[at : at + block, :] += term
    kept_out[...] = found[: asked // 2, :].astype(BF16)
    sent_out[...] = found[asked // 2 :, :].astype(BF16)


def fold_kernel(place, kept, got, kept_out, *sent_out):
    total = (kept[...].astype(F32) + got[...].astype(F32)).astype(BF16)
    if sent_out:
        half = kept_out.shape[0]
        kept_out[...] = total[:half]
        sent_out[0][...] = total[half:]
    else:
        kept_out[...] = total


VMEM = pl.BlockSpec(memory_space=pltpu.VMEM)
SMEM = pl.BlockSpec(memory_space=pltpu.SMEM)
ANY = pl.BlockSpec(memory_space=pl.ANY)


def called(kernel, place, inputs, outs, scratch=(), flops=1000, limit=4, far=()):
    moved = sum(v.size * v.dtype.itemsize for v in inputs)
    moved += sum(o.size * o.dtype.itemsize for o in outs)
    return pl.pallas_call(
        kernel,
        out_shape=outs,
        in_specs=[SMEM] + [ANY if at in far else VMEM for at in range(len(inputs))],
        out_specs=[VMEM] * len(outs),
        scratch_shapes=list(scratch),
        compiler_params=pltpu.CompilerParams(vmem_limit_bytes=limit * MEBI),
        cost_estimate=pl.CostEstimate(flops=flops, bytes_accessed=moved, transcendentals=0),
    )(place, *inputs)


def shaped(shape, dtype):
    return jax.ShapeDtypeStruct(shape, dtype)


def on_device(
    prompt_embeds,
    decode_ids,
    embed_table,
    norm_gain,
    x_weight,
    bc_weight,
    dt_weight,
    dt_bias,
    decay_log,
    conv_x,
    conv_bc,
    skip_gain,
    out_gain,
    out_weight,
):
    heads = dt_weight.shape[1]
    assert bc_weight.shape[1] == 1 and lax.axis_size("tp") == PARTS
    channels = x_weight.shape[1]
    taps = conv_x.shape[0]
    margin = taps - 1
    turned_bc = bc_weight.transpose(1, 2, 3, 0).reshape(-1, bc_weight.shape[0])
    turned_dt = dt_weight.T
    state_width = turned_bc.shape[0] // 2
    assert turned_bc.shape[0] == LANES
    tokens, part = prompt_embeds.shape
    rows, steps = decode_ids.shape
    assert steps + margin <= EDGE and rows <= LANES and part >= 3 * LANES
    asked = rows * steps
    groups = lax.axis_size("ctx")
    me_c = lax.axis_index("ctx").astype(jnp.int32)
    me_t = lax.axis_index("tp").astype(jnp.int32)
    vocab_here = embed_table.shape[0]
    bits = bits_of("ctx")
    assert len(bits) >= 2
    none = jnp.zeros((1,), jnp.int32)

    e2 = swapped(prompt_embeds, "tp", 2)
    e1 = swapped(prompt_embeds, "tp", 1)

    (notes,) = called(
        functools.partial(note_kernel, margin),
        none,
        [decode_ids.T, prompt_embeds],
        [shaped((EDGE, part), BF16)],
        [
            pltpu.VMEM((steps, rows), jnp.int32),
            pltpu.VMEM((2 * EDGE, part), BF16),
            pltpu.SemaphoreType.DMA((2,)),
        ],
        far=(0, 1),
    )

    def position(other):
        apart = me_c ^ other
        return sum(((apart >> k) & 1) << (len(bits) - 1 - k) for k in range(len(bits)))

    for bit in reversed(bits):
        got = swapped(notes, "ctx", bit)
        size = 2 * notes.shape[0]
        if bit > 1:
            (notes,) = called(join_kernel, none, [notes, got], [shaped((size, part), BF16)])
        else:
            notes, edge0 = called(
                last_join_kernel,
                jnp.stack([position(jnp.maximum(me_c - 1, 0)), position(groups - 1)]),
                [notes, got],
                [shaped((size, part), BF16), shaped((2 * EDGE, part), BF16)],
                [pltpu.VMEM((size, part), F32)],
            )
    edge2 = swapped(edge0, "tp", 2)
    edge1 = swapped(edge0, "tp", 1)
    e3 = swapped(e2, "tp", 1)
    edge3 = swapped(edge2, "tp", 1)
    edges = [edge0, edge1, edge2, edge3]

    half = groups * asked // 2
    chunk = min(vocab_here, 1024)
    assert vocab_here % chunk == 0
    kept, sent = called(
        functools.partial(lookup_kernel, steps, rows),
        me_c.reshape(1),
        [notes, embed_table],
        [shaped((half, part), BF16), shaped((half, part), BF16)],
        [
            pltpu.VMEM((vocab_here // chunk, chunk, part), BF16),
            pltpu.VMEM((2 * half, LANES), F32),
            pltpu.VMEM((2 * half, part), F32),
            pltpu.SemaphoreType.DMA((vocab_here // chunk,)),
        ],
        flops=4 * half * vocab_here * part,
        limit=40 if half > 512 else 16,
        far=(1,),
    )
    for bit in bits:
        got = swapped(sent, "ctx", bit)
        half = half // 2
        if bit == bits[-1]:
            (kept,) = called(fold_kernel, none, [kept, got], [shaped((asked, part), BF16)])
        else:
            kept, sent = called(
                fold_kernel,
                none,
                [kept, got],
                [shaped((half, part), BF16), shaped((half, part), BF16)],
                limit=16 if half > 512 else 4,
            )
    near = swapped(kept, "tp", 2)
    over1 = swapped(kept, "tp", 1)
    over3 = swapped(near, "tp", 1)

    weights = [
        norm_gain.reshape(PARTS, 1, part),
        x_weight,
        turned_bc,
        turned_dt,
        dt_bias.reshape(1, -1),
        decay_log.reshape(1, -1),
        conv_x,
        conv_bc.reshape(taps, 2, -1),
        skip_gain.reshape(1, -1),
    ]
    packed = state_width + 2 * EDGE
    step_lanes = 2 * LANES
    chunks = channels // step_lanes

    def front(decode, place, blocks, count):
        outs = [
            shaped((count, channels), F32),
            shaped((count, LANES), BF16),
            shaped((count, LANES), F32),
        ]
        scratch = []
        if not decode:
            outs += [
                shaped((packed, channels), BF16),
                shaped((state_width + EDGE, channels), F32),
            ]
            scratch = [pltpu.VMEM((count, part), BF16)]
        joined = margin * rows if decode else EDGE
        scratch += [
            pltpu.VMEM((PARTS, count + 2 * EDGE, part), BF16),
            pltpu.VMEM((count, channels), BF16),
            pltpu.VMEM((joined + count, step_lanes), F32),
            pltpu.VMEM((PARTS, 1, part), F32),
            pltpu.VMEM((chunks, PARTS * part, step_lanes), BF16),
        ]
        scratch += [pltpu.VMEM(w.shape, w.dtype) for w in weights[2:]]
        scratch += [pltpu.SemaphoreType.DMA((chunks + 9,))]
        return called(
            functools.partial(front_kernel, decode, rows, heads),
            place,
            edges + blocks + weights,
            outs,
            scratch,
            2 * count * PARTS * part * (channels + 2 * LANES),
            24,
            tuple(range(8, 8 + len(weights))) + (() if decode else (4,)),
        )

    y, bc, reach, message, state = front(
        False,
        jnp.stack([me_t, (me_c > 0).astype(jnp.int32)]),
        [prompt_embeds, e1, e2, e3],
        tokens,
    )

    came = state
    for bit in bits[:-1]:
        got = swapped(message, "ctx", bit)
        later = ((me_c & bit) != 0).astype(jnp.int32).reshape(1)
        message, state, came = called(
            functools.partial(step_kernel, bit == bits[0]),
            later,
            [got, state, came],
            [
                shaped((packed, channels), BF16),
                shaped((state_width + EDGE, channels), F32),
                shaped((state_width + EDGE, channels), F32),
            ],
            flops=8 * state_width * channels,
        )
    got = swapped(message, "ctx", bits[-1])
    later = ((me_c & bits[-1]) != 0).astype(jnp.int32)
    back_place = jnp.stack([me_t, later])

    def back(decode, held, y, bc, reach):
        count = y.shape[0]
        sent3, sent1, kept2, kept0 = called(
            functools.partial(back_kernel, decode, heads),
            back_place,
            [got, held, y, bc, reach, out_gain.reshape(1, -1), out_weight],
            [shaped((count, part), BF16)] * 2 + [shaped((count, part), F32)] * 2,
            [
                pltpu.VMEM((count, channels), F32),
                pltpu.VMEM((count, channels), BF16),
                pltpu.VMEM((1, channels), F32),
                pltpu.VMEM((PARTS, channels, part), BF16),
                pltpu.SemaphoreType.DMA((PARTS + 1,)),
            ],
            2 * count * channels * PARTS * part,
            16,
            (5, 6),
        )
        got3 = swapped(sent3, "tp", 1)
        got1 = swapped(sent1, "tp", 1)
        (far,) = called(far_kernel, none, [kept2, got3], [shaped((count, part), BF16)])
        far = swapped(far, "tp", 2)
        (total,) = called(total_kernel, none, [kept0, got1, far], [shaped((count, part), BF16)])
        return total

    prompt_out = back(False, came, y, bc, reach)

    dec_y, dec_bc, dec_reach = front(
        True, jnp.stack([me_t, jnp.ones((), jnp.int32)]), [kept, over1, near, over3], asked
    )
    decode_out = back(True, state, dec_y, dec_bc, dec_reach)
    decode_out = decode_out.reshape(steps, rows, part).transpose(1, 0, 2)
    return (prompt_out, decode_out)


def solution(mesh):
    return jax.shard_map(
        on_device,
        mesh=mesh,
        in_specs=(
            P("ctx", "tp"),
            P("ctx", None),
            P("ctx", "tp"),
            P(),
            P(None, "tp"),
            P(None, "tp", None, None),
            P(None, "tp"),
            P("tp"),
            P("tp"),
            P(None, "tp"),
            P(None, "tp", None, None),
            P("tp"),
            P("tp"),
            P("tp", None),
        ),
        out_specs=(P("ctx", "tp"), P("ctx", None, "tp")),
        check_vma=False,
    )
```

```python
import functools

import jax
import jax.numpy as jnp
from jax import lax
from jax.experimental import pallas as pl
from jax.experimental.pallas import tpu as pltpu
from jax.sharding import PartitionSpec as P

EPS = 1e-05
BF16 = jnp.bfloat16
F32 = jnp.float32
LANES = 128
PARTS = 4
EDGE = 8
MEBI = 1024 * 1024


def swapped(value, axis, bit):
    count = lax.axis_size(axis)
    return lax.ppermute(value, axis, [(i, i ^ bit) for i in range(count)])


def bits_of(axis):
    count = lax.axis_size(axis)
    assert count & (count - 1) == 0
    return [1 << k for k in range(count.bit_length() - 1)]


def dot(a, b):
    return jnp.dot(a, b, preferred_element_type=F32)


def across(a, b, axis):
    return lax.dot_general(a, b, (((axis,), (axis,)), ((), ())), preferred_element_type=F32)


def halves(value):
    high = value.astype(BF16)
    low = (value - high.astype(F32)).astype(BF16)
    return high, low


def iota(shape, axis):
    return lax.broadcasted_iota(jnp.int32, shape, axis)


def spreader(width, channels):
    head = iota((2 * LANES, channels), 0) & (LANES - 1)
    return jnp.where(head == iota((2 * LANES, channels), 1) // width, 1.0, 0.0).astype(BF16)


def widened(per_head, spread):
    high, low = halves(per_head)
    return dot(jnp.concatenate([high, low], axis=1), spread)


def padded(row):
    return jnp.concatenate([row, jnp.zeros((row.shape[0], LANES - row.shape[1]), F32)], axis=1)


def silu(value):
    return value / (1.0 + jnp.exp(-value))


def started(pairs, sems, first=0):
    copies = [
        pltpu.make_async_copy(source, target, sems.at[first + at])
        for at, (source, target) in enumerate(pairs)
    ]
    for copy in copies:
        copy.start()
    return copies


def front_kernel(
    decode,
    rows,
    heads,
    place,
    edge0,
    edge1,
    edge2,
    edge3,
    own,
    over1,
    over2,
    over3,
    gain,
    x_weight,
    bc_weight,
    dt_weight,
    dt_bias,
    decay_log,
    conv_x,
    conv_bc,
    skip_gain,
    y_out,
    bc_out,
    reach_out,
    *rest,
):
    if not decode:
        message_out, state_out = rest[:2]
        rest = rest[2:]
    normed, x_conv, joined = rest
    tokens, part = own.shape
    channels = x_weight.shape[1]
    step_lanes = 2 * LANES
    width = channels // heads
    state_width = bc_weight.shape[0] // 2
    taps = conv_x.shape[0]
    margin = taps - 1
    me, edge_on = place[0], place[1]

    blocks = [ref[...].astype(F32) for ref in (own, over1, over2, over3)]
    square = sum(jnp.sum(b * b, axis=1, keepdims=True) for b in blocks)
    factor = lax.rsqrt(square / (PARTS * part) + EPS)
    for r in range(PARTS):
        normed[me ^ r, :tokens, :] = (blocks[r] * factor * gain[me ^ r]).astype(BF16)
    valid = jnp.logical_and(iota((EDGE, part), 0) >= EDGE - margin, edge_on > 0)
    at = EDGE if decode else 0
    edges = [
        jnp.where(valid, ref[...].astype(F32)[at : at + EDGE], 0.0)
        for ref in (edge0, edge1, edge2, edge3)
    ]
    square = sum(jnp.sum(e * e, axis=1, keepdims=True) for e in edges)
    factor = lax.rsqrt(square / (PARTS * part) + EPS)
    for r in range(PARTS):
        edge = edges[r] * factor * gain[me ^ r]
        normed[me ^ r, tokens:, :] = jnp.concatenate([edge, jnp.zeros_like(edge)], axis=0).astype(BF16)

    def projected(weight_of):
        return sum(dot(normed[j], weight_of(j)) for j in range(PARTS))

    def convolved(raw, taps_of):
        raw = raw.astype(BF16).astype(F32)
        lanes = raw.shape[1]
        edge = raw[tokens : tokens + EDGE]
        if decode:
            for m in range(margin):
                one = edge[EDGE - margin + m : EDGE - margin + m + 1]
                joined[m * rows : (m + 1) * rows, :lanes] = jnp.broadcast_to(one, (rows, lanes))
            joined[margin * rows : margin * rows + tokens, :lanes] = raw[:tokens]
            starts = [k * rows for k in range(taps)]
        else:
            joined[:EDGE, :lanes] = edge
            joined[EDGE : EDGE + tokens, :lanes] = raw[:tokens]
            starts = [EDGE - margin + k for k in range(taps)]
        total = sum(taps_of(k) * joined[s : s + tokens, :lanes] for k, s in enumerate(starts))
        return silu(total)

    for lane in range(0, channels, step_lanes):
        raw = projected(lambda j: x_weight[j * part : (j + 1) * part, lane : lane + step_lanes])
        x_conv[:, lane : lane + step_lanes] = convolved(
            raw, lambda k: conv_x[k : k + 1, lane : lane + step_lanes]
        ).astype(BF16)

    fill = jnp.zeros((LANES - heads, PARTS * part), BF16)
    side = jnp.concatenate([bc_weight[...], dt_weight[...], fill], axis=0)
    raw = sum(across(normed[j], side[:, j * part : (j + 1) * part], 1) for j in range(PARTS))
    bc_taps = jnp.concatenate([conv_bc[:, 0, :], conv_bc[:, 1, :]], axis=1)
    bc_conv = convolved(raw[:, : 2 * state_width], lambda k: bc_taps[k : k + 1])
    bc_out[...] = bc_conv.astype(BF16)
    pre = raw[:tokens, 2 * state_width :] + padded(dt_bias[...])
    step_size = jnp.maximum(pre, 0.0) + jnp.log1p(jnp.exp(-jnp.abs(pre)))
    b_rows = bc_conv[:, :state_width].astype(BF16)
    c_rows = bc_conv[:, state_width:].astype(BF16)

    t_at = iota((tokens, tokens), 0)
    s_at = iota((tokens, tokens), 1)
    mask = t_at >= s_at
    if decode:
        mask = jnp.logical_and(mask, t_at % rows == s_at % rows)
    logs = step_size * -jnp.exp(padded(decay_log[...]))
    high, low = halves(logs)
    lowest = (logs - high.astype(F32) - low.astype(F32)).astype(BF16)
    sums = dot(
        jnp.where(mask, 1.0, 0.0).astype(BF16), jnp.concatenate([high, low, lowest], axis=1)
    )
    cum_log = sums[:, :LANES] + sums[:, LANES : 2 * LANES] + sums[:, 2 * LANES :]
    reach_out[...] = jnp.exp(cum_log)
    cum_across = cum_log.T
    step_across = step_size.T
    scores = across(c_rows, b_rows, 1)
    spread = spreader(width, channels)
    skip_row = widened(jnp.broadcast_to(padded(skip_gain[...]), (EDGE, LANES)), spread)[:1]

    per_tile = LANES // width
    lane_head = iota((tokens, LANES), 1) // width
    for tile in range(channels // LANES):
        lanes = slice(tile * LANES, (tile + 1) * LANES)
        x_tile = x_conv[:, lanes].astype(F32)
        left, right = [], []
        for k in range(per_tile):
            h = tile * per_tile + k
            gaps = cum_log[:, h : h + 1] - cum_across[h : h + 1, :]
            decays = jnp.exp(jnp.where(mask, gaps, -1e30))
            left.append((scores * decays * step_across[h : h + 1, :]).astype(BF16))
            right.append(jnp.where(lane_head == k, x_tile, 0.0).astype(BF16))
        within = sum(dot(a, b) for a, b in zip(left, right))
        y_out[:, lanes] = within + skip_row[:, lanes] * x_tile

    if not decode:
        last = cum_log[tokens - 1 : tokens]
        to_end = jnp.exp(last - cum_log) * step_size
        b_turned = bc_conv.T[:state_width].astype(BF16)
        decay = widened(jnp.broadcast_to(jnp.exp(last), (EDGE, LANES)), spread)
        state_out[state_width:, :] = decay
        high, low = halves(decay[:1])
        at = iota((2 * EDGE, channels), 0)
        message_out[state_width:, :] = jnp.where(
            at == 0, high.astype(F32), jnp.where(at == 1, low.astype(F32), 0.0)
        ).astype(BF16)
        for lane in range(0, channels, step_lanes):
            lanes = slice(lane, lane + step_lanes)
            scale = widened(to_end, spread[:, lanes])
            weighted = (x_conv[:, lanes].astype(F32) * scale).astype(BF16)
            state = dot(b_turned, weighted)
            state_out[:state_width, lanes] = state
            message_out[:state_width, lanes] = state.astype(BF16)


def unpacked(message, state_width):
    other = message[:state_width, :].astype(F32)
    tail = message[state_width:, :].astype(F32)
    return other, tail[0:1] + tail[1:2]


def step_kernel(first, place, message, state, came, message_out, state_out, came_out):
    later = place[0] > 0
    state_width = state.shape[0] - EDGE
    channels = state.shape[1]
    other, other_decay = unpacked(message, state_width)
    mine, my_decay = state[:state_width, :], state[state_width : state_width + 1, :]
    if first:
        before, passed = jnp.zeros_like(mine), jnp.ones_like(my_decay)
    else:
        before, passed = came[:state_width, :], came[state_width : state_width + 1, :]
    came_out[:state_width, :] = jnp.where(later, passed * other + before, before)
    passed = jnp.where(later, passed * other_decay, passed)
    came_out[state_width:, :] = jnp.broadcast_to(passed, (EDGE, channels))
    total = jnp.where(later, my_decay * other + mine, other_decay * mine + other)
    decayed = my_decay * other_decay
    state_out[:state_width, :] = total
    state_out[state_width:, :] = jnp.broadcast_to(decayed, (EDGE, channels))
    message_out[:state_width, :] = total.astype(BF16)
    high, low = halves(decayed)
    at = iota((2 * EDGE, channels), 0)
    message_out[state_width:, :] = jnp.where(
        at == 0, high.astype(F32), jnp.where(at == 1, low.astype(F32), 0.0)
    ).astype(BF16)


def back_kernel(
    decode,
    heads,
    place,
    message,
    held,
    y,
    bc,
    reach,
    gain,
    weight,
    sent3,
    sent1,
    kept2,
    kept0,
    full,
    mixed,
):
    me, later = place[0], place[1] > 0
    state_width = held.shape[0] - EDGE
    tokens, channels = y.shape
    part = weight.shape[1] // PARTS
    other, other_decay = unpacked(message, state_width)
    mine, my_decay = held[:state_width, :], held[state_width : state_width + 1, :]
    if decode:
        incoming = jnp.where(later, my_decay * other + mine, other_decay * mine + other)
    else:
        incoming = jnp.where(later, my_decay * other + mine, mine)
    high, low = halves(incoming)
    blank = jnp.zeros_like(high)
    table = jnp.concatenate([blank, high, blank, low], axis=0)
    twice = jnp.concatenate([bc[...], bc[...]], axis=1)
    spread = spreader(channels // heads, channels)
    step_lanes = 2 * LANES
    square = jnp.zeros((tokens, 1), F32)
    for lane in range(0, channels, step_lanes):
        lanes = slice(lane, lane + step_lanes)
        total = y[:, lanes] + dot(twice, table[:, lanes]) * widened(reach[...], spread[:, lanes])
        full[:, lanes] = total
        square = square + jnp.sum(total * total, axis=1, keepdims=True)
    factor = lax.rsqrt(square / channels + EPS)
    mixed[...] = (full[...] * factor * gain[...]).astype(BF16)
    for r, out in ((3, sent3), (1, sent1), (2, kept2), (0, kept0)):
        columns = pl.ds(pl.multiple_of((me ^ r) * part, part), part)
        out[...] = dot(mixed[...], weight[:, columns]).astype(out.dtype)


def far_kernel(place, kept, got, out):
    out[...] = (kept[...] + got[...].astype(F32)).astype(BF16)


def total_kernel(place, kept, got, far, out):
    out[...] = (kept[...] + got[...].astype(F32) + far[...].astype(F32)).astype(BF16)


def note_kernel(margin, place, ids_in, embeds_in, note, ids, embeds, sems):
    steps = ids_in.shape[0]
    for copy in started(
        [(ids_in, ids), (embeds_in.at[pl.ds(embeds_in.shape[0] - 2 * EDGE, 2 * EDGE), :], embeds)], sems
    ):
        copy.wait()
    ids = ids[...]
    part = embeds.shape[1]
    digits = [padded(d.astype(F32)) for d in (ids & 255, (ids >> 8) & 255, ids >> 16)]
    blank = jnp.zeros((steps, part - 3 * LANES), F32)
    top = jnp.concatenate(digits + [blank], axis=1)
    middle = jnp.zeros((EDGE - margin - steps, part), F32)
    last = embeds[...].astype(F32)[2 * EDGE - margin :]
    note[...] = jnp.concatenate([top, middle, last], axis=0).astype(BF16)


def join_kernel(place, mine, got, out):
    out[...] = jnp.concatenate([mine[...].astype(F32), got[...].astype(F32)], axis=0).astype(BF16)


def last_join_kernel(place, mine, got, out, picked, held):
    count = mine.shape[0]
    held[:count, :] = mine[...].astype(F32)
    held[count:, :] = got[...].astype(F32)
    out[...] = held[...].astype(BF16)
    edges = [held[pl.ds(pl.multiple_of(place[k] * EDGE, EDGE), EDGE), :] for k in range(2)]
    picked[...] = jnp.concatenate(edges, axis=0).astype(BF16)


def lookup_kernel(steps, rows, place, notes, table, kept_out, sent_out, wanted, found):
    chunk = min(table.shape[0], 1024)
    chunks = table.shape[0] // chunk
    first = (place[0] * (chunks * chunk)).astype(F32)
    held = notes[...].astype(F32)
    groups = held.shape[0] // EDGE
    digits = held[:, :LANES] + held[:, LANES : 2 * LANES] * 256.0 + held[:, 2 * LANES : 3 * LANES] * 65536.0
    same = iota((rows, LANES), 0) == iota((rows, LANES), 1)
    for q in range(groups):
        for s in range(steps):
            line = jnp.broadcast_to(digits[q * EDGE + s : q * EDGE + s + 1], (rows, LANES))
            column = jnp.sum(jnp.where(same, line, 0.0), axis=1, keepdims=True) - first
            at = (q * steps + s) * rows
            wanted[at : at + rows, :] = jnp.broadcast_to(column, (rows, LANES))
    asked = groups * steps * rows
    block = min(asked, 256)
    lane = iota((block, LANES), 1).astype(F32)
    for c in range(chunks):
        for at in range(0, asked, block):
            gap = wanted[at : at + block, :] - lane
            hot = [
                jnp.where(gap == float(c * chunk + k), 1.0, 0.0).astype(BF16)
                for k in range(0, chunk, LANES)
            ]
            term = dot(jnp.concatenate(hot, axis=1), table[c * chunk : (c + 1) * chunk, :])
            if c == 0:
                found[at : at + block, :] = term
            else:
                found[at : at + block, :] += term
    kept_out[...] = found[: asked // 2, :].astype(BF16)
    sent_out[...] = found[asked // 2 :, :].astype(BF16)


def fold_kernel(place, kept, got, kept_out, *sent_out):
    total = (kept[...].astype(F32) + got[...].astype(F32)).astype(BF16)
    if sent_out:
        half = kept_out.shape[0]
        kept_out[...] = total[:half]
        sent_out[0][...] = total[half:]
    else:
        kept_out[...] = total


VMEM = pl.BlockSpec(memory_space=pltpu.VMEM)
SMEM = pl.BlockSpec(memory_space=pltpu.SMEM)
HBM = pl.BlockSpec(memory_space=pltpu.HBM)


class Caller:
    def __init__(self):
        self.token = jnp.zeros((8, LANES), F32)

    def __call__(self, kernel, place, inputs, outs, scratch=(), us=1.0, limit=4, far=()):
        inputs = list(inputs)
        count = len(inputs)

        def ordered(place, token, *refs):
            refs, token_out = list(refs), refs[count]
            del refs[count]
            kernel(place, *refs)
            token_out[...] = jnp.zeros_like(token_out)

        results = pl.pallas_call(
            ordered,
            out_shape=[shaped((8, LANES), F32)] + outs,
            in_specs=[SMEM, VMEM] + [HBM if at in far else VMEM for at in range(count)],
            out_specs=[VMEM] * (1 + len(outs)),
            scratch_shapes=list(scratch),
            compiler_params=pltpu.CompilerParams(vmem_limit_bytes=limit * MEBI),
            cost_estimate=pl.CostEstimate(
                flops=int(us * 1e9), bytes_accessed=int(us * 1e6), transcendentals=0
            ),
        )(place, self.token, *inputs)
        self.token = results[0]
        return results[1:]


def shaped(shape, dtype):
    return jax.ShapeDtypeStruct(shape, dtype)


def on_device(
    prompt_embeds,
    decode_ids,
    embed_table,
    norm_gain,
    x_weight,
    bc_weight,
    dt_weight,
    dt_bias,
    decay_log,
    conv_x,
    conv_bc,
    skip_gain,
    out_gain,
    out_weight,
):
    heads = dt_weight.shape[1]
    assert bc_weight.shape[1] == 1 and lax.axis_size("tp") == PARTS
    channels = x_weight.shape[1]
    taps = conv_x.shape[0]
    margin = taps - 1
    turned_bc = bc_weight.transpose(1, 2, 3, 0).reshape(-1, bc_weight.shape[0])
    turned_dt = dt_weight.T
    state_width = turned_bc.shape[0] // 2
    assert turned_bc.shape[0] == LANES
    tokens, part = prompt_embeds.shape
    rows, steps = decode_ids.shape
    assert steps + margin <= EDGE and rows <= LANES and part >= 3 * LANES
    asked = rows * steps
    groups = lax.axis_size("ctx")
    me_c = lax.axis_index("ctx").astype(jnp.int32)
    me_t = lax.axis_index("tp").astype(jnp.int32)
    vocab_here = embed_table.shape[0]
    bits = bits_of("ctx")
    assert len(bits) >= 2
    none = jnp.zeros((1,), jnp.int32)
    called = Caller()

    e2 = swapped(prompt_embeds, "tp", 2)
    e1 = swapped(prompt_embeds, "tp", 1)

    (notes,) = called(
        functools.partial(note_kernel, margin),
        none,
        [decode_ids.T, prompt_embeds],
        [shaped((EDGE, part), BF16)],
        [
            pltpu.VMEM((steps, rows), jnp.int32),
            pltpu.VMEM((2 * EDGE, part), BF16),
            pltpu.SemaphoreType.DMA((2,)),
        ],
        us=2,
        far=(0, 1),
    )

    def position(other):
        apart = me_c ^ other
        return sum(((apart >> k) & 1) << (len(bits) - 1 - k) for k in range(len(bits)))

    for bit in reversed(bits):
        got = swapped(notes, "ctx", bit)
        size = 2 * notes.shape[0]
        if bit > 1:
            (notes,) = called(join_kernel, none, [notes, got], [shaped((size, part), BF16)], us=4)
        else:
            notes, edge0 = called(
                last_join_kernel,
                jnp.stack([position(jnp.maximum(me_c - 1, 0)), position(groups - 1)]),
                [notes, got],
                [shaped((size, part), BF16), shaped((2 * EDGE, part), BF16)],
                [pltpu.VMEM((size, part), F32)],
                us=4,
            )
    e3 = swapped(e2, "tp", 1)
    edges = [edge0] + [swapped(edge0, "tp", r) for r in range(1, PARTS)]

    half = groups * asked // 2
    assert vocab_here % min(vocab_here, 1024) == 0
    kept, sent = called(
        functools.partial(lookup_kernel, steps, rows),
        me_c.reshape(1),
        [notes, embed_table],
        [shaped((half, part), BF16), shaped((half, part), BF16)],
        [pltpu.VMEM((2 * half, LANES), F32), pltpu.VMEM((2 * half, part), F32)],
        us=3.5,
        limit=32 if half > 512 else 8,
    )

    weights = [
        norm_gain.reshape(PARTS, 1, part),
        x_weight,
        turned_bc,
        turned_dt,
        dt_bias.reshape(1, -1),
        decay_log.reshape(1, -1),
        conv_x,
        conv_bc.reshape(taps, 2, -1),
        skip_gain.reshape(1, -1),
    ]
    packed = state_width + 2 * EDGE

    def front(decode, edge_on, blocks, count):
        outs = [
            shaped((count, channels), F32),
            shaped((count, LANES), BF16),
            shaped((count, LANES), F32),
        ]
        if not decode:
            outs += [
                shaped((packed, channels), BF16),
                shaped((state_width + EDGE, channels), F32),
            ]
        joined = margin * rows if decode else EDGE
        return called(
            functools.partial(front_kernel, decode, rows, heads),
            jnp.stack([me_t, edge_on]),
            edges + blocks + weights,
            outs,
            [
                pltpu.VMEM((PARTS, count + 2 * EDGE, part), BF16),
                pltpu.VMEM((count, channels), BF16),
                pltpu.VMEM((joined + count, 2 * LANES), F32),
            ],
            us=2.5 if decode else 6,
            limit=16,
        )

    y, bc, reach, message, state = front(
        False, (me_c > 0).astype(jnp.int32), [prompt_embeds, e1, e2, e3], tokens
    )

    came = state
    for bit in bits:
        got = swapped(sent, "ctx", bit)
        half = half // 2
        if bit == bits[-1]:
            (kept,) = called(fold_kernel, none, [kept, got], [shaped((asked, part), BF16)], us=3)
        else:
            kept, sent = called(
                fold_kernel,
                none,
                [kept, got],
                [shaped((half, part), BF16), shaped((half, part), BF16)],
                us=3,
                limit=16 if half > 512 else 4,
            )
        got = swapped(message, "ctx", bit)
        later = ((me_c & bit) != 0).astype(jnp.int32)
        if bit != bits[-1]:
            message, state, came = called(
                functools.partial(step_kernel, bit == bits[0]),
                later.reshape(1),
                [got, state, came],
                [
                    shaped((packed, channels), BF16),
                    shaped((state_width + EDGE, channels), F32),
                    shaped((state_width + EDGE, channels), F32),
                ],
                us=3,
            )
    back_place = jnp.stack([me_t, later])
    near = swapped(kept, "tp", 2)
    over1 = swapped(kept, "tp", 1)
    over3 = swapped(near, "tp", 1)

    def back(decode, held, y, bc, reach):
        count = y.shape[0]
        return called(
            functools.partial(back_kernel, decode, heads),
            back_place,
            [got, held, y, bc, reach, out_gain.reshape(1, -1), out_weight],
            [shaped((count, part), BF16)] * 2 + [shaped((count, part), F32)] * 2,
            [pltpu.VMEM((count, channels), F32), pltpu.VMEM((count, channels), BF16)],
            us=2,
            limit=12,
        )

    def crossed(sent3, sent1, kept2, kept0):
        got3 = swapped(sent3, "tp", 1)
        got1 = swapped(sent1, "tp", 1)
        (far,) = called(far_kernel, none, [kept2, got3], [shaped(kept2.shape, BF16)])
        return kept0, got1, swapped(far, "tp", 2)

    def totalled(kept0, got1, far):
        return called(total_kernel, none, [kept0, got1, far], [shaped(kept0.shape, BF16)])[0]

    prompt_back = back(False, came, y, bc, reach)
    dec_y, dec_bc, dec_reach = front(
        True, jnp.ones((), jnp.int32), [kept, over1, near, over3], asked
    )
    prompt_crossed = crossed(*prompt_back)
    decode_back = back(True, state, dec_y, dec_bc, dec_reach)
    decode_crossed = crossed(*decode_back)
    decode_out = totalled(*decode_crossed)
    prompt_out = totalled(*prompt_crossed)
    decode_out = decode_out.reshape(steps, rows, part).transpose(1, 0, 2)
    return (prompt_out, decode_out)


def solution(mesh):
    return jax.shard_map(
        on_device,
        mesh=mesh,
        in_specs=(
            P("ctx", "tp"),
            P("ctx", None),
            P("ctx", "tp"),
            P(),
            P(None, "tp"),
            P(None, "tp", None, None),
            P(None, "tp"),
            P("tp"),
            P("tp"),
            P(None, "tp"),
            P(None, "tp", None, None),
            P("tp"),
            P("tp"),
            P("tp", None),
        ),
        out_specs=(P("ctx", "tp"), P("ctx", None, "tp")),
        check_vma=False,
    )
```

```python
import functools

import jax
import jax.numpy as jnp
from jax import lax
from jax.experimental import pallas as pl
from jax.experimental.pallas import tpu as pltpu
from jax.sharding import PartitionSpec as P

EPS = 1e-05
BF16 = jnp.bfloat16
F32 = jnp.float32
LANES = 128
PARTS = 4
EDGE = 8
MEBI = 1024 * 1024


def swapped(value, axis, bit):
    count = lax.axis_size(axis)
    return lax.ppermute(value, axis, [(i, i ^ bit) for i in range(count)])


def bits_of(axis):
    count = lax.axis_size(axis)
    assert count & (count - 1) == 0
    return [1 << k for k in range(count.bit_length() - 1)]


def dot(a, b):
    return jnp.dot(a, b, preferred_element_type=F32)


def across(a, b, axis):
    return lax.dot_general(a, b, (((axis,), (axis,)), ((), ())), preferred_element_type=F32)


def halves(value):
    high = value.astype(BF16)
    low = (value - high.astype(F32)).astype(BF16)
    return high, low


def iota(shape, axis):
    return lax.broadcasted_iota(jnp.int32, shape, axis)


def spreader(width, channels):
    head = iota((2 * LANES, channels), 0) & (LANES - 1)
    return jnp.where(head == iota((2 * LANES, channels), 1) // width, 1.0, 0.0).astype(BF16)


def widened(per_head, spread):
    high, low = halves(per_head)
    return dot(jnp.concatenate([high, low], axis=1), spread)


def padded(row):
    return jnp.concatenate([row, jnp.zeros((row.shape[0], LANES - row.shape[1]), F32)], axis=1)


def silu(value):
    return value / (1.0 + jnp.exp(-value))


def project_kernel(
    prompt,
    place,
    own,
    over1,
    over2,
    over3,
    gain,
    x_weight,
    bc_weight,
    dt_weight,
    dt_bias,
    x_out,
    bc_out,
    step_out,
    *rest,
):
    normed = rest[-1]
    me = place[0]
    tokens, part = own.shape
    channels, heads = x_weight.shape[1], dt_weight.shape[0]
    blocks = [ref[...].astype(F32) for ref in (own, over1, over2, over3)]
    square = sum(jnp.sum(b * b, axis=1, keepdims=True) for b in blocks)
    factor = lax.rsqrt(square / (PARTS * part) + EPS)
    for r in range(PARTS):
        normed[me ^ r] = (blocks[r] * factor * gain[me ^ r]).astype(BF16)
    fill = jnp.zeros((LANES - heads, PARTS * part), BF16)
    side = jnp.concatenate([bc_weight[...], dt_weight[...], fill], axis=0)
    raw = sum(across(normed[j], side[:, j * part : (j + 1) * part], 1) for j in range(PARTS))
    bc_out[...] = raw[:, :LANES].astype(BF16)
    pre = raw[:, LANES:] + padded(dt_bias[...])
    step_out[...] = jnp.maximum(pre, 0.0) + jnp.log1p(jnp.exp(-jnp.abs(pre)))
    last = 2 * EDGE
    if prompt:
        rest[0][:, channels:] = raw[tokens - last :, :LANES].astype(BF16)
        rest[1][...] = x_weight[...]
    for lane in range(0, channels, 2 * LANES):
        lanes = slice(lane, lane + 2 * LANES)
        raw = sum(dot(normed[j], x_weight[j * part : (j + 1) * part, lanes]) for j in range(PARTS))
        x_out[:, lanes] = raw.astype(BF16)
        if prompt:
            rest[0][:, lanes] = raw[tokens - last :].astype(BF16)


def summed_logs(step_size, decay_log, mask):
    logs = step_size * -jnp.exp(padded(decay_log[...]))
    high, low = halves(logs)
    lowest = (logs - high.astype(F32) - low.astype(F32)).astype(BF16)
    sums = dot(
        jnp.where(mask, 1.0, 0.0).astype(BF16), jnp.concatenate([high, low, lowest], axis=1)
    )
    return sums[:, :LANES] + sums[:, LANES : 2 * LANES] + sums[:, 2 * LANES :]


def joined_taps(conv_bc):
    return jnp.concatenate([conv_bc[:, 0, :], conv_bc[:, 1, :]], axis=1)


def block_mask(tokens, rows):
    t_at = iota((tokens, tokens), 0)
    s_at = iota((tokens, tokens), 1)
    mask = t_at >= s_at
    return mask if rows == 1 else jnp.logical_and(mask, t_at % rows == s_at % rows)


def mixed_rows(rows, heads, x_conv, bc_conv, step_size, cum_log, skip_gain, y_out):
    tokens, channels = x_conv.shape
    width = channels // heads
    state_width = bc_conv.shape[1] // 2
    mask = block_mask(tokens, rows)
    b_rows = bc_conv[:, :state_width].astype(BF16)
    c_rows = bc_conv[:, state_width:].astype(BF16)
    cum_across = cum_log.T
    step_across = step_size.T
    scores = across(c_rows, b_rows, 1)
    spread = spreader(width, channels)
    skip_row = widened(jnp.broadcast_to(padded(skip_gain[...]), (EDGE, LANES)), spread)[:1]
    per_tile = LANES // width
    lane_head = iota((tokens, LANES), 1) // width
    for tile in range(channels // LANES):
        lanes = slice(tile * LANES, (tile + 1) * LANES)
        x_tile = x_conv[:, lanes].astype(F32)
        within = skip_row[:, lanes] * x_tile
        for k in range(per_tile):
            h = tile * per_tile + k
            gaps = cum_log[:, h : h + 1] - cum_across[h : h + 1, :]
            decays = jnp.exp(jnp.where(mask, gaps, -1e30))
            mixing = (scores * decays * step_across[h : h + 1, :]).astype(BF16)
            within += dot(mixing, jnp.where(lane_head == k, x_tile, 0.0).astype(BF16))
        y_out[:, lanes] = within


def packed_message(message_out, total, side):
    state_width, channels = total.shape
    message_out[:state_width, :] = total.astype(BF16)
    high, low = halves(side[:1])
    at = iota((EDGE, channels), 0)
    rows = jnp.where(at == 0, high.astype(F32), jnp.where(at == 1, low.astype(F32), side))
    message_out[state_width:, :] = jnp.concatenate([rows, jnp.zeros_like(rows)], axis=0).astype(BF16)


def unpacked(message, state_width):
    other = message[:state_width, :].astype(F32)
    side = message[state_width:, :].astype(F32)[:EDGE]
    return other, side[0:1] + side[1:2], side


def convolved(joined, edge, raw, taps_of, taps):
    count, lanes = raw.shape
    margin = taps - 1
    joined[:EDGE, :lanes] = edge
    joined[EDGE : EDGE + count, :lanes] = raw
    starts = [EDGE - margin + k for k in range(taps)]
    return silu(sum(taps_of(k) * joined[s : s + count, :lanes] for k, s in enumerate(starts)))


def state_kernel(
    heads,
    place,
    x_raw,
    bc_raw,
    step_size,
    decay_log,
    conv_x,
    conv_bc,
    x_out,
    bc_out,
    cum_out,
    state_out,
    joined,
):
    tokens, channels = x_raw.shape
    state_width = bc_raw.shape[1] // 2
    taps = conv_x.shape[0]
    margin = taps - 1
    bc_taps = joined_taps(conv_bc)
    step_lanes = 2 * LANES
    raw = bc_raw[...].astype(F32)
    none = jnp.zeros((EDGE, step_lanes), F32)
    bc_conv = convolved(joined, none[:, :LANES], raw, lambda k: bc_taps[k : k + 1], taps)
    bc_out[...] = bc_conv.astype(BF16)
    cum_log = summed_logs(step_size[...], decay_log, block_mask(tokens, 1))
    cum_out[...] = cum_log
    spread = spreader(channels // heads, channels)
    to_end = jnp.exp(cum_log[tokens - 1 : tokens] - cum_log) * step_size[...]
    b_turned = bc_conv.T[:state_width]
    b_turned = jnp.where(iota(b_turned.shape, 1) >= margin, b_turned, 0.0).astype(BF16)
    for lane in range(0, channels, step_lanes):
        lanes = slice(lane, lane + step_lanes)
        raw = x_raw[:, lanes].astype(F32)
        x_conv = convolved(joined, none, raw, lambda k: conv_x[k : k + 1, lanes], taps).astype(BF16)
        x_out[:, lanes] = x_conv
        scale = widened(to_end, spread[:, lanes])
        weighted = (x_conv.astype(F32) * scale).astype(BF16)
        state_out[:, lanes] = dot(b_turned, weighted)


def fix_kernel(
    heads,
    place,
    halo,
    x_raw,
    bc_raw,
    step_size,
    cum_log,
    conv_x,
    conv_bc,
    partial,
    x_out,
    bc_out,
    message_out,
    state_out,
    joined,
):
    tokens, channels = x_raw.shape
    state_width = bc_raw.shape[1] // 2
    taps = conv_x.shape[0]
    margin = taps - 1
    last = 2 * EDGE
    edge = halo[...].astype(F32)[EDGE:]
    bc_taps = joined_taps(conv_bc)
    raw = bc_raw[:last, :].astype(F32)
    bc_conv = convolved(joined, edge[:, channels:], raw, lambda k: bc_taps[k : k + 1], taps)
    bc_out[...] = bc_conv.astype(BF16)
    raw = x_raw[:last, :].astype(F32)
    x_conv = convolved(joined, edge[:, :channels], raw, lambda k: conv_x[k : k + 1], taps)
    x_conv = x_conv.astype(BF16)
    x_out[...] = x_conv
    spread = spreader(channels // heads, channels)
    final = cum_log[tokens - 1 : tokens, :]
    to_end = jnp.exp(final - cum_log[:last, :]) * step_size[:last, :]
    both = jnp.concatenate([to_end, jnp.broadcast_to(jnp.exp(final), (last, LANES))], axis=0)
    both = widened(both, spread)
    weighted = (x_conv.astype(F32) * both[:last]).astype(BF16).astype(F32)
    fill = jnp.zeros((LANES - last, LANES), F32)
    b_turned = jnp.concatenate([bc_conv, fill], axis=0).T[:state_width]
    b_turned = jnp.where(iota(b_turned.shape, 1) < margin, b_turned, 0.0).astype(BF16)
    fill = jnp.zeros((LANES - last, channels), F32)
    weighted = jnp.concatenate([weighted, fill], axis=0).astype(BF16)
    total = partial[...] + dot(b_turned, weighted)
    bc_tail = bc_raw[tokens - last :, :].astype(F32)[last - margin :]
    bc_tail = jnp.concatenate([bc_tail, jnp.zeros((margin, channels - LANES), F32)], axis=1)
    x_tail = x_raw[tokens - last :, :].astype(F32)[last - margin :]
    blank = jnp.zeros((EDGE - 1 - 2 * margin, channels), F32)
    side = jnp.concatenate([both[last : last + 1], blank, x_tail, bc_tail], axis=0)
    state_out[:state_width, :] = total
    state_out[state_width:, :] = side
    packed_message(message_out, total, side)


def mix_kernel(
    heads, place, x_head, bc_head, x_rest, bc_rest, step_size, cum_log, skip_gain, y_out, reach_out, bc_out, x_conv
):
    first = x_head.shape[0]
    x_conv[:first, :] = x_head[...]
    x_conv[first:, :] = x_rest[first:, :]
    bc_out[:first, :] = bc_head[...]
    bc_out[first:, :] = bc_rest[first:, :]
    cum_log = cum_log[...]
    reach_out[...] = jnp.exp(cum_log)
    mixed_rows(1, heads, x_conv, bc_out[...].astype(F32), step_size[...], cum_log, skip_gain, y_out)


def step_kernel(first, place, message, state, came, message_out, state_out, came_out):
    later = place[0] > 0
    state_width = state.shape[0] - EDGE
    channels = state.shape[1]
    other, other_decay, other_side = unpacked(message, state_width)
    mine, my_side = state[:state_width, :], state[state_width:, :]
    my_decay = my_side[:1]
    if first:
        before, passed = jnp.zeros_like(mine), jnp.ones_like(my_decay)
    else:
        before, passed = came[:state_width, :], came[state_width : state_width + 1, :]
    came_out[:state_width, :] = jnp.where(later, passed * other + before, before)
    passed = jnp.where(later, passed * other_decay, passed)
    came_out[state_width:, :] = jnp.broadcast_to(passed, (EDGE, channels))
    total = jnp.where(later, my_decay * other + mine, other_decay * mine + other)
    state_out[:state_width, :] = total
    side = jnp.where(later, my_side, other_side)
    side = jnp.where(iota((EDGE, channels), 0) == 0, my_decay * other_decay, side)
    state_out[state_width:, :] = side
    packed_message(message_out, total, side)


def finished(heads, me, incoming, y, bc, reach, gain, weight, outs, full, mixed):
    tokens, channels = y.shape
    part = weight.shape[1] // PARTS
    high, low = halves(incoming)
    blank = jnp.zeros_like(high)
    table = jnp.concatenate([blank, high, blank, low], axis=0)
    twice = jnp.concatenate([bc, bc], axis=1)
    spread = spreader(channels // heads, channels)
    step_lanes = 2 * LANES
    square = jnp.zeros((tokens, 1), F32)
    for lane in range(0, channels, step_lanes):
        lanes = slice(lane, lane + step_lanes)
        total = y[:, lanes] + dot(twice, table[:, lanes]) * widened(reach, spread[:, lanes])
        full[:, lanes] = total
        square = square + jnp.sum(total * total, axis=1, keepdims=True)
    factor = lax.rsqrt(square / channels + EPS)
    mixed[...] = (full[...] * factor * gain[...]).astype(BF16)
    for r, out in zip((3, 1, 2, 0), outs):
        columns = pl.ds(pl.multiple_of((me ^ r) * part, part), part)
        out[...] = dot(mixed[...], weight[:, columns]).astype(out.dtype)


def prompt_back_kernel(
    heads, place, message, came, y, bc, reach, gain, weight, sent3, sent1, kept2, kept0, full, mixed
):
    me, later = place[0], place[1] > 0
    state_width = came.shape[0] - EDGE
    other, _, _ = unpacked(message, state_width)
    before, passed = came[:state_width, :], came[state_width : state_width + 1, :]
    incoming = jnp.where(later, passed * other + before, before)
    outs = (sent3, sent1, kept2, kept0)
    finished(heads, me, incoming, y, bc[...], reach[...], gain, weight, outs, full, mixed)


def decode_back_kernel(
    rows,
    heads,
    place,
    message,
    state,
    x_raw,
    bc_raw,
    step_size,
    decay_log,
    conv_x,
    conv_bc,
    skip_gain,
    gain,
    weight,
    sent3,
    sent1,
    kept2,
    kept0,
    full,
    mixed,
    joined,
    x_conv,
    y,
):
    me, later = place[0], place[1] > 0
    state_width = state.shape[0] - EDGE
    tokens, channels = x_raw.shape
    taps = conv_x.shape[0]
    margin = taps - 1
    other, other_decay, other_side = unpacked(message, state_width)
    mine, my_side = state[:state_width, :], state[state_width:, :]
    incoming = jnp.where(later, my_side[:1] * other + mine, other_decay * mine + other)
    side = jnp.where(later, my_side, other_side)
    x_tail = side[EDGE - 2 * margin : EDGE - margin]
    bc_tail = side[EDGE - margin :, :LANES]

    def convolved(raw, tail, taps_of):
        lanes = raw.shape[1]
        for m in range(margin):
            joined[m * rows : (m + 1) * rows, :lanes] = jnp.broadcast_to(
                tail[m : m + 1], (rows, lanes)
            )
        joined[margin * rows :, :lanes] = raw
        return silu(
            sum(taps_of(k) * joined[k * rows : k * rows + tokens, :lanes] for k in range(taps))
        )

    bc_taps = joined_taps(conv_bc)
    bc_conv = convolved(bc_raw[...].astype(F32), bc_tail, lambda k: bc_taps[k : k + 1])
    step_lanes = 2 * LANES
    for lane in range(0, channels, step_lanes):
        lanes = slice(lane, lane + step_lanes)
        x_conv[:, lanes] = convolved(
            x_raw[:, lanes].astype(F32), x_tail[:, lanes], lambda k: conv_x[k : k + 1, lanes]
        ).astype(BF16)
    cum_log = summed_logs(step_size[...], decay_log, block_mask(tokens, rows))
    mixed_rows(rows, heads, x_conv, bc_conv, step_size[...], cum_log, skip_gain, y)
    bc = bc_conv.astype(BF16)
    outs = (sent3, sent1, kept2, kept0)
    finished(heads, me, incoming, y, bc, jnp.exp(cum_log), gain, weight, outs, full, mixed)


def far_kernel(place, kept, got, out):
    out[...] = (kept[...] + got[...].astype(F32)).astype(BF16)


def total_kernel(rows, place, kept, got, far, dec_kept, dec_got, dec_far, out, dec_out):
    out[...] = (kept[...] + got[...].astype(F32) + far[...].astype(F32)).astype(BF16)
    total = dec_kept[...] + dec_got[...].astype(F32) + dec_far[...].astype(F32)
    asked = total.shape[0]
    steps = asked // rows
    at = iota((asked, asked), 0)
    order = (at % steps) * rows + at // steps == iota((asked, asked), 1)
    total = dot(jnp.where(order, 1.0, 0.0).astype(BF16), total.astype(BF16))
    for r in range(rows):
        dec_out[r] = total[r * steps : (r + 1) * steps].astype(BF16)


def note_kernel(place, ids, note):
    steps = ids.shape[0]
    ids = ids[...]
    digits = [padded(d.astype(F32)) for d in (ids & 255, (ids >> 8) & 255, ids >> 16)]
    top = jnp.concatenate(digits, axis=1)
    note[...] = jnp.concatenate([top, jnp.zeros((EDGE - steps, 3 * LANES), F32)], axis=0).astype(BF16)


def join_kernel(place, mine, got, out):
    out[...] = jnp.concatenate([mine[...].astype(F32), got[...].astype(F32)], axis=0).astype(BF16)


def started(pairs, sems):
    copies = [
        pltpu.make_async_copy(source, target, sems.at[at])
        for at, (source, target) in enumerate(pairs)
    ]
    for copy in copies:
        copy.start()
    return copies


def lookup_kernel(
    steps, rows, place, notes, got, ahead, table_in, kept_out, sent_out, wanted, found, table, sems
):
    chunks, chunk, _ = table.shape
    copies = started(
        [(table_in.at[pl.ds(c * chunk, chunk), :], table.at[c]) for c in range(chunks)], sems
    )
    first = (place[0] * (chunks * chunk)).astype(F32)
    held = jnp.concatenate([notes[...].astype(F32), got[...].astype(F32)], axis=0)
    groups = held.shape[0] // EDGE
    digits = held[:, :LANES] + held[:, LANES : 2 * LANES] * 256.0 + held[:, 2 * LANES : 3 * LANES] * 65536.0
    same = iota((rows, LANES), 0) == iota((rows, LANES), 1)
    for q in range(groups):
        for s in range(steps):
            line = jnp.broadcast_to(digits[q * EDGE + s : q * EDGE + s + 1], (rows, LANES))
            column = jnp.sum(jnp.where(same, line, 0.0), axis=1, keepdims=True) - first
            at = (q * steps + s) * rows
            wanted[at : at + rows, :] = jnp.broadcast_to(column, (rows, LANES))
    asked = groups * steps * rows
    block = min(asked, 256)
    lane = iota((block, LANES), 1).astype(F32)
    for c in range(chunks):
        copies[c].wait()
        for at in range(0, asked, block):
            gap = wanted[at : at + block, :] - lane
            hot = [
                jnp.where(gap == float(c * chunk + k), 1.0, 0.0).astype(BF16)
                for k in range(0, chunk, LANES)
            ]
            term = dot(jnp.concatenate(hot, axis=1), table[c])
            if c == 0:
                found[at : at + block, :] = term
            else:
                found[at : at + block, :] += term
    kept_out[...] = found[: asked // 2, :].astype(BF16)
    sent_out[...] = found[asked // 2 :, :].astype(BF16)


def fold_kernel(place, kept, got, kept_out, sent_out):
    total = (kept[...].astype(F32) + got[...].astype(F32)).astype(BF16)
    half = kept_out.shape[0]
    kept_out[...] = total[:half]
    sent_out[...] = total[half:]


def last_fold_kernel(place, kept, got, out):
    out[...] = (kept[...].astype(F32) + got[...].astype(F32)).astype(BF16)


VMEM = pl.BlockSpec(memory_space=pltpu.VMEM)
SMEM = pl.BlockSpec(memory_space=pltpu.SMEM)
HBM = pl.BlockSpec(memory_space=pltpu.HBM)


class Caller:
    def __init__(self):
        self.token = jnp.zeros((8, LANES), F32)

    def __call__(self, kernel, place, inputs, outs, scratch=(), us=1.0, limit=4, far=()):
        inputs = list(inputs)
        count = len(inputs)

        def ordered(place, token, *refs):
            refs, token_out = list(refs), refs[count]
            del refs[count]
            kernel(place, *refs)
            token_out[...] = jnp.zeros_like(token_out)

        results = pl.pallas_call(
            ordered,
            out_shape=[shaped((8, LANES), F32)] + outs,
            in_specs=[SMEM, VMEM] + [HBM if at in far else VMEM for at in range(count)],
            out_specs=[VMEM] * (1 + len(outs)),
            scratch_shapes=list(scratch),
            compiler_params=pltpu.CompilerParams(vmem_limit_bytes=limit * MEBI),
            cost_estimate=pl.CostEstimate(
                flops=int(us * 1e9), bytes_accessed=int(us * 1e6), transcendentals=0
            ),
        )(place, self.token, *inputs)
        self.token = results[0]
        return results[1:]


def shaped(shape, dtype):
    return jax.ShapeDtypeStruct(shape, dtype)


def on_device(
    prompt_embeds,
    decode_ids,
    embed_table,
    norm_gain,
    x_weight,
    bc_weight,
    dt_weight,
    dt_bias,
    decay_log,
    conv_x,
    conv_bc,
    skip_gain,
    out_gain,
    out_weight,
):
    heads = dt_weight.shape[1]
    assert bc_weight.shape[1] == 1 and lax.axis_size("tp") == PARTS
    channels = x_weight.shape[1]
    taps = conv_x.shape[0]
    margin = taps - 1
    turned_bc = bc_weight.transpose(1, 2, 3, 0).reshape(-1, bc_weight.shape[0])
    turned_dt = dt_weight.T
    state_width = turned_bc.shape[0] // 2
    assert turned_bc.shape[0] == LANES
    tokens, part = prompt_embeds.shape
    rows, steps = decode_ids.shape
    assert steps <= EDGE and rows <= LANES and 2 * margin < EDGE
    asked = rows * steps
    groups = lax.axis_size("ctx")
    me_c = lax.axis_index("ctx").astype(jnp.int32)
    me_t = lax.axis_index("tp").astype(jnp.int32)
    vocab_here = embed_table.shape[0]
    bits = bits_of("ctx")
    assert len(bits) >= 2
    none = jnp.zeros((1,), jnp.int32)
    called = Caller()

    e2 = swapped(prompt_embeds, "tp", 2)
    e1 = swapped(prompt_embeds, "tp", 1)

    e3 = swapped(e2, "tp", 1)

    (notes,) = called(
        note_kernel, none, [decode_ids.T], [shaped((EDGE, 3 * LANES), BF16)], us=2
    )
    halving = [bits[1], bits[0]] + bits[2:]
    for bit in reversed(halving):
        got = swapped(notes, "ctx", bit)
        if bit != halving[0]:
            size = 2 * notes.shape[0]
            (notes,) = called(
                join_kernel, none, [notes, got], [shaped((size, notes.shape[1]), BF16)]
            )

    half = groups * asked // 2
    chunk = max(LANES, vocab_here // 8)
    assert vocab_here % chunk == 0
    kept, sent = called(
        functools.partial(lookup_kernel, steps, rows),
        me_c.reshape(1),
        [notes, got, e2, embed_table],
        [shaped((half, part), BF16), shaped((half, part), BF16)],
        [
            pltpu.VMEM((2 * half, LANES), F32),
            pltpu.VMEM((2 * half, part), F32),
            pltpu.VMEM((vocab_here // chunk, chunk, part), BF16),
            pltpu.SemaphoreType.DMA((vocab_here // chunk,)),
        ],
        us=3.5,
        limit=50,
        far=(3,),
    )

    project_weights = [
        norm_gain.reshape(PARTS, 1, part),
        x_weight,
        turned_bc,
        turned_dt,
        dt_bias.reshape(1, -1),
    ]
    conv_weights = [decay_log.reshape(1, -1), conv_x, conv_bc.reshape(taps, 2, -1)]
    skip_row, gain_row = skip_gain.reshape(1, -1), out_gain.reshape(1, -1)
    packed = state_width + 2 * EDGE

    def project(prompt, blocks, us):
        count = blocks[0].shape[0]
        outs = [
            shaped((count, channels), BF16),
            shaped((count, LANES), BF16),
            shaped((count, LANES), F32),
        ]
        if prompt:
            outs.append(shaped((2 * EDGE, channels + LANES), BF16))
            outs.append(shaped(x_weight.shape, BF16))
        return called(
            functools.partial(project_kernel, prompt),
            me_t.reshape(1),
            blocks + project_weights,
            outs,
            [pltpu.VMEM((PARTS, count, part), BF16)],
            us=us,
            limit=12,
        )

    x_raw, bc_raw, step_size, halo, project_weights[1] = project(True, [prompt_embeds, e1, e2, e3], 3)
    halo = lax.ppermute(halo, "ctx", [(c, c + 1) for c in range(groups - 1)])

    x_rest, bc_rest, cum_log, partial = called(
        functools.partial(state_kernel, heads),
        none,
        [x_raw, bc_raw, step_size] + conv_weights,
        [
            shaped((tokens, channels), BF16),
            shaped((tokens, LANES), BF16),
            shaped((tokens, LANES), F32),
            shaped((state_width, channels), F32),
        ],
        [pltpu.VMEM((EDGE + tokens, 2 * LANES), F32)],
        us=2,
        limit=8,
    )
    x_head, bc_head, message, state = called(
        functools.partial(fix_kernel, heads),
        none,
        [halo, x_raw, bc_raw, step_size, cum_log] + conv_weights[1:] + [partial],
        [
            shaped((2 * EDGE, channels), BF16),
            shaped((2 * EDGE, LANES), BF16),
            shaped((packed, channels), BF16),
            shaped((state_width + EDGE, channels), F32),
        ],
        [pltpu.VMEM((3 * EDGE, channels), F32)],
        limit=8,
    )
    came = state
    def folded(kept, got):
        half = kept.shape[0] // 2
        return called(
            fold_kernel,
            none,
            [kept, got],
            [shaped((half, part), BF16), shaped((half, part), BF16)],
            limit=16 if half > 512 else 4,
        )

    y, reach, bc = called(
        functools.partial(mix_kernel, heads),
        none,
        [x_head, bc_head, x_rest, bc_rest, step_size, cum_log, skip_row],
        [
            shaped((tokens, channels), F32),
            shaped((tokens, LANES), F32),
            shaped((tokens, LANES), BF16),
        ],
        [pltpu.VMEM((tokens, channels), BF16)],
        us=2.5,
        limit=8,
    )

    for bit, halved in zip(bits, halving):
        embeds = swapped(sent, "ctx", halved)
        if halved == halving[-1]:
            (kept,) = called(last_fold_kernel, none, [kept, embeds], [shaped((asked, part), BF16)])
        else:
            kept, sent = folded(kept, embeds)
        got = swapped(message, "ctx", bit)
        later = ((me_c & bit) != 0).astype(jnp.int32)
        if bit != bits[-1]:
            message, state, came = called(
                functools.partial(step_kernel, bit == bits[0]),
                later.reshape(1),
                [got, state, came],
                [
                    shaped((packed, channels), BF16),
                    shaped((state_width + EDGE, channels), F32),
                    shaped((state_width + EDGE, channels), F32),
                ],
            )
    back_place = jnp.stack([me_t, later])
    near = swapped(kept, "tp", 2)
    over1 = swapped(kept, "tp", 1)
    over3 = swapped(near, "tp", 1)

    def back(kernel, count, inputs, scratch, us):
        return called(
            kernel,
            back_place,
            [got] + inputs + [gain_row, out_weight],
            [shaped((count, part), BF16)] * 2 + [shaped((count, part), F32)] * 2,
            [pltpu.VMEM((count, channels), F32), pltpu.VMEM((count, channels), BF16)] + scratch,
            us=us,
            limit=12,
        )

    def crossed(sent3, sent1, kept2, kept0):
        got3 = swapped(sent3, "tp", 1)
        got1 = swapped(sent1, "tp", 1)
        (far,) = called(far_kernel, none, [kept2, got3], [shaped(kept2.shape, BF16)])
        return kept0, got1, swapped(far, "tp", 2)

    prompt_back = back(
        functools.partial(prompt_back_kernel, heads), tokens, [came, y, bc, reach], [], 2
    )
    dec_x_raw, dec_bc_raw, dec_step = project(False, [kept, over1, near, over3], 1.5)
    prompt_crossed = crossed(*prompt_back)
    decode_back = back(
        functools.partial(decode_back_kernel, rows, heads),
        asked,
        [state, dec_x_raw, dec_bc_raw, dec_step] + conv_weights + [skip_row],
        [
            pltpu.VMEM((margin * rows + asked, 2 * LANES), F32),
            pltpu.VMEM((asked, channels), BF16),
            pltpu.VMEM((asked, channels), F32),
        ],
        2.5,
    )
    decode_crossed = crossed(*decode_back)
    prompt_out, decode_out = called(
        functools.partial(total_kernel, rows),
        none,
        [*prompt_crossed, *decode_crossed],
        [shaped((tokens, part), BF16), shaped((rows, steps, part), BF16)],
    )
    return (prompt_out, decode_out)


def solution(mesh):
    return jax.shard_map(
        on_device,
        mesh=mesh,
        in_specs=(
            P("ctx", "tp"),
            P("ctx", None),
            P("ctx", "tp"),
            P(),
            P(None, "tp"),
            P(None, "tp", None, None),
            P(None, "tp"),
            P("tp"),
            P("tp"),
            P(None, "tp"),
            P(None, "tp", None, None),
            P("tp"),
            P("tp"),
            P("tp", None),
        ),
        out_specs=(P("ctx", "tp"), P("ctx", None, "tp")),
        check_vma=False,
    )
```

```python
import functools

import jax
import jax.numpy as jnp
from jax import lax
from jax.experimental import pallas as pl
from jax.experimental.pallas import tpu as pltpu
from jax.sharding import PartitionSpec as P

EPS = 1e-05
BF16 = jnp.bfloat16
F32 = jnp.float32
LANES = 128
PARTS = 4
EDGE = 8
MEBI = 1024 * 1024


def swapped(value, axis, bit):
    count = lax.axis_size(axis)
    return lax.ppermute(value, axis, [(i, i ^ bit) for i in range(count)])


def bits_of(axis):
    count = lax.axis_size(axis)
    assert count & (count - 1) == 0
    return [1 << k for k in range(count.bit_length() - 1)]


def dot(a, b):
    return jnp.dot(a, b, preferred_element_type=F32)


def across(a, b, axis):
    return lax.dot_general(a, b, (((axis,), (axis,)), ((), ())), preferred_element_type=F32)


def halves(value):
    high = value.astype(BF16)
    low = (value - high.astype(F32)).astype(BF16)
    return high, low


def iota(shape, axis):
    return lax.broadcasted_iota(jnp.int32, shape, axis)


def spreader(width, channels):
    head = iota((2 * LANES, channels), 0) & (LANES - 1)
    return jnp.where(head == iota((2 * LANES, channels), 1) // width, 1.0, 0.0).astype(BF16)


def widened(per_head, spread):
    high, low = halves(per_head)
    return dot(jnp.concatenate([high, low], axis=1), spread)


def padded(row):
    return jnp.concatenate([row, jnp.zeros((row.shape[0], LANES - row.shape[1]), F32)], axis=1)


def silu(value):
    return value / (1.0 + jnp.exp(-value))


def started(pairs, sems):
    copies = [
        pltpu.make_async_copy(source, target, sems.at[at])
        for at, (source, target) in enumerate(pairs)
    ]
    for copy in copies:
        copy.start()
    return copies


def project_kernel(
    prompt,
    place,
    own,
    over1,
    over2,
    over3,
    gain,
    x_weight,
    bc_weight,
    dt_weight,
    dt_bias,
    x_out,
    bc_out,
    step_out,
    *rest,
):
    if prompt:
        halo_out, normed, chunks, total, sems = rest
        copies = started(
            [(x_weight.at[pl.ds(j * chunks.shape[1], chunks.shape[1]), :], chunks.at[j]) for j in range(PARTS)],
            sems,
        )
    else:
        (normed,) = rest
    me = place[0]
    tokens, part = own.shape
    channels, heads = x_weight.shape[1], dt_weight.shape[0]
    blocks = [ref[...].astype(F32) for ref in (own, over1, over2, over3)]
    square = sum(jnp.sum(b * b, axis=1, keepdims=True) for b in blocks)
    factor = lax.rsqrt(square / (PARTS * part) + EPS)
    for r in range(PARTS):
        normed[me ^ r] = (blocks[r] * factor * gain[me ^ r]).astype(BF16)
    fill = jnp.zeros((LANES - heads, PARTS * part), BF16)
    side = jnp.concatenate([bc_weight[...], dt_weight[...], fill], axis=0)
    raw = sum(across(normed[j], side[:, j * part : (j + 1) * part], 1) for j in range(PARTS))
    bc_out[...] = raw[:, :LANES].astype(BF16)
    pre = raw[:, LANES:] + padded(dt_bias[...])
    step_out[...] = jnp.maximum(pre, 0.0) + jnp.log1p(jnp.exp(-jnp.abs(pre)))
    last = 2 * EDGE
    step_lanes = 2 * LANES
    if not prompt:
        for lane in range(0, channels, step_lanes):
            lanes = slice(lane, lane + step_lanes)
            terms = [dot(normed[j], x_weight[j * part : (j + 1) * part, lanes]) for j in range(PARTS)]
            x_out[:, lanes] = sum(terms).astype(BF16)
        return
    halo_out[:, channels:] = raw[tokens - last :, :LANES].astype(BF16)
    for j in range(PARTS):
        copies[j].wait()
        for lane in range(0, channels, step_lanes):
            lanes = slice(lane, lane + step_lanes)
            term = dot(normed[j], chunks[j, :, lanes])
            if j > 0:
                term = total[:, lanes] + term
            if j < PARTS - 1:
                total[:, lanes] = term
            else:
                x_out[:, lanes] = term.astype(BF16)
                halo_out[:, lanes] = term[tokens - last :].astype(BF16)


def summed_logs(step_size, decay_log, mask):
    logs = step_size * -jnp.exp(padded(decay_log[...]))
    high, low = halves(logs)
    lowest = (logs - high.astype(F32) - low.astype(F32)).astype(BF16)
    sums = dot(
        jnp.where(mask, 1.0, 0.0).astype(BF16), jnp.concatenate([high, low, lowest], axis=1)
    )
    return sums[:, :LANES] + sums[:, LANES : 2 * LANES] + sums[:, 2 * LANES :]


def joined_taps(conv_bc):
    return jnp.concatenate([conv_bc[:, 0, :], conv_bc[:, 1, :]], axis=1)


def block_mask(tokens, rows):
    t_at = iota((tokens, tokens), 0)
    s_at = iota((tokens, tokens), 1)
    mask = t_at >= s_at
    return mask if rows == 1 else jnp.logical_and(mask, t_at % rows == s_at % rows)


def mixed_rows(rows, heads, x_conv, bc_conv, step_size, cum_log, skip_gain, y_out):
    tokens, channels = x_conv.shape
    width = channels // heads
    state_width = bc_conv.shape[1] // 2
    mask = block_mask(tokens, rows)
    b_rows = bc_conv[:, :state_width].astype(BF16)
    c_rows = bc_conv[:, state_width:].astype(BF16)
    cum_across = cum_log.T
    step_across = step_size.T
    scores = across(c_rows, b_rows, 1)
    spread = spreader(width, channels)
    skip_row = widened(jnp.broadcast_to(padded(skip_gain[...]), (EDGE, LANES)), spread)[:1]
    per_tile = LANES // width
    lane_head = iota((tokens, LANES), 1) // width
    for tile in range(channels // LANES):
        lanes = slice(tile * LANES, (tile + 1) * LANES)
        x_tile = x_conv[:, lanes].astype(F32)
        within = skip_row[:, lanes] * x_tile
        for k in range(per_tile):
            h = tile * per_tile + k
            gaps = cum_log[:, h : h + 1] - cum_across[h : h + 1, :]
            decays = jnp.exp(jnp.where(mask, gaps, -1e30))
            mixing = (scores * decays * step_across[h : h + 1, :]).astype(BF16)
            within += dot(mixing, jnp.where(lane_head == k, x_tile, 0.0).astype(BF16))
        y_out[:, lanes] = within


def packed_message(message_out, total, side):
    high, low = halves(side[:1])
    at = iota(side.shape, 0)
    rows = jnp.where(at == 0, high.astype(F32), jnp.where(at == 1, low.astype(F32), side))
    message_out[...] = jnp.concatenate([total, rows], axis=0).astype(BF16)


def unpacked(message, state_width):
    whole = message[...].astype(F32)
    side = whole[state_width:]
    return whole[:state_width], side[0:1] + side[1:2], side


def convolved(joined, edge, raw, taps_of, taps):
    count, lanes = raw.shape
    margin = taps - 1
    joined[:EDGE, :lanes] = edge
    joined[EDGE : EDGE + count, :lanes] = raw
    starts = [EDGE - margin + k for k in range(taps)]
    return silu(sum(taps_of(k) * joined[s : s + count, :lanes] for k, s in enumerate(starts)))


def state_kernel(
    heads,
    place,
    x_raw,
    bc_raw,
    step_size,
    decay_log,
    conv_x,
    conv_bc,
    x_out,
    bc_out,
    cum_out,
    state_out,
    joined,
):
    tokens, channels = x_raw.shape
    state_width = bc_raw.shape[1] // 2
    taps = conv_x.shape[0]
    margin = taps - 1
    bc_taps = joined_taps(conv_bc)
    step_lanes = 2 * LANES
    raw = bc_raw[...].astype(F32)
    none = jnp.zeros((EDGE, step_lanes), F32)
    bc_conv = convolved(joined, none[:, :LANES], raw, lambda k: bc_taps[k : k + 1], taps)
    bc_out[...] = bc_conv.astype(BF16)
    cum_log = summed_logs(step_size[...], decay_log, block_mask(tokens, 1))
    cum_out[...] = cum_log
    spread = spreader(channels // heads, channels)
    to_end = jnp.exp(cum_log[tokens - 1 : tokens] - cum_log) * step_size[...]
    b_turned = bc_conv.T[:state_width]
    b_turned = jnp.where(iota(b_turned.shape, 1) >= margin, b_turned, 0.0).astype(BF16)
    for lane in range(0, channels, step_lanes):
        lanes = slice(lane, lane + step_lanes)
        raw = x_raw[:, lanes].astype(F32)
        x_conv = convolved(joined, none, raw, lambda k: conv_x[k : k + 1, lanes], taps).astype(BF16)
        x_out[:, lanes] = x_conv
        scale = widened(to_end, spread[:, lanes])
        weighted = (x_conv.astype(F32) * scale).astype(BF16)
        state_out[:, lanes] = dot(b_turned, weighted)


def fix_kernel(
    heads,
    place,
    halo,
    x_raw,
    bc_raw,
    step_size,
    cum_log,
    conv_x,
    conv_bc,
    partial,
    x_out,
    bc_out,
    message_out,
    state_out,
    joined,
):
    tokens, channels = x_raw.shape
    state_width = bc_raw.shape[1] // 2
    taps = conv_x.shape[0]
    margin = taps - 1
    last = 2 * EDGE
    edge = halo[...].astype(F32)[EDGE:]
    bc_taps = joined_taps(conv_bc)
    raw = bc_raw[:last, :].astype(F32)
    bc_conv = convolved(joined, edge[:, channels:], raw, lambda k: bc_taps[k : k + 1], taps)
    bc_out[...] = bc_conv.astype(BF16)
    raw = x_raw[:last, :].astype(F32)
    x_conv = convolved(joined, edge[:, :channels], raw, lambda k: conv_x[k : k + 1], taps)
    x_conv = x_conv.astype(BF16)
    x_out[...] = x_conv
    spread = spreader(channels // heads, channels)
    final = cum_log[tokens - 1 : tokens, :]
    to_end = jnp.exp(final - cum_log[:last, :]) * step_size[:last, :]
    both = jnp.concatenate([to_end, jnp.broadcast_to(jnp.exp(final), (last, LANES))], axis=0)
    both = widened(both, spread)
    weighted = (x_conv.astype(F32) * both[:last]).astype(BF16).astype(F32)
    fill = jnp.zeros((LANES - last, LANES), F32)
    b_turned = jnp.concatenate([bc_conv, fill], axis=0).T[:state_width]
    b_turned = jnp.where(iota(b_turned.shape, 1) < margin, b_turned, 0.0).astype(BF16)
    fill = jnp.zeros((LANES - last, channels), F32)
    weighted = jnp.concatenate([weighted, fill], axis=0).astype(BF16)
    total = partial[...] + dot(b_turned, weighted)
    bc_tail = bc_raw[tokens - last :, :].astype(F32)[last - margin :]
    bc_tail = jnp.concatenate([bc_tail, jnp.zeros((margin, channels - LANES), F32)], axis=1)
    x_tail = x_raw[tokens - last :, :].astype(F32)[last - margin :]
    blank = jnp.zeros((EDGE - 1 - 2 * margin, channels), F32)
    side = jnp.concatenate([both[last : last + 1], blank, x_tail, bc_tail], axis=0)
    state_out[:state_width, :] = total
    state_out[state_width:, :] = side
    packed_message(message_out, total, side)


def mix_kernel(
    heads, place, x_head, bc_head, x_rest, bc_rest, step_size, cum_log, skip_gain, y_out, reach_out, bc_out, x_conv
):
    first = x_head.shape[0]
    x_conv[:first, :] = x_head[...]
    x_conv[first:, :] = x_rest[first:, :]
    bc_out[:first, :] = bc_head[...]
    bc_out[first:, :] = bc_rest[first:, :]
    cum_log = cum_log[...]
    reach_out[...] = jnp.exp(cum_log)
    mixed_rows(1, heads, x_conv, bc_out[...].astype(F32), step_size[...], cum_log, skip_gain, y_out)


def step_kernel(first, place, message, state, came, message_out, state_out, came_out):
    later = place[0] > 0
    state_width = state.shape[0] - EDGE
    channels = state.shape[1]
    other, other_decay, other_side = unpacked(message, state_width)
    mine, my_side = state[:state_width, :], state[state_width:, :]
    my_decay = my_side[:1]
    if first:
        before, passed = jnp.zeros_like(mine), jnp.ones_like(my_decay)
    else:
        before, passed = came[:state_width, :], came[state_width : state_width + 1, :]
    came_out[:state_width, :] = jnp.where(later, passed * other + before, before)
    passed = jnp.where(later, passed * other_decay, passed)
    came_out[state_width:, :] = jnp.broadcast_to(passed, (EDGE, channels))
    total = jnp.where(later, my_decay * other + mine, other_decay * mine + other)
    state_out[:state_width, :] = total
    side = jnp.where(later, my_side, other_side)
    side = jnp.where(iota((EDGE, channels), 0) == 0, my_decay * other_decay, side)
    state_out[state_width:, :] = side
    packed_message(message_out, total, side)


def finished(heads, me, incoming, y, bc, reach, gain, weight, outs, full, mixed):
    tokens, channels = y.shape
    high, low = halves(incoming)
    blank = jnp.zeros_like(high)
    table = jnp.concatenate([blank, high, blank, low], axis=0)
    twice = jnp.concatenate([bc, bc], axis=1)
    spread = spreader(channels // heads, channels)
    step_lanes = 2 * LANES
    square = jnp.zeros((tokens, 1), F32)
    for lane in range(0, channels, step_lanes):
        lanes = slice(lane, lane + step_lanes)
        total = y[:, lanes] + dot(twice, table[:, lanes]) * widened(reach, spread[:, lanes])
        full[:, lanes] = total
        square = square + jnp.sum(total * total, axis=1, keepdims=True)
    factor = lax.rsqrt(square / channels + EPS)
    mixed[...] = (full[...] * factor * gain[...]).astype(BF16)
    sent(me, mixed, weight, zip((3, 1, 2, 0), outs))


def sent(me, mixed, weight, wanted):
    part = weight.shape[1] // PARTS
    for r, out in wanted:
        columns = pl.ds(pl.multiple_of((me ^ r) * part, part), part)
        out[...] = dot(mixed[...], weight[:, columns]).astype(out.dtype)


def rest_kernel(place, mixed, weight, sent1, kept2, kept0):
    sent(place[0], mixed, weight, ((1, sent1), (2, kept2), (0, kept0)))


def prompt_back_kernel(
    heads, place, message, came, y, bc, reach, gain, weight, sent3, mixed, full
):
    me, later = place[0], place[1] > 0
    state_width = came.shape[0] - EDGE
    other, _, _ = unpacked(message, state_width)
    before, passed = came[:state_width, :], came[state_width : state_width + 1, :]
    incoming = jnp.where(later, passed * other + before, before)
    finished(heads, me, incoming, y, bc[...], reach[...], gain, weight, (sent3,), full, mixed)


def decode_back_kernel(
    rows,
    heads,
    place,
    message,
    state,
    x_raw,
    bc_raw,
    step_size,
    decay_log,
    conv_x,
    conv_bc,
    skip_gain,
    gain,
    weight,
    sent3,
    sent1,
    kept2,
    kept0,
    full,
    mixed,
    joined,
    x_conv,
    y,
):
    me, later = place[0], place[1] > 0
    state_width = state.shape[0] - EDGE
    tokens, channels = x_raw.shape
    taps = conv_x.shape[0]
    margin = taps - 1
    other, other_decay, other_side = unpacked(message, state_width)
    mine, my_side = state[:state_width, :], state[state_width:, :]
    incoming = jnp.where(later, my_side[:1] * other + mine, other_decay * mine + other)
    side = jnp.where(later, my_side, other_side)
    x_tail = side[EDGE - 2 * margin : EDGE - margin]
    bc_tail = side[EDGE - margin :, :LANES]

    def convolved(raw, tail, taps_of):
        lanes = raw.shape[1]
        for m in range(margin):
            joined[m * rows : (m + 1) * rows, :lanes] = jnp.broadcast_to(
                tail[m : m + 1], (rows, lanes)
            )
        joined[margin * rows :, :lanes] = raw
        return silu(
            sum(taps_of(k) * joined[k * rows : k * rows + tokens, :lanes] for k in range(taps))
        )

    bc_taps = joined_taps(conv_bc)
    bc_conv = convolved(bc_raw[...].astype(F32), bc_tail, lambda k: bc_taps[k : k + 1])
    step_lanes = 2 * LANES
    for lane in range(0, channels, step_lanes):
        lanes = slice(lane, lane + step_lanes)
        x_conv[:, lanes] = convolved(
            x_raw[:, lanes].astype(F32), x_tail[:, lanes], lambda k: conv_x[k : k + 1, lanes]
        ).astype(BF16)
    cum_log = summed_logs(step_size[...], decay_log, block_mask(tokens, rows))
    mixed_rows(rows, heads, x_conv, bc_conv, step_size[...], cum_log, skip_gain, y)
    bc = bc_conv.astype(BF16)
    outs = (sent3, sent1, kept2, kept0)
    finished(heads, me, incoming, y, bc, jnp.exp(cum_log), gain, weight, outs, full, mixed)


def far_kernel(place, kept, got, out):
    out[...] = (kept[...] + got[...].astype(F32)).astype(BF16)


def total_kernel(rows, place, kept, got, far, dec_kept, dec_got, dec_far, out, dec_out):
    out[...] = (kept[...] + got[...].astype(F32) + far[...].astype(F32)).astype(BF16)
    total = dec_kept[...] + dec_got[...].astype(F32) + dec_far[...].astype(F32)
    asked = total.shape[0]
    steps = asked // rows
    at = iota((asked, asked), 0)
    order = (at % steps) * rows + at // steps == iota((asked, asked), 1)
    total = dot(jnp.where(order, 1.0, 0.0).astype(BF16), total.astype(BF16))
    for r in range(rows):
        dec_out[r] = total[r * steps : (r + 1) * steps].astype(BF16)


def note_kernel(place, ids, note):
    steps = ids.shape[0]
    ids = ids[...]
    digits = [padded(d.astype(F32)) for d in (ids & 255, (ids >> 8) & 255, ids >> 16)]
    top = jnp.concatenate(digits, axis=1)
    note[...] = jnp.concatenate([top, jnp.zeros((EDGE - steps, 3 * LANES), F32)], axis=0).astype(BF16)


def join_kernel(place, mine, got, out):
    out[...] = jnp.concatenate([mine[...].astype(F32), got[...].astype(F32)], axis=0).astype(BF16)


def hand_kernel(place, mine, got, given, ahead, out, handed):
    join_kernel(place, mine, got, out)


def lookup_kernel(steps, rows, place, notes, got, table, kept_out, sent_out, wanted, found):
    chunk = min(table.shape[0], 1024)
    chunks = table.shape[0] // chunk
    first = (place[0] * (chunks * chunk)).astype(F32)
    held = jnp.concatenate([notes[...].astype(F32), got[...].astype(F32)], axis=0)
    groups = held.shape[0] // EDGE
    digits = held[:, :LANES] + held[:, LANES : 2 * LANES] * 256.0 + held[:, 2 * LANES : 3 * LANES] * 65536.0
    same = iota((rows, LANES), 0) == iota((rows, LANES), 1)
    for q in range(groups):
        for s in range(steps):
            line = jnp.broadcast_to(digits[q * EDGE + s : q * EDGE + s + 1], (rows, LANES))
            column = jnp.sum(jnp.where(same, line, 0.0), axis=1, keepdims=True) - first
            at = (q * steps + s) * rows
            wanted[at : at + rows, :] = jnp.broadcast_to(column, (rows, LANES))
    asked = groups * steps * rows
    block = min(asked, 256)
    lane = iota((block, LANES), 1).astype(F32)
    for c in range(chunks):
        for at in range(0, asked, block):
            gap = wanted[at : at + block, :] - lane
            hot = [
                jnp.where(gap == float(c * chunk + k), 1.0, 0.0).astype(BF16)
                for k in range(0, chunk, LANES)
            ]
            term = dot(jnp.concatenate(hot, axis=1), table[c * chunk : (c + 1) * chunk, :])
            if c == 0:
                found[at : at + block, :] = term
            else:
                found[at : at + block, :] += term
    kept_out[...] = found[: asked // 2, :].astype(BF16)
    sent_out[...] = found[asked // 2 :, :].astype(BF16)


def fold_kernel(place, kept, got, kept_out, sent_out):
    total = (kept[...].astype(F32) + got[...].astype(F32)).astype(BF16)
    half = kept_out.shape[0]
    kept_out[...] = total[:half]
    sent_out[...] = total[half:]


def last_fold_kernel(place, kept, got, out):
    out[...] = (kept[...].astype(F32) + got[...].astype(F32)).astype(BF16)


VMEM = pl.BlockSpec(memory_space=pltpu.VMEM)
SMEM = pl.BlockSpec(memory_space=pltpu.SMEM)
HBM = pl.BlockSpec(memory_space=pltpu.HBM)


class Caller:
    def __init__(self):
        self.token = jnp.zeros((8, LANES), F32)

    def __call__(self, kernel, place, inputs, outs, scratch=(), us=1.0, limit=4, far=(), same=()):
        inputs = list(inputs)
        count = len(inputs)

        def ordered(place, token, *refs):
            refs, token_out = list(refs), refs[count]
            del refs[count]
            kernel(place, *refs)
            token_out[...] = jnp.zeros_like(token_out)

        results = pl.pallas_call(
            ordered,
            out_shape=[shaped((8, LANES), F32)] + outs,
            in_specs=[SMEM, VMEM] + [HBM if at in far else VMEM for at in range(count)],
            out_specs=[VMEM] * (1 + len(outs)),
            scratch_shapes=list(scratch),
            input_output_aliases={2 + at: 1 + out for at, out in same},
            compiler_params=pltpu.CompilerParams(vmem_limit_bytes=limit * MEBI),
            cost_estimate=pl.CostEstimate(
                flops=int(us * 1e9), bytes_accessed=int(us * 1e6), transcendentals=0
            ),
        )(place, self.token, *inputs)
        self.token = results[0]
        return results[1:]


def shaped(shape, dtype):
    return jax.ShapeDtypeStruct(shape, dtype)


def on_device(
    prompt_embeds,
    decode_ids,
    embed_table,
    norm_gain,
    x_weight,
    bc_weight,
    dt_weight,
    dt_bias,
    decay_log,
    conv_x,
    conv_bc,
    skip_gain,
    out_gain,
    out_weight,
):
    heads = dt_weight.shape[1]
    assert bc_weight.shape[1] == 1 and lax.axis_size("tp") == PARTS
    channels = x_weight.shape[1]
    taps = conv_x.shape[0]
    margin = taps - 1
    turned_bc = bc_weight.transpose(1, 2, 3, 0).reshape(-1, bc_weight.shape[0])
    turned_dt = dt_weight.T
    state_width = turned_bc.shape[0] // 2
    assert turned_bc.shape[0] == LANES
    tokens, part = prompt_embeds.shape
    rows, steps = decode_ids.shape
    assert steps <= EDGE and rows <= LANES and 2 * margin < EDGE
    asked = rows * steps
    groups = lax.axis_size("ctx")
    me_c = lax.axis_index("ctx").astype(jnp.int32)
    me_t = lax.axis_index("tp").astype(jnp.int32)
    vocab_here = embed_table.shape[0]
    bits = bits_of("ctx")
    assert len(bits) >= 2
    none = jnp.zeros((1,), jnp.int32)
    called = Caller()

    e2 = swapped(prompt_embeds, "tp", 2)
    e1 = swapped(prompt_embeds, "tp", 1)


    (notes,) = called(
        note_kernel, none, [decode_ids.T], [shaped((EDGE, 3 * LANES), BF16)], us=2
    )
    halving = [bits[1], bits[0]] + bits[2:]
    for bit in reversed(halving):
        got = swapped(notes, "ctx", bit)
        joined = shaped((2 * notes.shape[0], notes.shape[1]), BF16)
        if bit == halving[1]:
            notes, e2 = called(
                hand_kernel,
                none,
                [notes, got, e2, embed_table],
                [joined, shaped(e2.shape, BF16)],
                limit=50,
                far=(3,),
                same=((2, 1),),
            )
        elif bit != halving[0]:
            (notes,) = called(join_kernel, none, [notes, got], [joined])
    e3 = swapped(e2, "tp", 1)

    project_weights = [
        norm_gain.reshape(PARTS, 1, part),
        x_weight,
        turned_bc,
        turned_dt,
        dt_bias.reshape(1, -1),
    ]
    conv_weights = [decay_log.reshape(1, -1), conv_x, conv_bc.reshape(taps, 2, -1)]
    skip_row, gain_row = skip_gain.reshape(1, -1), out_gain.reshape(1, -1)
    packed = state_width + EDGE

    def project(prompt, blocks, us):
        count = blocks[0].shape[0]
        scratch = []
        outs = [
            shaped((count, channels), BF16),
            shaped((count, LANES), BF16),
            shaped((count, LANES), F32),
        ]
        if prompt:
            outs.append(shaped((2 * EDGE, channels + LANES), BF16))
            scratch = [
                pltpu.VMEM((PARTS, part, channels), BF16),
                pltpu.VMEM((count, channels), F32),
                pltpu.SemaphoreType.DMA((PARTS,)),
            ]
        return called(
            functools.partial(project_kernel, prompt),
            me_t.reshape(1),
            blocks + project_weights,
            outs,
            [pltpu.VMEM((PARTS, count, part), BF16)] + scratch,
            us=us,
            limit=50 if prompt else 12,
            far=(5,) if prompt else (),
        )

    x_raw, bc_raw, step_size, halo = project(True, [prompt_embeds, e1, e2, e3], 3)
    halo = lax.ppermute(halo, "ctx", [(c, c + 1) for c in range(groups - 1)])

    half = groups * asked // 2
    assert vocab_here % min(vocab_here, 1024) == 0
    kept, sent = called(
        functools.partial(lookup_kernel, steps, rows),
        me_c.reshape(1),
        [notes, got, embed_table],
        [shaped((half, part), BF16), shaped((half, part), BF16)],
        [pltpu.VMEM((2 * half, LANES), F32), pltpu.VMEM((2 * half, part), F32)],
        us=2.5,
        limit=32 if half > 512 else 8,
    )

    x_rest, bc_rest, cum_log, partial = called(
        functools.partial(state_kernel, heads),
        none,
        [x_raw, bc_raw, step_size] + conv_weights,
        [
            shaped((tokens, channels), BF16),
            shaped((tokens, LANES), BF16),
            shaped((tokens, LANES), F32),
            shaped((state_width, channels), F32),
        ],
        [pltpu.VMEM((EDGE + tokens, 2 * LANES), F32)],
        us=2,
        limit=8,
    )
    x_head, bc_head, message, state = called(
        functools.partial(fix_kernel, heads),
        none,
        [halo, x_raw, bc_raw, step_size, cum_log] + conv_weights[1:] + [partial],
        [
            shaped((2 * EDGE, channels), BF16),
            shaped((2 * EDGE, LANES), BF16),
            shaped((packed, channels), BF16),
            shaped((state_width + EDGE, channels), F32),
        ],
        [pltpu.VMEM((3 * EDGE, channels), F32)],
        limit=8,
    )
    came = state
    def folded(kept, got):
        half = kept.shape[0] // 2
        return called(
            fold_kernel,
            none,
            [kept, got],
            [shaped((half, part), BF16), shaped((half, part), BF16)],
            limit=16 if half > 512 else 4,
        )

    y, reach, bc = called(
        functools.partial(mix_kernel, heads),
        none,
        [x_head, bc_head, x_rest, bc_rest, step_size, cum_log, skip_row],
        [
            shaped((tokens, channels), F32),
            shaped((tokens, LANES), F32),
            shaped((tokens, LANES), BF16),
        ],
        [pltpu.VMEM((tokens, channels), BF16)],
        us=2.5,
        limit=8,
    )

    for bit, halved in zip(bits, halving):
        embeds = swapped(sent, "ctx", halved)
        if halved == halving[-1]:
            (kept,) = called(last_fold_kernel, none, [kept, embeds], [shaped((asked, part), BF16)])
        else:
            kept, sent = folded(kept, embeds)
        got = swapped(message, "ctx", bit)
        later = ((me_c & bit) != 0).astype(jnp.int32)
        if bit != bits[-1]:
            message, state, came = called(
                functools.partial(step_kernel, bit == bits[0]),
                later.reshape(1),
                [got, state, came],
                [
                    shaped((packed, channels), BF16),
                    shaped((state_width + EDGE, channels), F32),
                    shaped((state_width + EDGE, channels), F32),
                ],
            )
    back_place = jnp.stack([me_t, later])
    near = swapped(kept, "tp", 2)
    over1 = swapped(kept, "tp", 1)
    over3 = swapped(near, "tp", 1)

    def back(kernel, count, inputs, scratch, us):
        return called(
            kernel,
            back_place,
            [got] + inputs + [gain_row, out_weight],
            [shaped((count, part), BF16)] * 2 + [shaped((count, part), F32)] * 2,
            [pltpu.VMEM((count, channels), F32), pltpu.VMEM((count, channels), BF16)] + scratch,
            us=us,
            limit=12,
        )

    def crossed(sent3, sent1, kept2, kept0):
        got3 = swapped(sent3, "tp", 1)
        got1 = swapped(sent1, "tp", 1)
        (far,) = called(far_kernel, none, [kept2, got3], [shaped(kept2.shape, BF16)])
        return kept0, got1, swapped(far, "tp", 2)

    prompt_sent3, prompt_mixed = called(
        functools.partial(prompt_back_kernel, heads),
        back_place,
        [got, came, y, bc, reach, gain_row, out_weight],
        [shaped((tokens, part), BF16), shaped((tokens, channels), BF16)],
        [pltpu.VMEM((tokens, channels), F32)],
        us=1.5,
        limit=12,
    )
    prompt_rest = called(
        rest_kernel,
        back_place,
        [prompt_mixed, out_weight],
        [shaped((tokens, part), BF16)] + [shaped((tokens, part), F32)] * 2,
    )
    dec_x_raw, dec_bc_raw, dec_step = project(False, [kept, over1, near, over3], 1.5)
    prompt_crossed = crossed(prompt_sent3, *prompt_rest)
    decode_back = back(
        functools.partial(decode_back_kernel, rows, heads),
        asked,
        [state, dec_x_raw, dec_bc_raw, dec_step] + conv_weights + [skip_row],
        [
            pltpu.VMEM((margin * rows + asked, 2 * LANES), F32),
            pltpu.VMEM((asked, channels), BF16),
            pltpu.VMEM((asked, channels), F32),
        ],
        2.5,
    )
    decode_crossed = crossed(*decode_back)
    prompt_out, decode_out = called(
        functools.partial(total_kernel, rows),
        none,
        [*prompt_crossed, *decode_crossed],
        [shaped((tokens, part), BF16), shaped((rows, steps, part), BF16)],
    )
    return (prompt_out, decode_out)


def solution(mesh):
    return jax.shard_map(
        on_device,
        mesh=mesh,
        in_specs=(
            P("ctx", "tp"),
            P("ctx", None),
            P("ctx", "tp"),
            P(),
            P(None, "tp"),
            P(None, "tp", None, None),
            P(None, "tp"),
            P("tp"),
            P("tp"),
            P(None, "tp"),
            P(None, "tp", None, None),
            P("tp"),
            P("tp"),
            P("tp", None),
        ),
        out_specs=(P("ctx", "tp"), P("ctx", None, "tp")),
        check_vma=False,
    )
```

```python
import functools

import jax
import jax.numpy as jnp
from jax import lax
from jax.experimental import pallas as pl
from jax.experimental.pallas import tpu as pltpu
from jax.sharding import PartitionSpec as P

EPS = 1e-05
BF16 = jnp.bfloat16
F32 = jnp.float32
LANES = 128
PARTS = 4
EDGE = 8
MEBI = 1024 * 1024


def swapped(value, axis, bit):
    count = lax.axis_size(axis)
    return lax.ppermute(value, axis, [(i, i ^ bit) for i in range(count)])


def bits_of(axis):
    count = lax.axis_size(axis)
    assert count & (count - 1) == 0
    return [1 << k for k in range(count.bit_length() - 1)]


def dot(a, b):
    return jnp.dot(a, b, preferred_element_type=F32)


def across(a, b, axis):
    return lax.dot_general(a, b, (((axis,), (axis,)), ((), ())), preferred_element_type=F32)


def halves(value):
    high = value.astype(BF16)
    low = (value - high.astype(F32)).astype(BF16)
    return high, low


def iota(shape, axis):
    return lax.broadcasted_iota(jnp.int32, shape, axis)


def spreader(width, channels):
    head = iota((2 * LANES, channels), 0) & (LANES - 1)
    return jnp.where(head == iota((2 * LANES, channels), 1) // width, 1.0, 0.0).astype(BF16)


def widened(per_head, spread):
    high, low = halves(per_head)
    return dot(jnp.concatenate([high, low], axis=1), spread)


def padded(row):
    return jnp.concatenate([row, jnp.zeros((row.shape[0], LANES - row.shape[1]), F32)], axis=1)


def silu(value):
    return value / (1.0 + jnp.exp(-value))


def started(pairs, sems):
    copies = [
        pltpu.make_async_copy(source, target, sems.at[at])
        for at, (source, target) in enumerate(pairs)
    ]
    for copy in copies:
        copy.start()
    return copies


def project_kernel(
    prompt,
    place,
    own,
    over1,
    over2,
    over3,
    gain,
    x_weight,
    bc_weight,
    dt_weight,
    dt_bias,
    x_out,
    bc_out,
    step_out,
    *rest,
):
    if prompt:
        halo_out, normed, chunks, total, sems = rest
        copies = started(
            [(x_weight.at[pl.ds(j * chunks.shape[1], chunks.shape[1]), :], chunks.at[j]) for j in range(PARTS)],
            sems,
        )
    else:
        (normed,) = rest
    me = place[0]
    tokens, part = own.shape
    channels, heads = x_weight.shape[1], dt_weight.shape[0]
    blocks = [ref[...].astype(F32) for ref in (own, over1, over2, over3)]
    square = sum(jnp.sum(b * b, axis=1, keepdims=True) for b in blocks)
    factor = lax.rsqrt(square / (PARTS * part) + EPS)
    for r in range(PARTS):
        normed[me ^ r] = (blocks[r] * factor * gain[me ^ r]).astype(BF16)
    fill = jnp.zeros((LANES - heads, PARTS * part), BF16)
    side = jnp.concatenate([bc_weight[...], dt_weight[...], fill], axis=0)
    raw = sum(across(normed[j], side[:, j * part : (j + 1) * part], 1) for j in range(PARTS))
    bc_out[...] = raw[:, :LANES].astype(BF16)
    pre = raw[:, LANES:] + padded(dt_bias[...])
    step_out[...] = jnp.maximum(pre, 0.0) + jnp.log1p(jnp.exp(-jnp.abs(pre)))
    last = 2 * EDGE
    step_lanes = 2 * LANES
    if not prompt:
        for lane in range(0, channels, step_lanes):
            lanes = slice(lane, lane + step_lanes)
            terms = [dot(normed[j], x_weight[j * part : (j + 1) * part, lanes]) for j in range(PARTS)]
            x_out[:, lanes] = sum(terms).astype(BF16)
        return
    halo_out[:, channels:] = raw[tokens - last :, :LANES].astype(BF16)
    for j in range(PARTS):
        copies[j].wait()
        for lane in range(0, channels, step_lanes):
            lanes = slice(lane, lane + step_lanes)
            term = dot(normed[j], chunks[j, :, lanes])
            if j > 0:
                term = total[:, lanes] + term
            if j < PARTS - 1:
                total[:, lanes] = term
            else:
                x_out[:, lanes] = term.astype(BF16)
                halo_out[:, lanes] = term[tokens - last :].astype(BF16)


def summed_logs(step_size, decay_log, mask):
    logs = step_size * -jnp.exp(padded(decay_log[...]))
    high, low = halves(logs)
    lowest = (logs - high.astype(F32) - low.astype(F32)).astype(BF16)
    sums = dot(
        jnp.where(mask, 1.0, 0.0).astype(BF16), jnp.concatenate([high, low, lowest], axis=1)
    )
    return sums[:, :LANES] + sums[:, LANES : 2 * LANES] + sums[:, 2 * LANES :]


def joined_taps(conv_bc):
    return jnp.concatenate([conv_bc[:, 0, :], conv_bc[:, 1, :]], axis=1)


def block_mask(tokens, rows):
    t_at = iota((tokens, tokens), 0)
    s_at = iota((tokens, tokens), 1)
    mask = t_at >= s_at
    return mask if rows == 1 else jnp.logical_and(mask, t_at % rows == s_at % rows)


def mixed_rows(rows, heads, x_conv, bc_conv, step_size, cum_log, skip_gain, y_out):
    tokens, channels = x_conv.shape
    width = channels // heads
    state_width = bc_conv.shape[1] // 2
    mask = block_mask(tokens, rows)
    b_rows = bc_conv[:, :state_width].astype(BF16)
    c_rows = bc_conv[:, state_width:].astype(BF16)
    cum_across = cum_log.T
    step_across = step_size.T
    scores = across(c_rows, b_rows, 1)
    spread = spreader(width, channels)
    skip_row = widened(jnp.broadcast_to(padded(skip_gain[...]), (EDGE, LANES)), spread)[:1]
    per_tile = LANES // width
    lane_head = iota((tokens, LANES), 1) // width
    for tile in range(channels // LANES):
        lanes = slice(tile * LANES, (tile + 1) * LANES)
        x_tile = x_conv[:, lanes].astype(F32)
        within = skip_row[:, lanes] * x_tile
        for k in range(per_tile):
            h = tile * per_tile + k
            gaps = cum_log[:, h : h + 1] - cum_across[h : h + 1, :]
            decays = jnp.exp(jnp.where(mask, gaps, -1e30))
            mixing = (scores * decays * step_across[h : h + 1, :]).astype(BF16)
            within += dot(mixing, jnp.where(lane_head == k, x_tile, 0.0).astype(BF16))
        y_out[:, lanes] = within


def packed_message(message_out, total, side):
    high, low = halves(side[:1])
    at = iota(side.shape, 0)
    rows = jnp.where(at == 0, high.astype(F32), jnp.where(at == 1, low.astype(F32), side))
    message_out[...] = jnp.concatenate([total, rows], axis=0).astype(BF16)


def unpacked(message, state_width):
    whole = message[...].astype(F32)
    side = whole[state_width:]
    return whole[:state_width], side[0:1] + side[1:2], side


def convolved(joined, edge, raw, taps_of, taps):
    count, lanes = raw.shape
    margin = taps - 1
    joined[:EDGE, :lanes] = edge
    joined[EDGE : EDGE + count, :lanes] = raw
    starts = [EDGE - margin + k for k in range(taps)]
    return silu(sum(taps_of(k) * joined[s : s + count, :lanes] for k, s in enumerate(starts)))


def state_kernel(
    heads,
    place,
    x_raw,
    bc_raw,
    step_size,
    decay_log,
    conv_x,
    conv_bc,
    x_out,
    bc_out,
    cum_out,
    state_out,
    joined,
):
    tokens, channels = x_raw.shape
    state_width = bc_raw.shape[1] // 2
    taps = conv_x.shape[0]
    margin = taps - 1
    bc_taps = joined_taps(conv_bc)
    step_lanes = 2 * LANES
    raw = bc_raw[...].astype(F32)
    none = jnp.zeros((EDGE, step_lanes), F32)
    bc_conv = convolved(joined, none[:, :LANES], raw, lambda k: bc_taps[k : k + 1], taps)
    bc_out[...] = bc_conv.astype(BF16)
    cum_log = summed_logs(step_size[...], decay_log, block_mask(tokens, 1))
    cum_out[...] = cum_log
    spread = spreader(channels // heads, channels)
    to_end = jnp.exp(cum_log[tokens - 1 : tokens] - cum_log) * step_size[...]
    b_turned = bc_conv.T[:state_width]
    b_turned = jnp.where(iota(b_turned.shape, 1) >= margin, b_turned, 0.0).astype(BF16)
    for lane in range(0, channels, step_lanes):
        lanes = slice(lane, lane + step_lanes)
        raw = x_raw[:, lanes].astype(F32)
        x_conv = convolved(joined, none, raw, lambda k: conv_x[k : k + 1, lanes], taps).astype(BF16)
        x_out[:, lanes] = x_conv
        scale = widened(to_end, spread[:, lanes])
        weighted = (x_conv.astype(F32) * scale).astype(BF16)
        state_out[:, lanes] = dot(b_turned, weighted)


def fix_kernel(
    heads,
    place,
    halo,
    x_raw,
    bc_raw,
    step_size,
    cum_log,
    conv_x,
    conv_bc,
    partial,
    x_out,
    bc_out,
    message_out,
    state_out,
    joined,
):
    tokens, channels = x_raw.shape
    state_width = bc_raw.shape[1] // 2
    taps = conv_x.shape[0]
    margin = taps - 1
    last = 2 * EDGE
    edge = halo[...].astype(F32)[EDGE:]
    bc_taps = joined_taps(conv_bc)
    raw = bc_raw[:last, :].astype(F32)
    bc_conv = convolved(joined, edge[:, channels:], raw, lambda k: bc_taps[k : k + 1], taps)
    bc_out[...] = bc_conv.astype(BF16)
    raw = x_raw[:last, :].astype(F32)
    x_conv = convolved(joined, edge[:, :channels], raw, lambda k: conv_x[k : k + 1], taps)
    x_conv = x_conv.astype(BF16)
    x_out[...] = x_conv
    spread = spreader(channels // heads, channels)
    final = cum_log[tokens - 1 : tokens, :]
    to_end = jnp.exp(final - cum_log[:last, :]) * step_size[:last, :]
    both = jnp.concatenate([to_end, jnp.broadcast_to(jnp.exp(final), (last, LANES))], axis=0)
    both = widened(both, spread)
    weighted = (x_conv.astype(F32) * both[:last]).astype(BF16).astype(F32)
    fill = jnp.zeros((LANES - last, LANES), F32)
    b_turned = jnp.concatenate([bc_conv, fill], axis=0).T[:state_width]
    b_turned = jnp.where(iota(b_turned.shape, 1) < margin, b_turned, 0.0).astype(BF16)
    fill = jnp.zeros((LANES - last, channels), F32)
    weighted = jnp.concatenate([weighted, fill], axis=0).astype(BF16)
    total = partial[...] + dot(b_turned, weighted)
    bc_tail = bc_raw[tokens - last :, :].astype(F32)[last - margin :]
    bc_tail = jnp.concatenate([bc_tail, jnp.zeros((margin, channels - LANES), F32)], axis=1)
    x_tail = x_raw[tokens - last :, :].astype(F32)[last - margin :]
    blank = jnp.zeros((EDGE - 1 - 2 * margin, channels), F32)
    side = jnp.concatenate([both[last : last + 1], blank, x_tail, bc_tail], axis=0)
    state_out[:state_width, :] = total
    state_out[state_width:, :] = side
    packed_message(message_out, total, side)


def mix_kernel(
    heads, place, x_head, bc_head, x_rest, bc_rest, step_size, cum_log, skip_gain, y_out, reach_out, bc_out, x_conv
):
    first = x_head.shape[0]
    x_conv[:first, :] = x_head[...]
    x_conv[first:, :] = x_rest[first:, :]
    bc_out[:first, :] = bc_head[...]
    bc_out[first:, :] = bc_rest[first:, :]
    cum_log = cum_log[...]
    reach_out[...] = jnp.exp(cum_log)
    mixed_rows(1, heads, x_conv, bc_out[...].astype(F32), step_size[...], cum_log, skip_gain, y_out)


def step_kernel(first, place, message, state, came, message_out, state_out, came_out):
    later = place[0] > 0
    state_width = state.shape[0] - EDGE
    channels = state.shape[1]
    other, other_decay, other_side = unpacked(message, state_width)
    mine, my_side = state[:state_width, :], state[state_width:, :]
    my_decay = my_side[:1]
    if first:
        before, passed = jnp.zeros_like(mine), jnp.ones_like(my_decay)
    else:
        before, passed = came[:state_width, :], came[state_width : state_width + 1, :]
    came_out[:state_width, :] = jnp.where(later, passed * other + before, before)
    passed = jnp.where(later, passed * other_decay, passed)
    came_out[state_width:, :] = jnp.broadcast_to(passed, (EDGE, channels))
    total = jnp.where(later, my_decay * other + mine, other_decay * mine + other)
    state_out[:state_width, :] = total
    side = jnp.where(later, my_side, other_side)
    side = jnp.where(iota((EDGE, channels), 0) == 0, my_decay * other_decay, side)
    state_out[state_width:, :] = side
    packed_message(message_out, total, side)


def finished(heads, me, incoming, y, bc, reach, gain, weight, outs, full, mixed):
    tokens, channels = y.shape
    high, low = halves(incoming)
    blank = jnp.zeros_like(high)
    table = jnp.concatenate([blank, high, blank, low], axis=0)
    twice = jnp.concatenate([bc, bc], axis=1)
    spread = spreader(channels // heads, channels)
    step_lanes = 2 * LANES
    square = jnp.zeros((tokens, 1), F32)
    for lane in range(0, channels, step_lanes):
        lanes = slice(lane, lane + step_lanes)
        total = y[:, lanes] + dot(twice, table[:, lanes]) * widened(reach, spread[:, lanes])
        full[:, lanes] = total
        square = square + jnp.sum(total * total, axis=1, keepdims=True)
    factor = lax.rsqrt(square / channels + EPS)
    mixed[...] = (full[...] * factor * gain[...]).astype(BF16)
    sent(me, mixed, weight, zip((3, 1, 2, 0), outs))


def sent(me, mixed, weight, wanted):
    part = weight.shape[1] // PARTS
    for r, out in wanted:
        columns = pl.ds(pl.multiple_of((me ^ r) * part, part), part)
        out[...] = dot(mixed[...], weight[:, columns]).astype(out.dtype)


def rest_kernel(place, mixed, weight, sent1, kept2, kept0):
    sent(place[0], mixed, weight, ((1, sent1), (2, kept2), (0, kept0)))


def prompt_back_kernel(
    heads, place, message, came, y, bc, reach, gain, weight, sent3, mixed, full
):
    me, later = place[0], place[1] > 0
    state_width = came.shape[0] - EDGE
    other, _, _ = unpacked(message, state_width)
    before, passed = came[:state_width, :], came[state_width : state_width + 1, :]
    incoming = jnp.where(later, passed * other + before, before)
    finished(heads, me, incoming, y, bc[...], reach[...], gain, weight, (sent3,), full, mixed)


def decode_back_kernel(
    rows,
    heads,
    place,
    message,
    state,
    x_raw,
    bc_raw,
    step_size,
    decay_log,
    conv_x,
    conv_bc,
    skip_gain,
    gain,
    weight,
    sent3,
    sent1,
    kept2,
    kept0,
    full,
    mixed,
    joined,
    x_conv,
    y,
):
    me, later = place[0], place[1] > 0
    state_width = state.shape[0] - EDGE
    tokens, channels = x_raw.shape
    taps = conv_x.shape[0]
    margin = taps - 1
    other, other_decay, other_side = unpacked(message, state_width)
    mine, my_side = state[:state_width, :], state[state_width:, :]
    incoming = jnp.where(later, my_side[:1] * other + mine, other_decay * mine + other)
    side = jnp.where(later, my_side, other_side)
    x_tail = side[EDGE - 2 * margin : EDGE - margin]
    bc_tail = side[EDGE - margin :, :LANES]

    def convolved(raw, tail, taps_of):
        lanes = raw.shape[1]
        for m in range(margin):
            joined[m * rows : (m + 1) * rows, :lanes] = jnp.broadcast_to(
                tail[m : m + 1], (rows, lanes)
            )
        joined[margin * rows :, :lanes] = raw
        return silu(
            sum(taps_of(k) * joined[k * rows : k * rows + tokens, :lanes] for k in range(taps))
        )

    bc_taps = joined_taps(conv_bc)
    bc_conv = convolved(bc_raw[...].astype(F32), bc_tail, lambda k: bc_taps[k : k + 1])
    step_lanes = 2 * LANES
    for lane in range(0, channels, step_lanes):
        lanes = slice(lane, lane + step_lanes)
        x_conv[:, lanes] = convolved(
            x_raw[:, lanes].astype(F32), x_tail[:, lanes], lambda k: conv_x[k : k + 1, lanes]
        ).astype(BF16)
    cum_log = summed_logs(step_size[...], decay_log, block_mask(tokens, rows))
    mixed_rows(rows, heads, x_conv, bc_conv, step_size[...], cum_log, skip_gain, y)
    bc = bc_conv.astype(BF16)
    outs = (sent3, sent1, kept2, kept0)
    finished(heads, me, incoming, y, bc, jnp.exp(cum_log), gain, weight, outs, full, mixed)


def far_kernel(place, kept, got, out):
    out[...] = (kept[...] + got[...].astype(F32)).astype(BF16)


def total_kernel(rows, place, kept, got, far, dec_kept, dec_got, dec_far, out, dec_out):
    out[...] = (kept[...] + got[...].astype(F32) + far[...].astype(F32)).astype(BF16)
    total = dec_kept[...] + dec_got[...].astype(F32) + dec_far[...].astype(F32)
    asked = total.shape[0]
    steps = asked // rows
    at = iota((asked, asked), 0)
    order = (at % steps) * rows + at // steps == iota((asked, asked), 1)
    total = dot(jnp.where(order, 1.0, 0.0).astype(BF16), total.astype(BF16))
    for r in range(rows):
        dec_out[r] = total[r * steps : (r + 1) * steps].astype(BF16)


def note_kernel(place, ids, note):
    steps = ids.shape[0]
    ids = ids[...]
    digits = [padded(d.astype(F32)) for d in (ids & 255, (ids >> 8) & 255, ids >> 16)]
    top = jnp.concatenate(digits, axis=1)
    note[...] = jnp.concatenate([top, jnp.zeros((EDGE - steps, 3 * LANES), F32)], axis=0).astype(BF16)


def join_kernel(place, mine, got, out):
    out[...] = jnp.concatenate([mine[...].astype(F32), got[...].astype(F32)], axis=0).astype(BF16)


def hand_kernel(place, given, handed):
    del given, handed


def lookup_kernel(
    steps, rows, place, notes, got, table_in, kept_out, sent_out, wanted, found, table, sems
):
    chunks, chunk, _ = table.shape
    copies = started(
        [(table_in.at[pl.ds(c * chunk, chunk), :], table.at[c]) for c in range(chunks)], sems
    )
    first = (place[0] * (chunks * chunk)).astype(F32)
    held = jnp.concatenate([notes[...].astype(F32), got[...].astype(F32)], axis=0)
    groups = held.shape[0] // EDGE
    digits = held[:, :LANES] + held[:, LANES : 2 * LANES] * 256.0 + held[:, 2 * LANES : 3 * LANES] * 65536.0
    same = iota((rows, LANES), 0) == iota((rows, LANES), 1)
    for q in range(groups):
        for s in range(steps):
            line = jnp.broadcast_to(digits[q * EDGE + s : q * EDGE + s + 1], (rows, LANES))
            column = jnp.sum(jnp.where(same, line, 0.0), axis=1, keepdims=True) - first
            at = (q * steps + s) * rows
            wanted[at : at + rows, :] = jnp.broadcast_to(column, (rows, LANES))
    asked = groups * steps * rows
    block = min(asked, 256)
    lane = iota((block, LANES), 1).astype(F32)
    for c in range(chunks):
        copies[c].wait()
        for at in range(0, asked, block):
            gap = wanted[at : at + block, :] - lane
            hot = [
                jnp.where(gap == float(c * chunk + k), 1.0, 0.0).astype(BF16)
                for k in range(0, chunk, LANES)
            ]
            term = dot(jnp.concatenate(hot, axis=1), table[c])
            if c == 0:
                found[at : at + block, :] = term
            else:
                found[at : at + block, :] += term
    kept_out[...] = found[: asked // 2, :].astype(BF16)
    sent_out[...] = found[asked // 2 :, :].astype(BF16)


def fold_kernel(place, kept, got, kept_out, sent_out):
    total = (kept[...].astype(F32) + got[...].astype(F32)).astype(BF16)
    half = kept_out.shape[0]
    kept_out[...] = total[:half]
    sent_out[...] = total[half:]


def last_fold_kernel(place, kept, got, out):
    out[...] = (kept[...].astype(F32) + got[...].astype(F32)).astype(BF16)


VMEM = pl.BlockSpec(memory_space=pltpu.VMEM)
SMEM = pl.BlockSpec(memory_space=pltpu.SMEM)
HBM = pl.BlockSpec(memory_space=pltpu.HBM)


class Caller:
    def __init__(self):
        self.token = jnp.zeros((8, LANES), F32)

    def __call__(self, kernel, place, inputs, outs, scratch=(), us=1.0, limit=4, far=(), same=()):
        inputs = list(inputs)
        count = len(inputs)

        def ordered(place, token, *refs):
            refs, token_out = list(refs), refs[count]
            del refs[count]
            kernel(place, *refs)
            token_out[...] = jnp.zeros_like(token_out)

        results = pl.pallas_call(
            ordered,
            out_shape=[shaped((8, LANES), F32)] + outs,
            in_specs=[SMEM, VMEM] + [HBM if at in far else VMEM for at in range(count)],
            out_specs=[VMEM] * (1 + len(outs)),
            scratch_shapes=list(scratch),
            input_output_aliases={2 + at: 1 + out for at, out in same},
            compiler_params=pltpu.CompilerParams(vmem_limit_bytes=limit * MEBI),
            cost_estimate=pl.CostEstimate(
                flops=int(us * 1e9), bytes_accessed=int(us * 1e6), transcendentals=0
            ),
        )(place, self.token, *inputs)
        self.token = results[0]
        return results[1:]


def shaped(shape, dtype):
    return jax.ShapeDtypeStruct(shape, dtype)


def on_device(
    prompt_embeds,
    decode_ids,
    embed_table,
    norm_gain,
    x_weight,
    bc_weight,
    dt_weight,
    dt_bias,
    decay_log,
    conv_x,
    conv_bc,
    skip_gain,
    out_gain,
    out_weight,
):
    heads = dt_weight.shape[1]
    assert bc_weight.shape[1] == 1 and lax.axis_size("tp") == PARTS
    channels = x_weight.shape[1]
    taps = conv_x.shape[0]
    margin = taps - 1
    turned_bc = bc_weight.transpose(1, 2, 3, 0).reshape(-1, bc_weight.shape[0])
    turned_dt = dt_weight.T
    state_width = turned_bc.shape[0] // 2
    assert turned_bc.shape[0] == LANES
    tokens, part = prompt_embeds.shape
    rows, steps = decode_ids.shape
    assert steps <= EDGE and rows <= LANES and 2 * margin < EDGE
    asked = rows * steps
    groups = lax.axis_size("ctx")
    me_c = lax.axis_index("ctx").astype(jnp.int32)
    me_t = lax.axis_index("tp").astype(jnp.int32)
    vocab_here = embed_table.shape[0]
    bits = bits_of("ctx")
    assert len(bits) >= 2
    none = jnp.zeros((1,), jnp.int32)
    called = Caller()

    e2 = swapped(prompt_embeds, "tp", 2)
    e1 = swapped(prompt_embeds, "tp", 1)


    (notes,) = called(
        note_kernel, none, [decode_ids.T], [shaped((EDGE, 3 * LANES), BF16)], us=2
    )
    halving = [bits[1], bits[0]] + bits[2:]

    def joined(notes, bit):
        out = shaped((2 * notes.shape[0], notes.shape[1]), BF16)
        return called(join_kernel, none, [notes, swapped(notes, "ctx", bit)], [out], us=0.05)[0]

    notes = joined(notes, halving[-1])
    (e2,) = called(
        hand_kernel, none, [e2], [shaped(e2.shape, BF16)], us=0.05, same=((0, 0),)
    )
    e3 = swapped(e2, "tp", 1)

    project_weights = [
        norm_gain.reshape(PARTS, 1, part),
        x_weight,
        turned_bc,
        turned_dt,
        dt_bias.reshape(1, -1),
    ]
    conv_weights = [decay_log.reshape(1, -1), conv_x, conv_bc.reshape(taps, 2, -1)]
    skip_row, gain_row = skip_gain.reshape(1, -1), out_gain.reshape(1, -1)
    packed = state_width + EDGE

    def project(prompt, blocks, us):
        count = blocks[0].shape[0]
        scratch = []
        outs = [
            shaped((count, channels), BF16),
            shaped((count, LANES), BF16),
            shaped((count, LANES), F32),
        ]
        if prompt:
            outs.append(shaped((2 * EDGE, channels + LANES), BF16))
            scratch = [
                pltpu.VMEM((PARTS, part, channels), BF16),
                pltpu.VMEM((count, channels), F32),
                pltpu.SemaphoreType.DMA((PARTS,)),
            ]
        return called(
            functools.partial(project_kernel, prompt),
            me_t.reshape(1),
            blocks + project_weights,
            outs,
            [pltpu.VMEM((PARTS, count, part), BF16)] + scratch,
            us=us,
            limit=50 if prompt else 12,
            far=(5,) if prompt else (),
        )

    x_raw, bc_raw, step_size, halo = project(True, [prompt_embeds, e1, e2, e3], 3)
    for bit in reversed(halving[1:-1]):
        notes = joined(notes, bit)
    got = swapped(notes, "ctx", halving[0])
    halo = lax.ppermute(halo, "ctx", [(c, c + 1) for c in range(groups - 1)])

    half = groups * asked // 2
    chunk = max(LANES, vocab_here // 4)
    assert vocab_here % chunk == 0
    kept, sent = called(
        functools.partial(lookup_kernel, steps, rows),
        me_c.reshape(1),
        [notes, got, embed_table],
        [shaped((half, part), BF16), shaped((half, part), BF16)],
        [
            pltpu.VMEM((2 * half, LANES), F32),
            pltpu.VMEM((2 * half, part), F32),
            pltpu.VMEM((vocab_here // chunk, chunk, part), BF16),
            pltpu.SemaphoreType.DMA((vocab_here // chunk,)),
        ],
        us=3.5,
        limit=50,
        far=(2,),
    )

    x_rest, bc_rest, cum_log, partial = called(
        functools.partial(state_kernel, heads),
        none,
        [x_raw, bc_raw, step_size] + conv_weights,
        [
            shaped((tokens, channels), BF16),
            shaped((tokens, LANES), BF16),
            shaped((tokens, LANES), F32),
            shaped((state_width, channels), F32),
        ],
        [pltpu.VMEM((EDGE + tokens, 2 * LANES), F32)],
        us=2,
        limit=8,
    )
    x_head, bc_head, message, state = called(
        functools.partial(fix_kernel, heads),
        none,
        [halo, x_raw, bc_raw, step_size, cum_log] + conv_weights[1:] + [partial],
        [
            shaped((2 * EDGE, channels), BF16),
            shaped((2 * EDGE, LANES), BF16),
            shaped((packed, channels), BF16),
            shaped((state_width + EDGE, channels), F32),
        ],
        [pltpu.VMEM((3 * EDGE, channels), F32)],
        limit=8,
    )
    came = state
    def folded(kept, got):
        half = kept.shape[0] // 2
        return called(
            fold_kernel,
            none,
            [kept, got],
            [shaped((half, part), BF16), shaped((half, part), BF16)],
            limit=16 if half > 512 else 4,
        )

    y, reach, bc = called(
        functools.partial(mix_kernel, heads),
        none,
        [x_head, bc_head, x_rest, bc_rest, step_size, cum_log, skip_row],
        [
            shaped((tokens, channels), F32),
            shaped((tokens, LANES), F32),
            shaped((tokens, LANES), BF16),
        ],
        [pltpu.VMEM((tokens, channels), BF16)],
        us=2.5,
        limit=8,
    )

    for bit, halved in zip(bits, halving):
        embeds = swapped(sent, "ctx", halved)
        if halved == halving[-1]:
            (kept,) = called(last_fold_kernel, none, [kept, embeds], [shaped((asked, part), BF16)])
        else:
            kept, sent = folded(kept, embeds)
        got = swapped(message, "ctx", bit)
        later = ((me_c & bit) != 0).astype(jnp.int32)
        if bit != bits[-1]:
            message, state, came = called(
                functools.partial(step_kernel, bit == bits[0]),
                later.reshape(1),
                [got, state, came],
                [
                    shaped((packed, channels), BF16),
                    shaped((state_width + EDGE, channels), F32),
                    shaped((state_width + EDGE, channels), F32),
                ],
            )
    back_place = jnp.stack([me_t, later])
    near = swapped(kept, "tp", 2)
    over1 = swapped(kept, "tp", 1)
    over3 = swapped(near, "tp", 1)

    def back(kernel, count, inputs, scratch, us):
        return called(
            kernel,
            back_place,
            [got] + inputs + [gain_row, out_weight],
            [shaped((count, part), BF16)] * 2 + [shaped((count, part), F32)] * 2,
            [pltpu.VMEM((count, channels), F32), pltpu.VMEM((count, channels), BF16)] + scratch,
            us=us,
            limit=12,
        )

    def crossed(sent3, sent1, kept2, kept0):
        got3 = swapped(sent3, "tp", 1)
        got1 = swapped(sent1, "tp", 1)
        (far,) = called(far_kernel, none, [kept2, got3], [shaped(kept2.shape, BF16)])
        return kept0, got1, swapped(far, "tp", 2)

    prompt_sent3, prompt_mixed = called(
        functools.partial(prompt_back_kernel, heads),
        back_place,
        [got, came, y, bc, reach, gain_row, out_weight],
        [shaped((tokens, part), BF16), shaped((tokens, channels), BF16)],
        [pltpu.VMEM((tokens, channels), F32)],
        us=1.5,
        limit=12,
    )
    prompt_rest = called(
        rest_kernel,
        back_place,
        [prompt_mixed, out_weight],
        [shaped((tokens, part), BF16)] + [shaped((tokens, part), F32)] * 2,
    )
    dec_x_raw, dec_bc_raw, dec_step = project(False, [kept, over1, near, over3], 1.5)
    prompt_crossed = crossed(prompt_sent3, *prompt_rest)
    decode_back = back(
        functools.partial(decode_back_kernel, rows, heads),
        asked,
        [state, dec_x_raw, dec_bc_raw, dec_step] + conv_weights + [skip_row],
        [
            pltpu.VMEM((margin * rows + asked, 2 * LANES), F32),
            pltpu.VMEM((asked, channels), BF16),
            pltpu.VMEM((asked, channels), F32),
        ],
        2.5,
    )
    decode_crossed = crossed(*decode_back)
    prompt_out, decode_out = called(
        functools.partial(total_kernel, rows),
        none,
        [*prompt_crossed, *decode_crossed],
        [shaped((tokens, part), BF16), shaped((rows, steps, part), BF16)],
    )
    return (prompt_out, decode_out)


def solution(mesh):
    return jax.shard_map(
        on_device,
        mesh=mesh,
        in_specs=(
            P("ctx", "tp"),
            P("ctx", None),
            P("ctx", "tp"),
            P(),
            P(None, "tp"),
            P(None, "tp", None, None),
            P(None, "tp"),
            P("tp"),
            P("tp"),
            P(None, "tp"),
            P(None, "tp", None, None),
            P("tp"),
            P("tp"),
            P("tp", None),
        ),
        out_specs=(P("ctx", "tp"), P("ctx", None, "tp")),
        check_vma=False,
    )
```

```python
import functools

import jax
import jax.numpy as jnp
from jax import lax
from jax.experimental import pallas as pl
from jax.experimental.pallas import tpu as pltpu
from jax.sharding import PartitionSpec as P

EPS = 1e-05
BF16 = jnp.bfloat16
F32 = jnp.float32
LANES = 128
PARTS = 4
EDGE = 8
MEBI = 1024 * 1024


def swapped(value, axis, bit):
    count = lax.axis_size(axis)
    return lax.ppermute(value, axis, [(i, i ^ bit) for i in range(count)])


def bits_of(axis):
    count = lax.axis_size(axis)
    assert count & (count - 1) == 0
    return [1 << k for k in range(count.bit_length() - 1)]


def dot(a, b):
    return jnp.dot(a, b, preferred_element_type=F32)


def across(a, b, axis):
    return lax.dot_general(a, b, (((axis,), (axis,)), ((), ())), preferred_element_type=F32)


def halves(value):
    high = value.astype(BF16)
    low = (value - high.astype(F32)).astype(BF16)
    return high, low


def iota(shape, axis):
    return lax.broadcasted_iota(jnp.int32, shape, axis)


def spreader(width, channels):
    head = iota((2 * LANES, channels), 0) & (LANES - 1)
    return jnp.where(head == iota((2 * LANES, channels), 1) // width, 1.0, 0.0).astype(BF16)


def widened(per_head, spread):
    high, low = halves(per_head)
    return dot(jnp.concatenate([high, low], axis=1), spread)


def padded(row):
    return jnp.concatenate([row, jnp.zeros((row.shape[0], LANES - row.shape[1]), F32)], axis=1)


def silu(value):
    return value / (1.0 + jnp.exp(-value))


def started(pairs, sems):
    copies = [
        pltpu.make_async_copy(source, target, sems.at[at])
        for at, (source, target) in enumerate(pairs)
    ]
    for copy in copies:
        copy.start()
    return copies


def project_kernel(
    prompt,
    place,
    own,
    over1,
    over2,
    over3,
    gain,
    x_weight,
    bc_weight,
    dt_weight,
    dt_bias,
    x_out,
    bc_out,
    step_out,
    *rest,
):
    if prompt:
        halo_out, normed, chunks, total, sems = rest
        copies = started(
            [(x_weight.at[pl.ds(j * chunks.shape[1], chunks.shape[1]), :], chunks.at[j]) for j in range(PARTS)],
            sems,
        )
    else:
        (normed,) = rest
    me = place[0]
    tokens, part = own.shape
    channels, heads = x_weight.shape[1], dt_weight.shape[0]
    blocks = [ref[...].astype(F32) for ref in (own, over1, over2, over3)]
    square = sum(jnp.sum(b * b, axis=1, keepdims=True) for b in blocks)
    factor = lax.rsqrt(square / (PARTS * part) + EPS)
    for r in range(PARTS):
        normed[me ^ r] = (blocks[r] * factor * gain[me ^ r]).astype(BF16)
    fill = jnp.zeros((LANES - heads, PARTS * part), BF16)
    side = jnp.concatenate([bc_weight[...], dt_weight[...], fill], axis=0)
    raw = sum(across(normed[j], side[:, j * part : (j + 1) * part], 1) for j in range(PARTS))
    bc_out[...] = raw[:, :LANES].astype(BF16)
    pre = raw[:, LANES:] + padded(dt_bias[...])
    step_out[...] = jnp.maximum(pre, 0.0) + jnp.log1p(jnp.exp(-jnp.abs(pre)))
    last = 2 * EDGE
    step_lanes = 2 * LANES
    if not prompt:
        for lane in range(0, channels, step_lanes):
            lanes = slice(lane, lane + step_lanes)
            terms = [dot(normed[j], x_weight[j * part : (j + 1) * part, lanes]) for j in range(PARTS)]
            x_out[:, lanes] = sum(terms).astype(BF16)
        return
    halo_out[:, channels:] = raw[tokens - last :, :LANES].astype(BF16)
    for j in range(PARTS):
        copies[j].wait()
        for lane in range(0, channels, step_lanes):
            lanes = slice(lane, lane + step_lanes)
            term = dot(normed[j], chunks[j, :, lanes])
            if j > 0:
                term = total[:, lanes] + term
            if j < PARTS - 1:
                total[:, lanes] = term
            else:
                x_out[:, lanes] = term.astype(BF16)
                halo_out[:, lanes] = term[tokens - last :].astype(BF16)


def summed_logs(step_size, decay_log, mask):
    logs = step_size * -jnp.exp(padded(decay_log[...]))
    high, low = halves(logs)
    lowest = (logs - high.astype(F32) - low.astype(F32)).astype(BF16)
    sums = dot(
        jnp.where(mask, 1.0, 0.0).astype(BF16), jnp.concatenate([high, low, lowest], axis=1)
    )
    return sums[:, :LANES] + sums[:, LANES : 2 * LANES] + sums[:, 2 * LANES :]


def joined_taps(conv_bc):
    return jnp.concatenate([conv_bc[:, 0, :], conv_bc[:, 1, :]], axis=1)


def block_mask(tokens, rows):
    t_at = iota((tokens, tokens), 0)
    s_at = iota((tokens, tokens), 1)
    mask = t_at >= s_at
    return mask if rows == 1 else jnp.logical_and(mask, t_at % rows == s_at % rows)


def mixed_rows(rows, heads, x_conv, bc_conv, step_size, cum_log, skip_gain, y_out):
    tokens, channels = x_conv.shape
    width = channels // heads
    state_width = bc_conv.shape[1] // 2
    mask = block_mask(tokens, rows)
    b_rows = bc_conv[:, :state_width].astype(BF16)
    c_rows = bc_conv[:, state_width:].astype(BF16)
    cum_across = cum_log.T
    step_across = step_size.T
    scores = across(c_rows, b_rows, 1)
    spread = spreader(width, channels)
    skip_row = widened(jnp.broadcast_to(padded(skip_gain[...]), (EDGE, LANES)), spread)[:1]
    per_tile = LANES // width
    lane_head = iota((tokens, LANES), 1) // width
    for tile in range(channels // LANES):
        lanes = slice(tile * LANES, (tile + 1) * LANES)
        x_tile = x_conv[:, lanes].astype(F32)
        within = skip_row[:, lanes] * x_tile
        for k in range(per_tile):
            h = tile * per_tile + k
            gaps = cum_log[:, h : h + 1] - cum_across[h : h + 1, :]
            decays = jnp.exp(jnp.where(mask, gaps, -1e30))
            mixing = (scores * decays * step_across[h : h + 1, :]).astype(BF16)
            within += dot(mixing, jnp.where(lane_head == k, x_tile, 0.0).astype(BF16))
        y_out[:, lanes] = within


def packed_message(message_out, total, side):
    high, low = halves(side[:1])
    at = iota(side.shape, 0)
    rows = jnp.where(at == 0, high.astype(F32), jnp.where(at == 1, low.astype(F32), side))
    message_out[...] = jnp.concatenate([total, rows], axis=0).astype(BF16)


def unpacked(message, state_width):
    whole = message[...].astype(F32)
    side = whole[state_width:]
    return whole[:state_width], side[0:1] + side[1:2], side


def convolved(joined, edge, raw, taps_of, taps):
    count, lanes = raw.shape
    margin = taps - 1
    joined[:EDGE, :lanes] = edge
    joined[EDGE : EDGE + count, :lanes] = raw
    starts = [EDGE - margin + k for k in range(taps)]
    return silu(sum(taps_of(k) * joined[s : s + count, :lanes] for k, s in enumerate(starts)))


def state_kernel(
    heads,
    place,
    x_raw,
    bc_raw,
    step_size,
    decay_log,
    conv_x,
    conv_bc,
    x_out,
    bc_out,
    cum_out,
    state_out,
    joined,
):
    tokens, channels = x_raw.shape
    state_width = bc_raw.shape[1] // 2
    taps = conv_x.shape[0]
    margin = taps - 1
    bc_taps = joined_taps(conv_bc)
    step_lanes = 2 * LANES
    raw = bc_raw[...].astype(F32)
    none = jnp.zeros((EDGE, step_lanes), F32)
    bc_conv = convolved(joined, none[:, :LANES], raw, lambda k: bc_taps[k : k + 1], taps)
    bc_out[...] = bc_conv.astype(BF16)
    cum_log = summed_logs(step_size[...], decay_log, block_mask(tokens, 1))
    cum_out[...] = cum_log
    spread = spreader(channels // heads, channels)
    to_end = jnp.exp(cum_log[tokens - 1 : tokens] - cum_log) * step_size[...]
    b_turned = bc_conv.T[:state_width]
    b_turned = jnp.where(iota(b_turned.shape, 1) >= margin, b_turned, 0.0).astype(BF16)
    for lane in range(0, channels, step_lanes):
        lanes = slice(lane, lane + step_lanes)
        raw = x_raw[:, lanes].astype(F32)
        x_conv = convolved(joined, none, raw, lambda k: conv_x[k : k + 1, lanes], taps).astype(BF16)
        x_out[:, lanes] = x_conv
        scale = widened(to_end, spread[:, lanes])
        weighted = (x_conv.astype(F32) * scale).astype(BF16)
        state_out[:, lanes] = dot(b_turned, weighted)


def fix_kernel(
    heads,
    place,
    halo,
    x_raw,
    bc_raw,
    step_size,
    cum_log,
    conv_x,
    conv_bc,
    partial,
    x_out,
    bc_out,
    message_out,
    state_out,
    joined,
):
    tokens, channels = x_raw.shape
    state_width = bc_raw.shape[1] // 2
    taps = conv_x.shape[0]
    margin = taps - 1
    last = 2 * EDGE
    edge = halo[...].astype(F32)[EDGE:]
    bc_taps = joined_taps(conv_bc)
    raw = bc_raw[:last, :].astype(F32)
    bc_conv = convolved(joined, edge[:, channels:], raw, lambda k: bc_taps[k : k + 1], taps)
    bc_out[...] = bc_conv.astype(BF16)
    raw = x_raw[:last, :].astype(F32)
    x_conv = convolved(joined, edge[:, :channels], raw, lambda k: conv_x[k : k + 1], taps)
    x_conv = x_conv.astype(BF16)
    x_out[...] = x_conv
    spread = spreader(channels // heads, channels)
    final = cum_log[tokens - 1 : tokens, :]
    to_end = jnp.exp(final - cum_log[:last, :]) * step_size[:last, :]
    both = jnp.concatenate([to_end, jnp.broadcast_to(jnp.exp(final), (last, LANES))], axis=0)
    both = widened(both, spread)
    weighted = (x_conv.astype(F32) * both[:last]).astype(BF16).astype(F32)
    fill = jnp.zeros((LANES - last, LANES), F32)
    b_turned = jnp.concatenate([bc_conv, fill], axis=0).T[:state_width]
    b_turned = jnp.where(iota(b_turned.shape, 1) < margin, b_turned, 0.0).astype(BF16)
    fill = jnp.zeros((LANES - last, channels), F32)
    weighted = jnp.concatenate([weighted, fill], axis=0).astype(BF16)
    total = partial[...] + dot(b_turned, weighted)
    bc_tail = bc_raw[tokens - last :, :].astype(F32)[last - margin :]
    bc_tail = jnp.concatenate([bc_tail, jnp.zeros((margin, channels - LANES), F32)], axis=1)
    x_tail = x_raw[tokens - last :, :].astype(F32)[last - margin :]
    blank = jnp.zeros((EDGE - 1 - 2 * margin, channels), F32)
    side = jnp.concatenate([both[last : last + 1], blank, x_tail, bc_tail], axis=0)
    state_out[:state_width, :] = total
    state_out[state_width:, :] = side
    packed_message(message_out, total, side)


def mix_kernel(
    heads, place, x_head, bc_head, x_rest, bc_rest, step_size, cum_log, skip_gain, y_out, reach_out, bc_out, x_conv
):
    first = x_head.shape[0]
    x_conv[:first, :] = x_head[...]
    x_conv[first:, :] = x_rest[first:, :]
    bc_out[:first, :] = bc_head[...]
    bc_out[first:, :] = bc_rest[first:, :]
    cum_log = cum_log[...]
    reach_out[...] = jnp.exp(cum_log)
    mixed_rows(1, heads, x_conv, bc_out[...].astype(F32), step_size[...], cum_log, skip_gain, y_out)


def step_kernel(first, place, message, state, came, message_out, state_out, came_out):
    later = place[0] > 0
    state_width = state.shape[0] - EDGE
    channels = state.shape[1]
    other, other_decay, other_side = unpacked(message, state_width)
    mine, my_side = state[:state_width, :], state[state_width:, :]
    my_decay = my_side[:1]
    if first:
        before, passed = jnp.zeros_like(mine), jnp.ones_like(my_decay)
    else:
        before, passed = came[:state_width, :], came[state_width : state_width + 1, :]
    came_out[:state_width, :] = jnp.where(later, passed * other + before, before)
    passed = jnp.where(later, passed * other_decay, passed)
    came_out[state_width:, :] = jnp.broadcast_to(passed, (EDGE, channels))
    total = jnp.where(later, my_decay * other + mine, other_decay * mine + other)
    state_out[:state_width, :] = total
    side = jnp.where(later, my_side, other_side)
    side = jnp.where(iota((EDGE, channels), 0) == 0, my_decay * other_decay, side)
    state_out[state_width:, :] = side
    packed_message(message_out, total, side)


def finished(heads, me, incoming, y, bc, reach, gain, weight, outs, full, mixed):
    tokens, channels = y.shape
    high, low = halves(incoming)
    blank = jnp.zeros_like(high)
    table = jnp.concatenate([blank, high, blank, low], axis=0)
    twice = jnp.concatenate([bc, bc], axis=1)
    spread = spreader(channels // heads, channels)
    step_lanes = 2 * LANES
    square = jnp.zeros((tokens, 1), F32)
    for lane in range(0, channels, step_lanes):
        lanes = slice(lane, lane + step_lanes)
        total = y[:, lanes] + dot(twice, table[:, lanes]) * widened(reach, spread[:, lanes])
        full[:, lanes] = total
        square = square + jnp.sum(total * total, axis=1, keepdims=True)
    factor = lax.rsqrt(square / channels + EPS)
    mixed[...] = (full[...] * factor * gain[...]).astype(BF16)
    sent(me, mixed, weight, zip((3, 1, 2, 0), outs))


def sent(me, mixed, weight, wanted):
    part = weight.shape[1] // PARTS
    for r, out in wanted:
        columns = pl.ds(pl.multiple_of((me ^ r) * part, part), part)
        out[...] = dot(mixed[...], weight[:, columns]).astype(out.dtype)


def rest_kernel(blocks, place, mixed, weight, *outs):
    sent(place[0], mixed, weight, zip(blocks, outs))


def prompt_back_kernel(
    heads, place, message, came, y, bc, reach, gain, weight, sent3, mixed, full
):
    me, later = place[0], place[1] > 0
    state_width = came.shape[0] - EDGE
    other, _, _ = unpacked(message, state_width)
    before, passed = came[:state_width, :], came[state_width : state_width + 1, :]
    incoming = jnp.where(later, passed * other + before, before)
    finished(heads, me, incoming, y, bc[...], reach[...], gain, weight, (sent3,), full, mixed)


def decode_back_kernel(
    rows,
    heads,
    place,
    message,
    state,
    x_raw,
    bc_raw,
    step_size,
    decay_log,
    conv_x,
    conv_bc,
    skip_gain,
    prompt_mixed,
    gain,
    weight,
    sent3,
    sent1,
    kept2,
    kept0,
    prompt_kept0,
    full,
    mixed,
    joined,
    x_conv,
    y,
):
    me, later = place[0], place[1] > 0
    state_width = state.shape[0] - EDGE
    tokens, channels = x_raw.shape
    taps = conv_x.shape[0]
    margin = taps - 1
    other, other_decay, other_side = unpacked(message, state_width)
    mine, my_side = state[:state_width, :], state[state_width:, :]
    incoming = jnp.where(later, my_side[:1] * other + mine, other_decay * mine + other)
    side = jnp.where(later, my_side, other_side)
    x_tail = side[EDGE - 2 * margin : EDGE - margin]
    bc_tail = side[EDGE - margin :, :LANES]

    def convolved(raw, tail, taps_of):
        lanes = raw.shape[1]
        for m in range(margin):
            joined[m * rows : (m + 1) * rows, :lanes] = jnp.broadcast_to(
                tail[m : m + 1], (rows, lanes)
            )
        joined[margin * rows :, :lanes] = raw
        return silu(
            sum(taps_of(k) * joined[k * rows : k * rows + tokens, :lanes] for k in range(taps))
        )

    bc_taps = joined_taps(conv_bc)
    bc_conv = convolved(bc_raw[...].astype(F32), bc_tail, lambda k: bc_taps[k : k + 1])
    step_lanes = 2 * LANES
    for lane in range(0, channels, step_lanes):
        lanes = slice(lane, lane + step_lanes)
        x_conv[:, lanes] = convolved(
            x_raw[:, lanes].astype(F32), x_tail[:, lanes], lambda k: conv_x[k : k + 1, lanes]
        ).astype(BF16)
    cum_log = summed_logs(step_size[...], decay_log, block_mask(tokens, rows))
    mixed_rows(rows, heads, x_conv, bc_conv, step_size[...], cum_log, skip_gain, y)
    bc = bc_conv.astype(BF16)
    outs = (sent3, sent1, kept2, kept0)
    finished(heads, me, incoming, y, bc, jnp.exp(cum_log), gain, weight, outs, full, mixed)
    sent(me, prompt_mixed, weight, ((0, prompt_kept0),))


def far_kernel(place, kept, got, out):
    out[...] = (kept[...] + got[...].astype(F32)).astype(BF16)


def total_kernel(rows, place, kept, got, far, dec_kept, dec_got, dec_far, out, dec_out):
    out[...] = (kept[...] + got[...].astype(F32) + far[...].astype(F32)).astype(BF16)
    total = dec_kept[...] + dec_got[...].astype(F32) + dec_far[...].astype(F32)
    asked = total.shape[0]
    steps = asked // rows
    at = iota((asked, asked), 0)
    order = (at % steps) * rows + at // steps == iota((asked, asked), 1)
    total = dot(jnp.where(order, 1.0, 0.0).astype(BF16), total.astype(BF16))
    for r in range(rows):
        dec_out[r] = total[r * steps : (r + 1) * steps].astype(BF16)


def note_kernel(place, ids, note):
    steps = ids.shape[0]
    ids = ids[...]
    digits = [padded(d.astype(F32)) for d in (ids & 255, (ids >> 8) & 255, ids >> 16)]
    top = jnp.concatenate(digits, axis=1)
    note[...] = jnp.concatenate([top, jnp.zeros((EDGE - steps, 3 * LANES), F32)], axis=0).astype(BF16)


def join_kernel(place, mine, got, out):
    out[...] = jnp.concatenate([mine[...].astype(F32), got[...].astype(F32)], axis=0).astype(BF16)


def hand_kernel(place, given, handed):
    del given, handed


def lookup_kernel(
    steps, rows, place, notes, got, table_in, kept_out, sent_out, wanted, found, table, sems
):
    chunks, chunk, _ = table.shape
    copies = started(
        [(table_in.at[pl.ds(c * chunk, chunk), :], table.at[c]) for c in range(chunks)], sems
    )
    first = (place[0] * (chunks * chunk)).astype(F32)
    held = jnp.concatenate([notes[...].astype(F32), got[...].astype(F32)], axis=0)
    groups = held.shape[0] // EDGE
    digits = held[:, :LANES] + held[:, LANES : 2 * LANES] * 256.0 + held[:, 2 * LANES : 3 * LANES] * 65536.0
    same = iota((rows, LANES), 0) == iota((rows, LANES), 1)
    for q in range(groups):
        for s in range(steps):
            line = jnp.broadcast_to(digits[q * EDGE + s : q * EDGE + s + 1], (rows, LANES))
            column = jnp.sum(jnp.where(same, line, 0.0), axis=1, keepdims=True) - first
            at = (q * steps + s) * rows
            wanted[at : at + rows, :] = jnp.broadcast_to(column, (rows, LANES))
    asked = groups * steps * rows
    block = min(asked, 256)
    lane = iota((block, LANES), 1).astype(F32)
    for c in range(chunks):
        copies[c].wait()
        for at in range(0, asked, block):
            gap = wanted[at : at + block, :] - lane
            hot = [
                jnp.where(gap == float(c * chunk + k), 1.0, 0.0).astype(BF16)
                for k in range(0, chunk, LANES)
            ]
            term = dot(jnp.concatenate(hot, axis=1), table[c])
            if c == 0:
                found[at : at + block, :] = term
            else:
                found[at : at + block, :] += term
    kept_out[...] = found[: asked // 2, :].astype(BF16)
    sent_out[...] = found[asked // 2 :, :].astype(BF16)


def fold_kernel(place, kept, got, kept_out, sent_out):
    total = (kept[...].astype(F32) + got[...].astype(F32)).astype(BF16)
    half = kept_out.shape[0]
    kept_out[...] = total[:half]
    sent_out[...] = total[half:]


def last_fold_kernel(place, kept, got, out):
    out[...] = (kept[...].astype(F32) + got[...].astype(F32)).astype(BF16)


VMEM = pl.BlockSpec(memory_space=pltpu.VMEM)
SMEM = pl.BlockSpec(memory_space=pltpu.SMEM)
HBM = pl.BlockSpec(memory_space=pltpu.HBM)


class Caller:
    def __init__(self):
        self.token = jnp.zeros((8, LANES), F32)

    def __call__(self, kernel, place, inputs, outs, scratch=(), us=1.0, limit=4, far=(), same=()):
        inputs = list(inputs)
        count = len(inputs)

        def ordered(place, token, *refs):
            refs, token_out = list(refs), refs[count]
            del refs[count]
            kernel(place, *refs)
            token_out[...] = jnp.zeros_like(token_out)

        results = pl.pallas_call(
            ordered,
            out_shape=[shaped((8, LANES), F32)] + outs,
            in_specs=[SMEM, VMEM] + [HBM if at in far else VMEM for at in range(count)],
            out_specs=[VMEM] * (1 + len(outs)),
            scratch_shapes=list(scratch),
            input_output_aliases={2 + at: 1 + out for at, out in same},
            compiler_params=pltpu.CompilerParams(vmem_limit_bytes=limit * MEBI),
            cost_estimate=pl.CostEstimate(
                flops=int(us * 1e9), bytes_accessed=int(us * 1e6), transcendentals=0
            ),
        )(place, self.token, *inputs)
        self.token = results[0]
        return results[1:]


def shaped(shape, dtype):
    return jax.ShapeDtypeStruct(shape, dtype)


def on_device(
    prompt_embeds,
    decode_ids,
    embed_table,
    norm_gain,
    x_weight,
    bc_weight,
    dt_weight,
    dt_bias,
    decay_log,
    conv_x,
    conv_bc,
    skip_gain,
    out_gain,
    out_weight,
):
    heads = dt_weight.shape[1]
    assert bc_weight.shape[1] == 1 and lax.axis_size("tp") == PARTS
    channels = x_weight.shape[1]
    taps = conv_x.shape[0]
    margin = taps - 1
    turned_bc = bc_weight.transpose(1, 2, 3, 0).reshape(-1, bc_weight.shape[0])
    turned_dt = dt_weight.T
    state_width = turned_bc.shape[0] // 2
    assert turned_bc.shape[0] == LANES
    tokens, part = prompt_embeds.shape
    rows, steps = decode_ids.shape
    assert steps <= EDGE and rows <= LANES and 2 * margin < EDGE
    asked = rows * steps
    groups = lax.axis_size("ctx")
    me_c = lax.axis_index("ctx").astype(jnp.int32)
    me_t = lax.axis_index("tp").astype(jnp.int32)
    vocab_here = embed_table.shape[0]
    bits = bits_of("ctx")
    assert len(bits) >= 2
    none = jnp.zeros((1,), jnp.int32)
    called = Caller()

    e2 = swapped(prompt_embeds, "tp", 2)
    e1 = swapped(prompt_embeds, "tp", 1)


    (notes,) = called(
        note_kernel, none, [decode_ids.T], [shaped((EDGE, 3 * LANES), BF16)], us=2
    )
    halving = [bits[1], bits[0]] + bits[2:]

    def joined(notes, bit):
        out = shaped((2 * notes.shape[0], notes.shape[1]), BF16)
        return called(join_kernel, none, [notes, swapped(notes, "ctx", bit)], [out], us=0.05)[0]

    notes = joined(notes, halving[-1])
    (e2,) = called(
        hand_kernel, none, [e2], [shaped(e2.shape, BF16)], us=0.05, same=((0, 0),)
    )
    e3 = swapped(e2, "tp", 1)

    project_weights = [
        norm_gain.reshape(PARTS, 1, part),
        x_weight,
        turned_bc,
        turned_dt,
        dt_bias.reshape(1, -1),
    ]
    conv_weights = [decay_log.reshape(1, -1), conv_x, conv_bc.reshape(taps, 2, -1)]
    skip_row, gain_row = skip_gain.reshape(1, -1), out_gain.reshape(1, -1)
    packed = state_width + EDGE

    def project(prompt, blocks, us):
        count = blocks[0].shape[0]
        scratch = []
        outs = [
            shaped((count, channels), BF16),
            shaped((count, LANES), BF16),
            shaped((count, LANES), F32),
        ]
        if prompt:
            outs.append(shaped((2 * EDGE, channels + LANES), BF16))
            scratch = [
                pltpu.VMEM((PARTS, part, channels), BF16),
                pltpu.VMEM((count, channels), F32),
                pltpu.SemaphoreType.DMA((PARTS,)),
            ]
        return called(
            functools.partial(project_kernel, prompt),
            me_t.reshape(1),
            blocks + project_weights,
            outs,
            [pltpu.VMEM((PARTS, count, part), BF16)] + scratch,
            us=us,
            limit=50 if prompt else 12,
            far=(5,) if prompt else (),
        )

    x_raw, bc_raw, step_size, halo = project(True, [prompt_embeds, e1, e2, e3], 3)
    for bit in reversed(halving[1:-1]):
        notes = joined(notes, bit)
    got = swapped(notes, "ctx", halving[0])
    halo = lax.ppermute(halo, "ctx", [(c, c + 1) for c in range(groups - 1)])

    half = groups * asked // 2
    chunk = max(LANES, vocab_here // 4)
    assert vocab_here % chunk == 0
    kept, sent = called(
        functools.partial(lookup_kernel, steps, rows),
        me_c.reshape(1),
        [notes, got, embed_table],
        [shaped((half, part), BF16), shaped((half, part), BF16)],
        [
            pltpu.VMEM((2 * half, LANES), F32),
            pltpu.VMEM((2 * half, part), F32),
            pltpu.VMEM((vocab_here // chunk, chunk, part), BF16),
            pltpu.SemaphoreType.DMA((vocab_here // chunk,)),
        ],
        us=3.5,
        limit=50,
        far=(2,),
    )

    x_rest, bc_rest, cum_log, partial = called(
        functools.partial(state_kernel, heads),
        none,
        [x_raw, bc_raw, step_size] + conv_weights,
        [
            shaped((tokens, channels), BF16),
            shaped((tokens, LANES), BF16),
            shaped((tokens, LANES), F32),
            shaped((state_width, channels), F32),
        ],
        [pltpu.VMEM((EDGE + tokens, 2 * LANES), F32)],
        us=2,
        limit=8,
    )
    x_head, bc_head, message, state = called(
        functools.partial(fix_kernel, heads),
        none,
        [halo, x_raw, bc_raw, step_size, cum_log] + conv_weights[1:] + [partial],
        [
            shaped((2 * EDGE, channels), BF16),
            shaped((2 * EDGE, LANES), BF16),
            shaped((packed, channels), BF16),
            shaped((state_width + EDGE, channels), F32),
        ],
        [pltpu.VMEM((3 * EDGE, channels), F32)],
        limit=8,
    )
    came = state
    def folded(kept, got):
        half = kept.shape[0] // 2
        return called(
            fold_kernel,
            none,
            [kept, got],
            [shaped((half, part), BF16), shaped((half, part), BF16)],
            limit=16 if half > 512 else 4,
        )

    y, reach, bc = called(
        functools.partial(mix_kernel, heads),
        none,
        [x_head, bc_head, x_rest, bc_rest, step_size, cum_log, skip_row],
        [
            shaped((tokens, channels), F32),
            shaped((tokens, LANES), F32),
            shaped((tokens, LANES), BF16),
        ],
        [pltpu.VMEM((tokens, channels), BF16)],
        us=2.5,
        limit=8,
    )

    for bit, halved in zip(bits, halving):
        embeds = swapped(sent, "ctx", halved)
        if halved == halving[-1]:
            (kept,) = called(last_fold_kernel, none, [kept, embeds], [shaped((asked, part), BF16)])
        else:
            kept, sent = folded(kept, embeds)
        got = swapped(message, "ctx", bit)
        later = ((me_c & bit) != 0).astype(jnp.int32)
        if bit != bits[-1]:
            message, state, came = called(
                functools.partial(step_kernel, bit == bits[0]),
                later.reshape(1),
                [got, state, came],
                [
                    shaped((packed, channels), BF16),
                    shaped((state_width + EDGE, channels), F32),
                    shaped((state_width + EDGE, channels), F32),
                ],
            )
    back_place = jnp.stack([me_t, later])
    near = swapped(kept, "tp", 2)
    over1 = swapped(kept, "tp", 1)
    over3 = swapped(near, "tp", 1)

    def back(kernel, count, inputs, scratch, us):
        return called(
            kernel,
            back_place,
            [got] + inputs + [gain_row, out_weight],
            [shaped((count, part), BF16)] * 2
            + [shaped((count, part), F32)] * 2
            + [shaped((tokens, part), F32)],
            [pltpu.VMEM((count, channels), F32), pltpu.VMEM((count, channels), BF16)] + scratch,
            us=us,
            limit=12,
        )

    def crossed(sent3, sent1, kept2, kept0):
        got3 = swapped(sent3, "tp", 1)
        got1 = swapped(sent1, "tp", 1)
        (far,) = called(far_kernel, none, [kept2, got3], [shaped(kept2.shape, BF16)])
        return kept0, got1, swapped(far, "tp", 2)

    prompt_sent3, prompt_mixed = called(
        functools.partial(prompt_back_kernel, heads),
        back_place,
        [got, came, y, bc, reach, gain_row, out_weight],
        [shaped((tokens, part), BF16), shaped((tokens, channels), BF16)],
        [pltpu.VMEM((tokens, channels), F32)],
        us=1.5,
        limit=12,
    )
    prompt_sent1, prompt_kept2 = called(
        functools.partial(rest_kernel, (1, 2)),
        back_place,
        [prompt_mixed, out_weight],
        [shaped((tokens, part), BF16), shaped((tokens, part), F32)],
    )
    dec_x_raw, dec_bc_raw, dec_step = project(False, [kept, over1, near, over3], 1.5)
    (far,) = called(
        far_kernel,
        none,
        [prompt_kept2, swapped(prompt_sent3, "tp", 1)],
        [shaped((tokens, part), BF16)],
    )
    far = swapped(far, "tp", 2)
    *decode_back, prompt_kept0 = back(
        functools.partial(decode_back_kernel, rows, heads),
        asked,
        [state, dec_x_raw, dec_bc_raw, dec_step] + conv_weights + [skip_row, prompt_mixed],
        [
            pltpu.VMEM((margin * rows + asked, 2 * LANES), F32),
            pltpu.VMEM((asked, channels), BF16),
            pltpu.VMEM((asked, channels), F32),
        ],
        2.5,
    )
    decode_crossed = crossed(*decode_back)
    prompt_out, decode_out = called(
        functools.partial(total_kernel, rows),
        none,
        [prompt_kept0, swapped(prompt_sent1, "tp", 1), far, *decode_crossed],
        [shaped((tokens, part), BF16), shaped((rows, steps, part), BF16)],
    )
    return (prompt_out, decode_out)


def solution(mesh):
    return jax.shard_map(
        on_device,
        mesh=mesh,
        in_specs=(
            P("ctx", "tp"),
            P("ctx", None),
            P("ctx", "tp"),
            P(),
            P(None, "tp"),
            P(None, "tp", None, None),
            P(None, "tp"),
            P("tp"),
            P("tp"),
            P(None, "tp"),
            P(None, "tp", None, None),
            P("tp"),
            P("tp"),
            P("tp", None),
        ),
        out_specs=(P("ctx", "tp"), P("ctx", None, "tp")),
        check_vma=False,
    )
```

```python
import functools

import jax
import jax.numpy as jnp
from jax import lax
from jax.experimental import pallas as pl
from jax.experimental.pallas import tpu as pltpu
from jax.sharding import PartitionSpec as P

EPS = 1e-05
BF16 = jnp.bfloat16
F32 = jnp.float32
LANES = 128
PARTS = 4
EDGE = 8
MEBI = 1024 * 1024


def swapped(value, axis, bit):
    count = lax.axis_size(axis)
    return lax.ppermute(value, axis, [(i, i ^ bit) for i in range(count)])


def bits_of(axis):
    count = lax.axis_size(axis)
    assert count & (count - 1) == 0
    return [1 << k for k in range(count.bit_length() - 1)]


def dot(a, b):
    return jnp.dot(a, b, preferred_element_type=F32)


def across(a, b, axis):
    return lax.dot_general(a, b, (((axis,), (axis,)), ((), ())), preferred_element_type=F32)


def halves(value):
    high = value.astype(BF16)
    low = (value - high.astype(F32)).astype(BF16)
    return high, low


def iota(shape, axis):
    return lax.broadcasted_iota(jnp.int32, shape, axis)


def spreader(width, channels):
    head = iota((2 * LANES, channels), 0) & (LANES - 1)
    return jnp.where(head == iota((2 * LANES, channels), 1) // width, 1.0, 0.0).astype(BF16)


def widened(per_head, spread):
    high, low = halves(per_head)
    return dot(jnp.concatenate([high, low], axis=1), spread)


def padded(row):
    return jnp.concatenate([row, jnp.zeros((row.shape[0], LANES - row.shape[1]), F32)], axis=1)


def silu(value):
    return value / (1.0 + jnp.exp(-value))


def started(pairs, sems):
    copies = [
        pltpu.make_async_copy(source, target, sems.at[at])
        for at, (source, target) in enumerate(pairs)
    ]
    for copy in copies:
        copy.start()
    return copies


def project_kernel(
    prompt,
    place,
    own,
    over1,
    over2,
    over3,
    gain,
    x_weight,
    bc_weight,
    dt_weight,
    dt_bias,
    x_out,
    bc_out,
    step_out,
    *rest,
):
    if prompt:
        halo_out, normed, chunks, total, sems = rest
        copies = started(
            [(x_weight.at[pl.ds(j * chunks.shape[1], chunks.shape[1]), :], chunks.at[j]) for j in range(PARTS)],
            sems,
        )
    else:
        (normed,) = rest
    me = place[0]
    tokens, part = own.shape
    channels, heads = x_weight.shape[1], dt_weight.shape[0]
    blocks = [ref[...].astype(F32) for ref in (own, over1, over2, over3)]
    square = sum(jnp.sum(b * b, axis=1, keepdims=True) for b in blocks)
    factor = lax.rsqrt(square / (PARTS * part) + EPS)
    for r in range(PARTS):
        normed[me ^ r] = (blocks[r] * factor * gain[me ^ r]).astype(BF16)
    fill = jnp.zeros((LANES - heads, PARTS * part), BF16)
    side = jnp.concatenate([bc_weight[...], dt_weight[...], fill], axis=0)
    raw = sum(across(normed[j], side[:, j * part : (j + 1) * part], 1) for j in range(PARTS))
    bc_out[...] = raw[:, :LANES].astype(BF16)
    pre = raw[:, LANES:] + padded(dt_bias[...])
    step_out[...] = jnp.maximum(pre, 0.0) + jnp.log1p(jnp.exp(-jnp.abs(pre)))
    last = 2 * EDGE
    step_lanes = 2 * LANES
    if not prompt:
        for lane in range(0, channels, step_lanes):
            lanes = slice(lane, lane + step_lanes)
            terms = [dot(normed[j], x_weight[j * part : (j + 1) * part, lanes]) for j in range(PARTS)]
            x_out[:, lanes] = sum(terms).astype(BF16)
        return
    halo_out[:, channels:] = raw[tokens - last :, :LANES].astype(BF16)
    for j in range(PARTS):
        copies[j].wait()
        for lane in range(0, channels, step_lanes):
            lanes = slice(lane, lane + step_lanes)
            term = dot(normed[j], chunks[j, :, lanes])
            if j > 0:
                term = total[:, lanes] + term
            if j < PARTS - 1:
                total[:, lanes] = term
            else:
                x_out[:, lanes] = term.astype(BF16)
                halo_out[:, lanes] = term[tokens - last :].astype(BF16)


def summed_logs(step_size, decay_log, mask):
    logs = step_size * -jnp.exp(padded(decay_log[...]))
    high, low = halves(logs)
    lowest = (logs - high.astype(F32) - low.astype(F32)).astype(BF16)
    sums = dot(
        jnp.where(mask, 1.0, 0.0).astype(BF16), jnp.concatenate([high, low, lowest], axis=1)
    )
    return sums[:, :LANES] + sums[:, LANES : 2 * LANES] + sums[:, 2 * LANES :]


def joined_taps(conv_bc):
    return jnp.concatenate([conv_bc[:, 0, :], conv_bc[:, 1, :]], axis=1)


def block_mask(tokens, rows):
    t_at = iota((tokens, tokens), 0)
    s_at = iota((tokens, tokens), 1)
    mask = t_at >= s_at
    return mask if rows == 1 else jnp.logical_and(mask, t_at % rows == s_at % rows)


def mixed_rows(rows, heads, x_conv, bc_conv, step_size, cum_log, skip_gain, y_out):
    tokens, channels = x_conv.shape
    width = channels // heads
    state_width = bc_conv.shape[1] // 2
    mask = block_mask(tokens, rows)
    b_rows = bc_conv[:, :state_width].astype(BF16)
    c_rows = bc_conv[:, state_width:].astype(BF16)
    cum_across = cum_log.T
    step_across = step_size.T
    scores = across(c_rows, b_rows, 1)
    spread = spreader(width, channels)
    skip_row = widened(jnp.broadcast_to(padded(skip_gain[...]), (EDGE, LANES)), spread)[:1]
    per_tile = LANES // width
    lane_head = iota((tokens, LANES), 1) // width
    for tile in range(channels // LANES):
        lanes = slice(tile * LANES, (tile + 1) * LANES)
        x_tile = x_conv[:, lanes].astype(F32)
        within = skip_row[:, lanes] * x_tile
        for k in range(per_tile):
            h = tile * per_tile + k
            gaps = cum_log[:, h : h + 1] - cum_across[h : h + 1, :]
            decays = jnp.exp(jnp.where(mask, gaps, -1e30))
            mixing = (scores * decays * step_across[h : h + 1, :]).astype(BF16)
            within += dot(mixing, jnp.where(lane_head == k, x_tile, 0.0).astype(BF16))
        y_out[:, lanes] = within


def packed_message(message_out, total, side):
    high, low = halves(side[:1])
    at = iota(side.shape, 0)
    rows = jnp.where(at == 0, high.astype(F32), jnp.where(at == 1, low.astype(F32), side))
    message_out[...] = jnp.concatenate([total, rows], axis=0).astype(BF16)


def unpacked(message, state_width):
    whole = message[...].astype(F32)
    side = whole[state_width:]
    return whole[:state_width], side[0:1] + side[1:2], side


def convolved(joined, edge, raw, taps_of, taps):
    count, lanes = raw.shape
    margin = taps - 1
    joined[:EDGE, :lanes] = edge
    joined[EDGE : EDGE + count, :lanes] = raw
    starts = [EDGE - margin + k for k in range(taps)]
    return silu(sum(taps_of(k) * joined[s : s + count, :lanes] for k, s in enumerate(starts)))


def state_kernel(
    heads,
    place,
    x_raw,
    bc_raw,
    step_size,
    decay_log,
    conv_x,
    conv_bc,
    x_out,
    bc_out,
    cum_out,
    state_out,
    joined,
):
    tokens, channels = x_raw.shape
    state_width = bc_raw.shape[1] // 2
    taps = conv_x.shape[0]
    margin = taps - 1
    bc_taps = joined_taps(conv_bc)
    step_lanes = 2 * LANES
    raw = bc_raw[...].astype(F32)
    none = jnp.zeros((EDGE, step_lanes), F32)
    bc_conv = convolved(joined, none[:, :LANES], raw, lambda k: bc_taps[k : k + 1], taps)
    bc_out[...] = bc_conv.astype(BF16)
    cum_log = summed_logs(step_size[...], decay_log, block_mask(tokens, 1))
    cum_out[...] = cum_log
    spread = spreader(channels // heads, channels)
    to_end = jnp.exp(cum_log[tokens - 1 : tokens] - cum_log) * step_size[...]
    b_turned = bc_conv.T[:state_width]
    b_turned = jnp.where(iota(b_turned.shape, 1) >= margin, b_turned, 0.0).astype(BF16)
    for lane in range(0, channels, step_lanes):
        lanes = slice(lane, lane + step_lanes)
        raw = x_raw[:, lanes].astype(F32)
        x_conv = convolved(joined, none, raw, lambda k: conv_x[k : k + 1, lanes], taps).astype(BF16)
        x_out[:, lanes] = x_conv
        scale = widened(to_end, spread[:, lanes])
        weighted = (x_conv.astype(F32) * scale).astype(BF16)
        state_out[:, lanes] = dot(b_turned, weighted)


def fix_kernel(
    heads,
    place,
    halo,
    x_raw,
    bc_raw,
    step_size,
    cum_log,
    conv_x,
    conv_bc,
    partial,
    x_out,
    bc_out,
    message_out,
    state_out,
    joined,
):
    tokens, channels = x_raw.shape
    state_width = bc_raw.shape[1] // 2
    taps = conv_x.shape[0]
    margin = taps - 1
    last = 2 * EDGE
    edge = halo[...].astype(F32)[EDGE:]
    bc_taps = joined_taps(conv_bc)
    raw = bc_raw[:last, :].astype(F32)
    bc_conv = convolved(joined, edge[:, channels:], raw, lambda k: bc_taps[k : k + 1], taps)
    bc_out[...] = bc_conv.astype(BF16)
    raw = x_raw[:last, :].astype(F32)
    x_conv = convolved(joined, edge[:, :channels], raw, lambda k: conv_x[k : k + 1], taps)
    x_conv = x_conv.astype(BF16)
    x_out[...] = x_conv
    spread = spreader(channels // heads, channels)
    final = cum_log[tokens - 1 : tokens, :]
    to_end = jnp.exp(final - cum_log[:last, :]) * step_size[:last, :]
    both = jnp.concatenate([to_end, jnp.broadcast_to(jnp.exp(final), (last, LANES))], axis=0)
    both = widened(both, spread)
    weighted = (x_conv.astype(F32) * both[:last]).astype(BF16).astype(F32)
    fill = jnp.zeros((LANES - last, LANES), F32)
    b_turned = jnp.concatenate([bc_conv, fill], axis=0).T[:state_width]
    b_turned = jnp.where(iota(b_turned.shape, 1) < margin, b_turned, 0.0).astype(BF16)
    fill = jnp.zeros((LANES - last, channels), F32)
    weighted = jnp.concatenate([weighted, fill], axis=0).astype(BF16)
    total = partial[...] + dot(b_turned, weighted)
    bc_tail = bc_raw[tokens - last :, :].astype(F32)[last - margin :]
    bc_tail = jnp.concatenate([bc_tail, jnp.zeros((margin, channels - LANES), F32)], axis=1)
    x_tail = x_raw[tokens - last :, :].astype(F32)[last - margin :]
    blank = jnp.zeros((EDGE - 1 - 2 * margin, channels), F32)
    side = jnp.concatenate([both[last : last + 1], blank, x_tail, bc_tail], axis=0)
    state_out[:state_width, :] = total
    state_out[state_width:, :] = side
    packed_message(message_out, total, side)


def mix_kernel(
    heads, place, x_head, bc_head, x_rest, bc_rest, step_size, cum_log, skip_gain, y_out, reach_out, bc_out, x_conv
):
    first = x_head.shape[0]
    x_conv[:first, :] = x_head[...]
    x_conv[first:, :] = x_rest[first:, :]
    bc_out[:first, :] = bc_head[...]
    bc_out[first:, :] = bc_rest[first:, :]
    cum_log = cum_log[...]
    reach_out[...] = jnp.exp(cum_log)
    mixed_rows(1, heads, x_conv, bc_out[...].astype(F32), step_size[...], cum_log, skip_gain, y_out)


def step_kernel(first, place, message, state, came, message_out, state_out, came_out):
    later = place[0] > 0
    state_width = state.shape[0] - EDGE
    channels = state.shape[1]
    other, other_decay, other_side = unpacked(message, state_width)
    mine, my_side = state[:state_width, :], state[state_width:, :]
    my_decay = my_side[:1]
    if first:
        before, passed = jnp.zeros_like(mine), jnp.ones_like(my_decay)
    else:
        before, passed = came[:state_width, :], came[state_width : state_width + 1, :]
    came_out[:state_width, :] = jnp.where(later, passed * other + before, before)
    passed = jnp.where(later, passed * other_decay, passed)
    came_out[state_width:, :] = jnp.broadcast_to(passed, (EDGE, channels))
    total = jnp.where(later, my_decay * other + mine, other_decay * mine + other)
    state_out[:state_width, :] = total
    side = jnp.where(later, my_side, other_side)
    side = jnp.where(iota((EDGE, channels), 0) == 0, my_decay * other_decay, side)
    state_out[state_width:, :] = side
    packed_message(message_out, total, side)


def finished(heads, me, incoming, y, bc, reach, gain, weight, outs, full, mixed):
    tokens, channels = y.shape
    high, low = halves(incoming)
    blank = jnp.zeros_like(high)
    table = jnp.concatenate([blank, high, blank, low], axis=0)
    twice = jnp.concatenate([bc, bc], axis=1)
    spread = spreader(channels // heads, channels)
    step_lanes = 2 * LANES
    square = jnp.zeros((tokens, 1), F32)
    for lane in range(0, channels, step_lanes):
        lanes = slice(lane, lane + step_lanes)
        total = y[:, lanes] + dot(twice, table[:, lanes]) * widened(reach, spread[:, lanes])
        full[:, lanes] = total
        square = square + jnp.sum(total * total, axis=1, keepdims=True)
    factor = lax.rsqrt(square / channels + EPS)
    mixed[...] = (full[...] * factor * gain[...]).astype(BF16)
    sent(me, mixed, weight, zip((3, 1, 2, 0), outs))


def sent(me, mixed, weight, wanted):
    part = weight.shape[1] // PARTS
    for r, out in wanted:
        columns = pl.ds(pl.multiple_of((me ^ r) * part, part), part)
        out[...] = dot(mixed[...], weight[:, columns]).astype(out.dtype)


def rest_kernel(place, mixed, weight, sent1, kept2, kept0):
    sent(place[0], mixed, weight, ((1, sent1), (2, kept2), (0, kept0)))


def prompt_back_kernel(
    heads, place, message, came, y, bc, reach, gain, weight, sent3, mixed, full
):
    me, later = place[0], place[1] > 0
    state_width = came.shape[0] - EDGE
    other, _, _ = unpacked(message, state_width)
    before, passed = came[:state_width, :], came[state_width : state_width + 1, :]
    incoming = jnp.where(later, passed * other + before, before)
    finished(heads, me, incoming, y, bc[...], reach[...], gain, weight, (sent3,), full, mixed)


def decode_back_kernel(
    rows,
    heads,
    place,
    message,
    state,
    x_raw,
    bc_raw,
    step_size,
    decay_log,
    conv_x,
    conv_bc,
    skip_gain,
    gain,
    weight,
    sent3,
    sent1,
    kept2,
    kept0,
    full,
    mixed,
    joined,
    x_conv,
    y,
):
    me, later = place[0], place[1] > 0
    state_width = state.shape[0] - EDGE
    tokens, channels = x_raw.shape
    taps = conv_x.shape[0]
    margin = taps - 1
    other, other_decay, other_side = unpacked(message, state_width)
    mine, my_side = state[:state_width, :], state[state_width:, :]
    incoming = jnp.where(later, my_side[:1] * other + mine, other_decay * mine + other)
    side = jnp.where(later, my_side, other_side)
    x_tail = side[EDGE - 2 * margin : EDGE - margin]
    bc_tail = side[EDGE - margin :, :LANES]

    def convolved(raw, tail, taps_of):
        lanes = raw.shape[1]
        for m in range(margin):
            joined[m * rows : (m + 1) * rows, :lanes] = jnp.broadcast_to(
                tail[m : m + 1], (rows, lanes)
            )
        joined[margin * rows :, :lanes] = raw
        return silu(
            sum(taps_of(k) * joined[k * rows : k * rows + tokens, :lanes] for k in range(taps))
        )

    bc_taps = joined_taps(conv_bc)
    bc_conv = convolved(bc_raw[...].astype(F32), bc_tail, lambda k: bc_taps[k : k + 1])
    step_lanes = 2 * LANES
    for lane in range(0, channels, step_lanes):
        lanes = slice(lane, lane + step_lanes)
        x_conv[:, lanes] = convolved(
            x_raw[:, lanes].astype(F32), x_tail[:, lanes], lambda k: conv_x[k : k + 1, lanes]
        ).astype(BF16)
    cum_log = summed_logs(step_size[...], decay_log, block_mask(tokens, rows))
    mixed_rows(rows, heads, x_conv, bc_conv, step_size[...], cum_log, skip_gain, y)
    bc = bc_conv.astype(BF16)
    outs = (sent3, sent1, kept2, kept0)
    finished(heads, me, incoming, y, bc, jnp.exp(cum_log), gain, weight, outs, full, mixed)


def far_kernel(place, kept, got, out):
    out[...] = (kept[...] + got[...].astype(F32)).astype(BF16)


def total_kernel(place, kept, got, far, out):
    out[...] = (kept[...] + got[...].astype(F32) + far[...].astype(F32)).astype(BF16)


def decode_total_kernel(rows, place, dec_kept, dec_got, dec_far, dec_out):
    total = dec_kept[...] + dec_got[...].astype(F32) + dec_far[...].astype(F32)
    asked = total.shape[0]
    steps = asked // rows
    at = iota((asked, asked), 0)
    order = (at % steps) * rows + at // steps == iota((asked, asked), 1)
    total = dot(jnp.where(order, 1.0, 0.0).astype(BF16), total.astype(BF16))
    for r in range(rows):
        dec_out[r] = total[r * steps : (r + 1) * steps].astype(BF16)


def note_kernel(place, ids, note):
    steps = ids.shape[0]
    ids = ids[...]
    digits = [padded(d.astype(F32)) for d in (ids & 255, (ids >> 8) & 255, ids >> 16)]
    top = jnp.concatenate(digits, axis=1)
    note[...] = jnp.concatenate([top, jnp.zeros((EDGE - steps, 3 * LANES), F32)], axis=0).astype(BF16)


def join_kernel(place, mine, got, out):
    out[...] = jnp.concatenate([mine[...].astype(F32), got[...].astype(F32)], axis=0).astype(BF16)


def hand_kernel(place, given, handed):
    del given, handed


def lookup_kernel(
    steps, rows, place, notes, got, table_in, kept_out, sent_out, wanted, found, table, sems
):
    chunks, chunk, _ = table.shape
    copies = started(
        [(table_in.at[pl.ds(c * chunk, chunk), :], table.at[c]) for c in range(chunks)], sems
    )
    first = (place[0] * (chunks * chunk)).astype(F32)
    held = jnp.concatenate([notes[...].astype(F32), got[...].astype(F32)], axis=0)
    groups = held.shape[0] // EDGE
    digits = held[:, :LANES] + held[:, LANES : 2 * LANES] * 256.0 + held[:, 2 * LANES : 3 * LANES] * 65536.0
    same = iota((rows, LANES), 0) == iota((rows, LANES), 1)
    for q in range(groups):
        for s in range(steps):
            line = jnp.broadcast_to(digits[q * EDGE + s : q * EDGE + s + 1], (rows, LANES))
            column = jnp.sum(jnp.where(same, line, 0.0), axis=1, keepdims=True) - first
            at = (q * steps + s) * rows
            wanted[at : at + rows, :] = jnp.broadcast_to(column, (rows, LANES))
    asked = groups * steps * rows
    block = min(asked, 256)
    lane = iota((block, LANES), 1).astype(F32)
    for c in range(chunks):
        copies[c].wait()
        for at in range(0, asked, block):
            gap = wanted[at : at + block, :] - lane
            hot = [
                jnp.where(gap == float(c * chunk + k), 1.0, 0.0).astype(BF16)
                for k in range(0, chunk, LANES)
            ]
            term = dot(jnp.concatenate(hot, axis=1), table[c])
            if c == 0:
                found[at : at + block, :] = term
            else:
                found[at : at + block, :] += term
    kept_out[...] = found[: asked // 2, :].astype(BF16)
    sent_out[...] = found[asked // 2 :, :].astype(BF16)


def fold_kernel(place, kept, got, kept_out, sent_out):
    total = (kept[...].astype(F32) + got[...].astype(F32)).astype(BF16)
    half = kept_out.shape[0]
    kept_out[...] = total[:half]
    sent_out[...] = total[half:]


def last_fold_kernel(place, kept, got, out):
    out[...] = (kept[...].astype(F32) + got[...].astype(F32)).astype(BF16)


VMEM = pl.BlockSpec(memory_space=pltpu.VMEM)
SMEM = pl.BlockSpec(memory_space=pltpu.SMEM)
HBM = pl.BlockSpec(memory_space=pltpu.HBM)


class Caller:
    def __init__(self):
        self.token = jnp.zeros((8, LANES), F32)

    def __call__(self, kernel, place, inputs, outs, scratch=(), us=1.0, limit=4, far=(), same=()):
        inputs = list(inputs)
        count = len(inputs)

        def ordered(place, token, *refs):
            refs, token_out = list(refs), refs[count]
            del refs[count]
            kernel(place, *refs)
            token_out[...] = jnp.zeros_like(token_out)

        results = pl.pallas_call(
            ordered,
            out_shape=[shaped((8, LANES), F32)] + outs,
            in_specs=[SMEM, VMEM] + [HBM if at in far else VMEM for at in range(count)],
            out_specs=[VMEM] * (1 + len(outs)),
            scratch_shapes=list(scratch),
            input_output_aliases={2 + at: 1 + out for at, out in same},
            compiler_params=pltpu.CompilerParams(vmem_limit_bytes=limit * MEBI),
            cost_estimate=pl.CostEstimate(
                flops=int(us * 1e9), bytes_accessed=int(us * 1e6), transcendentals=0
            ),
        )(place, self.token, *inputs)
        self.token = results[0]
        return results[1:]


def shaped(shape, dtype):
    return jax.ShapeDtypeStruct(shape, dtype)


def on_device(
    prompt_embeds,
    decode_ids,
    embed_table,
    norm_gain,
    x_weight,
    bc_weight,
    dt_weight,
    dt_bias,
    decay_log,
    conv_x,
    conv_bc,
    skip_gain,
    out_gain,
    out_weight,
):
    heads = dt_weight.shape[1]
    assert bc_weight.shape[1] == 1 and lax.axis_size("tp") == PARTS
    channels = x_weight.shape[1]
    taps = conv_x.shape[0]
    margin = taps - 1
    turned_bc = bc_weight.transpose(1, 2, 3, 0).reshape(-1, bc_weight.shape[0])
    turned_dt = dt_weight.T
    state_width = turned_bc.shape[0] // 2
    assert turned_bc.shape[0] == LANES
    tokens, part = prompt_embeds.shape
    rows, steps = decode_ids.shape
    assert steps <= EDGE and rows <= LANES and 2 * margin < EDGE
    asked = rows * steps
    groups = lax.axis_size("ctx")
    me_c = lax.axis_index("ctx").astype(jnp.int32)
    me_t = lax.axis_index("tp").astype(jnp.int32)
    vocab_here = embed_table.shape[0]
    bits = bits_of("ctx")
    assert len(bits) >= 2
    none = jnp.zeros((1,), jnp.int32)
    called = Caller()

    e2 = swapped(prompt_embeds, "tp", 2)
    e1 = swapped(prompt_embeds, "tp", 1)


    (notes,) = called(
        note_kernel, none, [decode_ids.T], [shaped((EDGE, 3 * LANES), BF16)], us=2
    )
    halving = [bits[1], bits[0]] + bits[2:]

    def joined(notes, bit):
        out = shaped((2 * notes.shape[0], notes.shape[1]), BF16)
        return called(join_kernel, none, [notes, swapped(notes, "ctx", bit)], [out], us=0.05)[0]

    notes = joined(notes, halving[-1])
    (e2,) = called(
        hand_kernel, none, [e2], [shaped(e2.shape, BF16)], us=0.05, same=((0, 0),)
    )
    e3 = swapped(e2, "tp", 1)

    project_weights = [
        norm_gain.reshape(PARTS, 1, part),
        x_weight,
        turned_bc,
        turned_dt,
        dt_bias.reshape(1, -1),
    ]
    conv_weights = [decay_log.reshape(1, -1), conv_x, conv_bc.reshape(taps, 2, -1)]
    skip_row, gain_row = skip_gain.reshape(1, -1), out_gain.reshape(1, -1)
    packed = state_width + EDGE

    def project(prompt, blocks, us):
        count = blocks[0].shape[0]
        scratch = []
        outs = [
            shaped((count, channels), BF16),
            shaped((count, LANES), BF16),
            shaped((count, LANES), F32),
        ]
        if prompt:
            outs.append(shaped((2 * EDGE, channels + LANES), BF16))
            scratch = [
                pltpu.VMEM((PARTS, part, channels), BF16),
                pltpu.VMEM((count, channels), F32),
                pltpu.SemaphoreType.DMA((PARTS,)),
            ]
        return called(
            functools.partial(project_kernel, prompt),
            me_t.reshape(1),
            blocks + project_weights,
            outs,
            [pltpu.VMEM((PARTS, count, part), BF16)] + scratch,
            us=us,
            limit=50 if prompt else 12,
            far=(5,) if prompt else (),
        )

    x_raw, bc_raw, step_size, halo = project(True, [prompt_embeds, e1, e2, e3], 3)
    for bit in reversed(halving[1:-1]):
        notes = joined(notes, bit)
    got = swapped(notes, "ctx", halving[0])
    halo = lax.ppermute(halo, "ctx", [(c, c + 1) for c in range(groups - 1)])

    half = groups * asked // 2
    chunk = max(LANES, vocab_here // 4)
    assert vocab_here % chunk == 0
    kept, sent = called(
        functools.partial(lookup_kernel, steps, rows),
        me_c.reshape(1),
        [notes, got, embed_table],
        [shaped((half, part), BF16), shaped((half, part), BF16)],
        [
            pltpu.VMEM((2 * half, LANES), F32),
            pltpu.VMEM((2 * half, part), F32),
            pltpu.VMEM((vocab_here // chunk, chunk, part), BF16),
            pltpu.SemaphoreType.DMA((vocab_here // chunk,)),
        ],
        us=3.5,
        limit=50,
        far=(2,),
    )

    x_rest, bc_rest, cum_log, partial = called(
        functools.partial(state_kernel, heads),
        none,
        [x_raw, bc_raw, step_size] + conv_weights,
        [
            shaped((tokens, channels), BF16),
            shaped((tokens, LANES), BF16),
            shaped((tokens, LANES), F32),
            shaped((state_width, channels), F32),
        ],
        [pltpu.VMEM((EDGE + tokens, 2 * LANES), F32)],
        us=2,
        limit=8,
    )
    x_head, bc_head, message, state = called(
        functools.partial(fix_kernel, heads),
        none,
        [halo, x_raw, bc_raw, step_size, cum_log] + conv_weights[1:] + [partial],
        [
            shaped((2 * EDGE, channels), BF16),
            shaped((2 * EDGE, LANES), BF16),
            shaped((packed, channels), BF16),
            shaped((state_width + EDGE, channels), F32),
        ],
        [pltpu.VMEM((3 * EDGE, channels), F32)],
        limit=8,
    )
    came = state
    def folded(kept, got):
        half = kept.shape[0] // 2
        return called(
            fold_kernel,
            none,
            [kept, got],
            [shaped((half, part), BF16), shaped((half, part), BF16)],
            limit=16 if half > 512 else 4,
        )

    y, reach, bc = called(
        functools.partial(mix_kernel, heads),
        none,
        [x_head, bc_head, x_rest, bc_rest, step_size, cum_log, skip_row],
        [
            shaped((tokens, channels), F32),
            shaped((tokens, LANES), F32),
            shaped((tokens, LANES), BF16),
        ],
        [pltpu.VMEM((tokens, channels), BF16)],
        us=2.5,
        limit=8,
    )

    for bit, halved in zip(bits, halving):
        embeds = swapped(sent, "ctx", halved)
        if halved == halving[-1]:
            (kept,) = called(last_fold_kernel, none, [kept, embeds], [shaped((asked, part), BF16)])
        else:
            kept, sent = folded(kept, embeds)
        got = swapped(message, "ctx", bit)
        later = ((me_c & bit) != 0).astype(jnp.int32)
        if bit != bits[-1]:
            message, state, came = called(
                functools.partial(step_kernel, bit == bits[0]),
                later.reshape(1),
                [got, state, came],
                [
                    shaped((packed, channels), BF16),
                    shaped((state_width + EDGE, channels), F32),
                    shaped((state_width + EDGE, channels), F32),
                ],
            )
    back_place = jnp.stack([me_t, later])
    near = swapped(kept, "tp", 2)
    over1 = swapped(kept, "tp", 1)
    over3 = swapped(near, "tp", 1)

    def back(kernel, count, inputs, scratch, us):
        return called(
            kernel,
            back_place,
            [got] + inputs + [gain_row, out_weight],
            [shaped((count, part), BF16)] * 2 + [shaped((count, part), F32)] * 2,
            [pltpu.VMEM((count, channels), F32), pltpu.VMEM((count, channels), BF16)] + scratch,
            us=us,
            limit=12,
        )

    def crossed(sent3, sent1, kept2, kept0):
        got3 = swapped(sent3, "tp", 1)
        got1 = swapped(sent1, "tp", 1)
        (far,) = called(far_kernel, none, [kept2, got3], [shaped(kept2.shape, BF16)])
        return kept0, got1, swapped(far, "tp", 2)

    prompt_sent3, prompt_mixed = called(
        functools.partial(prompt_back_kernel, heads),
        back_place,
        [got, came, y, bc, reach, gain_row, out_weight],
        [shaped((tokens, part), BF16), shaped((tokens, channels), BF16)],
        [pltpu.VMEM((tokens, channels), F32)],
        us=1.5,
        limit=12,
    )
    prompt_rest = called(
        rest_kernel,
        back_place,
        [prompt_mixed, out_weight],
        [shaped((tokens, part), BF16)] + [shaped((tokens, part), F32)] * 2,
    )
    dec_x_raw, dec_bc_raw, dec_step = project(False, [kept, over1, near, over3], 1.5)
    prompt_crossed = crossed(prompt_sent3, *prompt_rest)
    decode_back = back(
        functools.partial(decode_back_kernel, rows, heads),
        asked,
        [state, dec_x_raw, dec_bc_raw, dec_step] + conv_weights + [skip_row],
        [
            pltpu.VMEM((margin * rows + asked, 2 * LANES), F32),
            pltpu.VMEM((asked, channels), BF16),
            pltpu.VMEM((asked, channels), F32),
        ],
        2.5,
    )
    decode_crossed = crossed(*decode_back)
    (prompt_out,) = called(
        total_kernel, none, [*prompt_crossed], [shaped((tokens, part), BF16)]
    )
    (decode_out,) = called(
        functools.partial(decode_total_kernel, rows),
        none,
        [*decode_crossed],
        [shaped((rows, steps, part), BF16)],
    )
    return (prompt_out, decode_out)


def solution(mesh):
    return jax.shard_map(
        on_device,
        mesh=mesh,
        in_specs=(
            P("ctx", "tp"),
            P("ctx", None),
            P("ctx", "tp"),
            P(),
            P(None, "tp"),
            P(None, "tp", None, None),
            P(None, "tp"),
            P("tp"),
            P("tp"),
            P(None, "tp"),
            P(None, "tp", None, None),
            P("tp"),
            P("tp"),
            P("tp", None),
        ),
        out_specs=(P("ctx", "tp"), P("ctx", None, "tp")),
        check_vma=False,
    )
```
